32 devices in a mesh: tile: 8 (over z, core), tm: 4 (over y, x).
Axes of the slice: x: 2, y: 2, z: 4, core: 2. Of those that a mesh axis runs over, the one named last changes fastest.
Arguments:
- src_snap: bfloat16 [128, 8, 128, 256], P('tile', 'tm'), may hold values from -6 to 6
- rcv_snap: bfloat16 [128, 8, 128, 256], P('tile', 'tm'), may hold values from -6 to 6
- q_rate: float32 [256], replicated, may hold values from 0.05 to 1.5
- nbr_device: int32 [128, 2], replicated, may hold values from 0 to 7, all different within a row; in each aligned block of 16 rows (0 to 15, 16 to 31, ...) at most 5 rows name the same one
- nbr_index: int32 [128, 2], replicated, may hold values from 0 to 15
- depth_extent: int32 [128], P('tile'), may hold values from 16 to 256, as said below
Outputs:
- image: float32 [128, 8, 49, 256], P(('tile', 'tm'))
The draws below stay inside these ranges and needn't reach their ends.
Inputs may be any that keep to these rules, and one draw needn't show every extreme that they name: `nbr_device`: the two devices of a row differ; among the rows of one device (aligned blocks of 16 rows) no device is named more than 5 times, and in some device's rows one device is named exactly 5 times. Cells of a tile's gathers at depth depth_extent[s] and below are zero.
All inputs are finite; a program needn't handle non-finite values.
Results may differ from the reference program's by a relative error of at most 0.0003.
Values may be sent and summed in bfloat16 or wider, within the bound.
A program may use at most 128 MiB of HBM per device.

```python
import math
import jax
import jax.numpy as jnp
import numpy as np
from jax import lax

TPD = 16
Z = 256
BW = 128
GSTEP = 16
HMAX = 24
SLOTS = 128
TIMES = 8
GB = 8
OFFS = 49
RIM_L = 16
RIM_R = 17
CAP = 5
N_TILE = 8


def draw_depth_extent(key, part):
    key_deep, key_low, key_high, key_pick, key_other = jax.random.split(key, 5)
    device_count = SLOTS // TPD
    shallow_limit = max(1, Z // 16)
    deep_flag = jax.random.randint(key_deep, (device_count,), 0, 2)
    shallow = jax.random.randint(key_low, (SLOTS,), shallow_limit, Z // 2 + 1)
    deeper = jax.random.randint(key_high, (SLOTS,), Z // 2 + 1, Z + 1)
    owner_device = jnp.arange(SLOTS) // TPD
    extent = jnp.where(deep_flag[owner_device] == 1, deeper, shallow)
    chosen = jax.random.randint(key_pick, (), 0, SLOTS)
    other_pick = (chosen + 1 + jax.random.randint(key_other, (), 0, SLOTS - 1)) % SLOTS
    extent = extent.at[chosen].set(Z).at[other_pick].set(shallow_limit)
    return extent.astype(jnp.int32)


def plant(values, own_key, low, top_value):
    place = [jax.random.randint(jax.random.fold_in(own_key, axis), (), 0, length) for axis, length in enumerate(values.shape)]
    longest = values.shape.index(max(values.shape))
    next_to = place[:longest] + [(place[longest] + 1) % values.shape[longest]] + place[longest + 1:]
    return values.at[tuple(place)].set(low).at[tuple(next_to)].set(top_value)


def block_scale(own_key, shape, cuts, least, largest):
    loudness, own = 1.0, jax.random.fold_in(own_key, 6)
    for axis_at, shards_of in cuts:
        heights = jnp.exp(jax.random.uniform(jax.random.fold_in(own, axis_at), (shards_of,), jnp.float32, least / len(cuts), largest / len(cuts)))
        loudness = loudness * jnp.repeat(heights, shape[axis_at] // shards_of).reshape([-1 if axis == axis_at else 1 for axis in range(len(shape))])
    return loudness


def shared_out(key, own, number, rows, amount, top, reach, slope):
    sequence = jax.random.permutation(key, amount)
    heavy_load, usual = shares(amount, rows * top, reach, slope, True), shares(amount, rows * top, reach, slope, False)
    places = jnp.arange(amount)

    def named(sizes, rotation):
        used = int((sizes > 0).sum())
        fixed = max(1, used // 4)
        shifted = fixed + (places - fixed + rotation * (used - fixed)) % max(1, amount - fixed)
        return jnp.zeros((amount,), jnp.int32).at[sequence[jnp.where(places < fixed, places, shifted)]].set(jnp.asarray(sizes, jnp.int32))

    sizes = jnp.where(number % 4 == 0, named(heavy_load, number // 4), named(usual, number - number // 4 - 1))
    mixed = jax.random.permutation(jax.random.fold_in(own, 3), amount)
    source_of, receiver = mixed[0:amount // 2 * 2:2], mixed[1:amount // 2 * 2:2]
    margin = jnp.minimum(sizes[source_of] - 1, reach - sizes[receiver]) // 2
    margin = jnp.where((source_of == sequence[0]) | (receiver == sequence[0]) | (sizes[receiver] == 0), 0, jnp.maximum(margin, 0))
    shifted = jax.random.randint(jax.random.fold_in(own, 4), (amount // 2,), 0, 1 << 20) % (margin + 1)
    sizes = sizes.at[source_of].add(-shifted).at[receiver].add(shifted)
    labels = jnp.searchsorted(jnp.cumsum(sizes), jnp.arange(rows * top), side="right").astype(jnp.int32)
    listing = labels.reshape(top, rows).T
    listing = listing[jax.random.permutation(jax.random.fold_in(own, 1), rows)]
    rotation = jax.random.randint(jax.random.fold_in(own, 2), (rows, 1), 0, top)
    return jnp.take_along_axis(listing, (jnp.arange(top)[None, :] + rotation) % top, axis=1)


def shares(number_of, total, most, slope, full):
    weights = [(1 << 20) // math.isqrt(rank ** slope) + 1 for rank in range(1, number_of + 1)]
    largest = most if full else min(most, max(-(-total // number_of), total * weights[0] // sum(weights)))
    least = 1 if total - largest >= number_of - 1 else 0
    given, rest = [largest] + [least] * (number_of - 1), total - largest - least * (number_of - 1)
    while rest > 0:
        free = [i for i in range(1, number_of) if given[i] < largest] or [i for i in range(1, number_of) if given[i] < most]
        pool, left = sum([weights[i] for i in free]), rest
        for i in free:
            extra = min(most - given[i], max(1, left * weights[i] // pool), rest)
            given[i] = given[i] + extra
            rest = rest - extra
    return np.array(given)


def normal_values(key, dims, deviation, reach, pieces=(), kind=jnp.bfloat16):
    level = block_scale(key, dims, pieces, -0.22, 0.18) if pieces else 1.0
    result = jax.random.normal(key, dims, jnp.float32) * deviation * level
    return jnp.minimum(jnp.maximum(result, -reach), reach).astype(kind)


def setup_inputs(seed: int = 0) -> dict:
    splits = jax.random.split(jax.random.key(seed), 7)
    src_snap = normal_values(splits[0], (SLOTS, TIMES, BW, Z), 1.0, 6.0, ((0, 8), (1, 4)))
    rcv_snap = normal_values(splits[1], (SLOTS, TIMES, BW, Z), 1.0, 6.0, ((0, 8), (1, 4)))
    q_rate = jnp.clip(jnp.exp(jax.random.uniform(splits[2], (Z,), jnp.float32, math.log(0.05), math.log(1.5))), 0.05, 1.5)
    nbr_device_keys = jax.random.split(jax.random.fold_in(splits[3], 1), SLOTS // TPD)
    nbr_device_turns = jax.random.permutation(jax.random.fold_in(splits[3], 3), SLOTS // TPD)
    nbr_device = jax.vmap(lambda own, number: shared_out(jax.random.fold_in(splits[3], 2), own, number, TPD, N_TILE, 2, CAP, 0))(nbr_device_keys, nbr_device_turns).reshape((SLOTS, 2))
    nbr_index = plant(jax.random.randint(splits[4], (SLOTS, 2), 0, TPD), jax.random.fold_in(splits[4], 1), 0, TPD - 1).astype(jnp.int32)
    depth_extent = draw_depth_extent(jax.random.fold_in(splits[6], 71), 0)
    return {"src_snap": src_snap, "rcv_snap": rcv_snap, "q_rate": q_rate, "nbr_device": nbr_device, "nbr_index": nbr_index, "depth_extent": depth_extent}


def reference(src_snap, rcv_snap, q_rate, nbr_device, nbr_index, depth_extent):
    time_steps = jnp.arange(TIMES).astype(jnp.float32)
    weight = jnp.exp(q_rate[None, :] * time_steps[:, None] / TIMES)
    norm_scale = 1.0 / math.sqrt(TIMES)
    depth_index = jnp.arange(Z).astype(jnp.int32)
    begins = [RIM_L + GSTEP * gather + GSTEP // 2 - HMAX for gather in range(GB)]

    def one_tile(slot):
        left_slot = nbr_device[slot, 0] * TPD + nbr_index[slot, 0]
        right_slot = nbr_device[slot, 1] * TPD + nbr_index[slot, 1]

        def strip(field):
            return jnp.concatenate([field[left_slot][:, BW - RIM_L:, :], field[slot], field[right_slot][:, :RIM_R, :]], axis=1)
        src_strip = strip(src_snap).astype(jnp.float32)
        rcv_strip = strip(rcv_snap).astype(jnp.float32)
        src_window = jnp.stack([src_strip[:, begin:begin + OFFS, :] for begin in begins], axis=1)[:, :, ::-1, :]
        rcv_window = jnp.stack([rcv_strip[:, begin:begin + OFFS, :] for begin in begins], axis=1)
        total = lax.optimization_barrier(jnp.sum(src_window * rcv_window * weight[:, None, None, :], axis=0))
        depth_mask = (depth_index < depth_extent[slot]).astype(jnp.float32)
        return total * norm_scale * depth_mask[None, None, :]
    return lax.map(one_tile, jnp.arange(SLOTS).astype(jnp.int32))
```

```python
import functools
import math

import jax
import jax.numpy as jnp
from jax import lax
from jax.experimental import pallas as pl
from jax.experimental.pallas import tpu as pltpu
from jax.sharding import PartitionSpec as P

GSTEP = 16
HMAX = 24
GB = 8
OFFS = 49
RIM_L = 16
RIM_R = 17
ROWS = 16
SPAN = 56
MESH = pl.DeviceIdType.MESH


def one_hot(rows, columns, rule):
    row = lax.broadcasted_iota(jnp.int32, (rows, columns), 0)
    column = lax.broadcasted_iota(jnp.int32, (rows, columns), 1)
    return rule(row, column).astype(jnp.float32).astype(jnp.bfloat16)


def pick(matrix, values):
    return jnp.dot(matrix, values, preferred_element_type=jnp.float32)


def kernel(
    sizes,
    send_tab,
    arrive_tab,
    extent_ref,
    rate_ref,
    src_ref,
    rcv_ref,
    out_ref,
    edge_cells,
    a_send,
    a_recv,
    b_send,
    b_recv,
    centre,
    acc,
    edge_sem,
    own_sem,
    main_send_sem,
    main_recv_sem,
    a_send_sem,
    a_recv_sem,
    b_send_sem,
    b_recv_sem,
):
    tiles, steps, width, depth, devices, times, capacity, share = sizes
    pieces = 2 * steps
    fields = (src_ref, rcv_ref)
    me_tile = lax.axis_index("tile")
    me_tm = lax.axis_index("tm")

    def rest(count, me, j):
        return lax.rem(me + j, count)

    edge_copies = []
    for f in range(2):
        for k, first in enumerate((width - ROWS, 0, ROWS)):
            copy = pltpu.make_async_copy(
                fields[f].at[:, :, pl.ds(first, ROWS), :],
                edge_cells.at[f, k],
                edge_sem.at[f * 3 + k],
            )
            copy.start()
            edge_copies.append(copy)
    own_copies = []
    for f in range(2):
        copy = pltpu.make_async_copy(
            fields[f].at[pl.ds(me_tm * share, share)], centre.at[f, me_tm], own_sem.at[f]
        )
        copy.start()
        own_copies.append(copy)

    barrier = pltpu.get_barrier_semaphore()
    for j in range(1, times):
        pl.semaphore_signal(
            barrier, inc=1, device_id=(me_tile, rest(times, me_tm, j)), device_id_type=MESH
        )
    for j in range(1, devices):
        pl.semaphore_signal(
            barrier, inc=1, device_id=(rest(devices, me_tile, j), me_tm), device_id_type=MESH
        )
    pl.semaphore_wait(barrier, times + devices - 2)

    main_copies = []
    for j in range(1, times):
        to = rest(times, me_tm, j)
        for f in range(2):
            copy = pltpu.make_async_remote_copy(
                src_ref=fields[f].at[pl.ds(to * share, share)],
                dst_ref=centre.at[f, me_tm],
                send_sem=main_send_sem.at[j, f],
                recv_sem=main_recv_sem.at[j, f],
                device_id=(me_tile, to),
                device_id_type=MESH,
            )
            copy.start()
            main_copies.append(copy)

    for copy in edge_copies:
        copy.wait()

    a_extra = a_send.shape[1] - capacity * pieces
    compress = one_hot(
        a_extra * ROWS, capacity * pieces * ROWS, lambda row, column: column == row * ROWS
    )

    def pack(to):
        extra = []
        for k in range(capacity):
            index = send_tab[0, to, k]
            side = send_tab[1, to, k]
            for f in range(2):
                first = k * pieces + f * steps
                a_send[to, first : first + steps] = edge_cells[f, side, index]
                extra.append(edge_cells[f, 2, index].reshape(steps * ROWS, depth))
        packed = pick(compress, jnp.concatenate(extra, axis=0))
        a_send[to, capacity * pieces :] = packed.astype(jnp.bfloat16).reshape(
            a_extra, ROWS, depth
        )

    def a_copy(j):
        to = rest(devices, me_tile, j)
        return pltpu.make_async_remote_copy(
            src_ref=a_send.at[to],
            dst_ref=a_recv.at[me_tile],
            send_sem=a_send_sem.at[j],
            recv_sem=a_recv_sem.at[j],
            device_id=(to, me_tm),
            device_id_type=MESH,
        )

    @pl.loop(1, devices)
    def _(j):
        pack(rest(devices, me_tile, j))
        a_copy(j).start()

    pack(me_tile)
    a_recv[me_tile] = a_send[me_tile]

    rate = rate_ref[...]

    def weight(part, t):
        step = (part * steps + t).astype(jnp.float32)
        return jnp.exp(rate * step / (steps * times))

    turn_centre = one_hot(
        width - 8, width, lambda row, column: column == width - ROWS - row
    )
    last = width // GSTEP * GSTEP - HMAX * 2

    def centre_pass(part, fresh):
        @pl.loop(0, share)
        def _(i):
            sums = [None] * GB
            for t in range(steps):
                turned = pick(turn_centre, centre[0, part, i, t]) * weight(part, t)
                straight = centre[1, part, i, t].astype(jnp.float32)
                for g in range(1, GB - 2):
                    back = last - GSTEP * g
                    ahead = GSTEP * (g - 1)
                    product = turned[back : back + SPAN] * straight[ahead : ahead + SPAN]
                    sums[g] = product if sums[g] is None else sums[g] + product
            for g in range(1, GB - 2):
                if fresh:
                    acc[i, g] = sums[g]
                else:
                    acc[i, g] += sums[g]

    for copy in own_copies:
        copy.wait()
    centre_pass(me_tm, True)

    @pl.loop(1, devices)
    def _(j):
        a_copy(j).wait()

    b_rims = 2 * share * steps * 2
    b_extra = b_send.shape[1] - b_rims

    def unpack(to):
        packed = None
        for i in range(share):
            tile = to * share + i
            for side in range(2):
                source = arrive_tab[0, 2 * tile + side]
                rank = arrive_tab[1, 2 * tile + side]
                rim = a_recv[source, pl.ds(rank * pieces, pieces)]
                for f in range(2):
                    for t in range(steps):
                        b_send[to, ((f * share + i) * steps + t) * 2 + side] = rim[f * steps + t]
            extra = a_recv[source, capacity * pieces :].reshape(a_extra * ROWS, depth)
            choose = one_hot(
                b_extra * ROWS,
                a_extra * ROWS,
                lambda row, column: (row >= i * pieces)
                & (row < (i + 1) * pieces)
                & (column == rank * pieces + row - i * pieces),
            )
            chosen = pick(choose, extra)
            packed = chosen if packed is None else packed + chosen
        b_send[to, b_rims:] = packed.astype(jnp.bfloat16).reshape(b_extra, ROWS, depth)

    def b_copy(j):
        to = rest(times, me_tm, j)
        return pltpu.make_async_remote_copy(
            src_ref=b_send.at[to],
            dst_ref=b_recv.at[me_tm],
            send_sem=b_send_sem.at[j],
            recv_sem=b_recv_sem.at[j],
            device_id=(me_tile, to),
            device_id_type=MESH,
        )

    @pl.loop(1, times)
    def _(j):
        unpack(rest(times, me_tm, j))
        b_copy(j).start()

    unpack(me_tm)
    b_recv[me_tm] = b_send[me_tm]

    def finish(gathers):
        @pl.loop(0, share)
        def _(i):
            extent = extent_ref[me_tm * share + i]
            cell = lax.broadcasted_iota(jnp.int32, (1, depth), 1)
            mask = (cell < extent).astype(jnp.float32)
            for g in gathers:
                out_ref[i, g] = (
                    acc[i, g][:OFFS] * (1.0 / math.sqrt(steps * times)) * mask
                )

    turn_first = one_hot(SPAN, 4 * ROWS, lambda row, column: column == OFFS - 1 - row)
    turn_last = one_hot(SPAN + ROWS, 4 * ROWS, lambda row, column: column == 4 * ROWS - row)
    wide = width - 3 * ROWS

    def edge_pass(part, fresh):
        @pl.loop(0, share)
        def _(i):
            extra = b_recv[part, b_rims:].reshape(b_extra * ROWS, depth)
            sums = [None] * 3
            for t in range(steps):
                scale = weight(part, t)
                place = i * pieces + t
                rims = (i * steps + t) * 2
                rims_rcv = ((share + i) * steps + t) * 2
                src_left = b_recv[part, rims]
                src_right = b_recv[part, rims + 1]
                rcv_left = b_recv[part, rims_rcv]
                rcv_right = b_recv[part, rims_rcv + 1]
                turned = pick(
                    turn_first,
                    jnp.concatenate([src_left, centre[0, part, i, t, : 3 * ROWS]], axis=0),
                )
                straight = jnp.concatenate(
                    [rcv_left, centre[1, part, i, t, : 3 * ROWS]], axis=0
                ).astype(jnp.float32)
                products = [turned * scale * straight[:SPAN]]
                turn_extra = one_hot(
                    SPAN + ROWS,
                    b_extra * ROWS,
                    lambda row, column: (row == 0) & (column == place),
                )
                turned = pick(
                    turn_last,
                    jnp.concatenate([centre[0, part, i, t, wide:], src_right], axis=0),
                ) + pick(turn_extra, extra)
                turned = turned * scale
                rcv_extra = pick(
                    one_hot(
                        8,
                        b_extra * ROWS,
                        lambda row, column: (row == 0) & (column == place + steps),
                    ),
                    extra,
                )
                straight = jnp.concatenate(
                    [
                        centre[1, part, i, t, wide:].astype(jnp.float32),
                        rcv_right.astype(jnp.float32),
                        rcv_extra,
                    ],
                    axis=0,
                )
                products.append(turned[ROWS:] * straight[:SPAN])
                products.append(turned[:SPAN] * straight[ROWS:])
                sums = [
                    product if total is None else total + product
                    for total, product in zip(sums, products)
                ]
            for g, total in zip((0, GB - 2, GB - 1), sums):
                if fresh:
                    acc[i, g] = total
                else:
                    acc[i, g] += total

    edge_pass(me_tm, True)
    for j in range(1, times):
        for f in range(2):
            main_copies[2 * (j - 1) + f].wait_recv()
        centre_pass(rest(times, me_tm, times - j), False)
    finish(range(1, GB - 2))
    for j in range(1, times):
        b_copy(j).wait_recv()
        edge_pass(rest(times, me_tm, times - j), False)
    finish((0, GB - 2, GB - 1))

    for copy in main_copies:
        copy.wait_send()
    for j in range(1, times):
        b_copy(j).wait_send()


def routes(nbr_device, nbr_index, devices, capacity, tiles):
    own = lax.axis_index("tile")
    count = 2 * tiles
    device = nbr_device.reshape(devices, count)
    index = nbr_index.reshape(devices, count)
    ids = jnp.arange(count, dtype=jnp.int32)
    earlier = ids[None, :] < ids[:, None]
    same = (device[:, :, None] == device[:, None, :]) & earlier[None]
    rank = jnp.sum(same.astype(jnp.int32), axis=2)
    slot = jnp.arange(capacity, dtype=jnp.int32)
    hit = ((device == own)[:, None, :] & (rank[:, None, :] == slot[None, :, None])).astype(jnp.int32)
    wanted = jnp.stack([index, jnp.broadcast_to((ids % 2)[None, :], index.shape)])
    send_tab = jnp.sum(hit[None] * wanted[:, :, None, :], axis=3)
    arrive = jnp.stack([device, rank])
    arrive_tab = lax.dynamic_slice_in_dim(arrive, own, 1, 1)[:, 0]
    return send_tab, arrive_tab


def local(src_snap, rcv_snap, q_rate, nbr_device, nbr_index, depth_extent):
    tiles, steps, width, depth = src_snap.shape
    devices = lax.axis_size("tile")
    times = lax.axis_size("tm")
    capacity = (2 * tiles + devices - 1) // devices + 1
    share = tiles // times
    send_tab, arrive_tab = routes(nbr_device, nbr_index, devices, capacity, tiles)
    pieces = 2 * steps
    a_blocks = capacity * pieces + -(-capacity * pieces // ROWS)
    b_blocks = 2 * share * steps * 2 + -(-share * pieces // ROWS)
    sizes = (tiles, steps, width, depth, devices, times, capacity, share)
    half = jnp.bfloat16
    products = share * GB * OFFS * depth * steps * times
    return pl.pallas_call(
        functools.partial(kernel, sizes),
        out_shape=jax.ShapeDtypeStruct((share, GB, OFFS, depth), jnp.float32),
        in_specs=[pl.BlockSpec(memory_space=pltpu.SMEM)] * 3
        + [pl.BlockSpec(memory_space=pltpu.VMEM)]
        + [pl.BlockSpec(memory_space=pl.ANY)] * 2,
        out_specs=pl.BlockSpec(memory_space=pltpu.VMEM),
        scratch_shapes=[
            pltpu.VMEM((2, 3, tiles, steps, ROWS, depth), half),
            pltpu.VMEM((devices, a_blocks, ROWS, depth), half),
            pltpu.VMEM((devices, a_blocks, ROWS, depth), half),
            pltpu.VMEM((times, b_blocks, ROWS, depth), half),
            pltpu.VMEM((times, b_blocks, ROWS, depth), half),
            pltpu.VMEM((2, times, share, steps, width, depth), half),
            pltpu.VMEM((share, GB, SPAN, depth), jnp.float32),
            pltpu.SemaphoreType.DMA((6,)),
            pltpu.SemaphoreType.DMA((2,)),
            pltpu.SemaphoreType.DMA((times, 2)),
            pltpu.SemaphoreType.DMA((times, 2)),
            pltpu.SemaphoreType.DMA((devices,)),
            pltpu.SemaphoreType.DMA((devices,)),
            pltpu.SemaphoreType.DMA((times,)),
            pltpu.SemaphoreType.DMA((times,)),
        ],
        compiler_params=pltpu.CompilerParams(
            collective_id=0, has_side_effects=True, vmem_limit_bytes=40 * 1024 * 1024
        ),
        cost_estimate=pl.CostEstimate(
            flops=3 * products, bytes_accessed=4 * tiles * steps * width * depth, transcendentals=0
        ),
    )(send_tab, arrive_tab, depth_extent, q_rate.reshape(1, depth), src_snap, rcv_snap)


def solution(mesh):
    placed = (P("tile", "tm", None, None), P("tile", "tm", None, None), P(), P(), P(), P("tile"))
    return jax.shard_map(
        local,
        mesh=mesh,
        in_specs=placed,
        out_specs=P(("tile", "tm"), None, None, None),
        check_vma=False,
    )
```

```python
import functools
import math

import jax
import jax.numpy as jnp
from jax import lax
from jax.experimental import pallas as pl
from jax.experimental.pallas import tpu as pltpu
from jax.sharding import PartitionSpec as P

GSTEP = 16
HMAX = 24
GB = 8
OFFS = 49
RIM_L = 16
RIM_R = 17
ROWS = 16
SPAN = 56
MESH = pl.DeviceIdType.MESH


def one_hot(rows, columns, rule):
    row = lax.broadcasted_iota(jnp.int32, (rows, columns), 0)
    column = lax.broadcasted_iota(jnp.int32, (rows, columns), 1)
    return rule(row, column).astype(jnp.float32).astype(jnp.bfloat16)


def pick(matrix, values):
    return jnp.dot(matrix, values, preferred_element_type=jnp.float32)


def kernel(
    sizes,
    send_tab,
    arrive_tab,
    extent_ref,
    rate_ref,
    src_ref,
    rcv_ref,
    out_ref,
    edge_cells,
    a_send,
    a_recv,
    b_send,
    b_recv,
    centre,
    acc,
    edge_sem,
    own_sem,
    main_send_sem,
    main_recv_sem,
    a_send_sem,
    a_recv_sem,
    b_send_sem,
    b_recv_sem,
):
    tiles, steps, width, depth, devices, times, capacity, share = sizes
    pieces = 2 * steps
    fields = (src_ref, rcv_ref)
    me_tile = lax.axis_index("tile")
    me_tm = lax.axis_index("tm")

    def rest(count, me, j):
        return lax.rem(me + j, count)

    edge_copies = []
    for f in range(2):
        for k, first in enumerate((width - ROWS, 0, ROWS)):
            copy = pltpu.make_async_copy(
                fields[f].at[:, :, pl.ds(first, ROWS), :],
                edge_cells.at[f, k],
                edge_sem.at[f * 3 + k],
            )
            copy.start()
            edge_copies.append(copy)
    own_copies = []
    for f in range(2):
        copy = pltpu.make_async_copy(
            fields[f].at[pl.ds(me_tm * share, share)], centre.at[f, me_tm], own_sem.at[f]
        )
        copy.start()
        own_copies.append(copy)

    barrier = pltpu.get_barrier_semaphore()
    for j in range(1, times):
        pl.semaphore_signal(
            barrier, inc=1, device_id=(me_tile, rest(times, me_tm, j)), device_id_type=MESH
        )
    for j in range(1, devices):
        pl.semaphore_signal(
            barrier, inc=1, device_id=(rest(devices, me_tile, j), me_tm), device_id_type=MESH
        )
    pl.semaphore_wait(barrier, times + devices - 2)

    main_copies = []
    for j in range(1, times):
        to = rest(times, me_tm, j)
        for f in range(2):
            copy = pltpu.make_async_remote_copy(
                src_ref=fields[f].at[pl.ds(to * share, share)],
                dst_ref=centre.at[f, me_tm],
                send_sem=main_send_sem.at[j, f],
                recv_sem=main_recv_sem.at[j, f],
                device_id=(me_tile, to),
                device_id_type=MESH,
            )
            copy.start()
            main_copies.append(copy)

    for copy in edge_copies:
        copy.wait()

    a_extra = a_send.shape[1] - capacity * pieces
    compress = one_hot(
        a_extra * ROWS, capacity * pieces * ROWS, lambda row, column: column == row * ROWS
    )

    def pack(to):
        extra = []
        for k in range(capacity):
            index = send_tab[0, to, k]
            side = send_tab[1, to, k]
            for f in range(2):
                first = k * pieces + f * steps
                a_send[to, first : first + steps] = edge_cells[f, side, index]
                extra.append(edge_cells[f, 2, index].reshape(steps * ROWS, depth))
        packed = pick(compress, jnp.concatenate(extra, axis=0))
        a_send[to, capacity * pieces :] = packed.astype(jnp.bfloat16).reshape(
            a_extra, ROWS, depth
        )

    def a_copy(j):
        to = rest(devices, me_tile, j)
        return pltpu.make_async_remote_copy(
            src_ref=a_send.at[to],
            dst_ref=a_recv.at[me_tile],
            send_sem=a_send_sem.at[j],
            recv_sem=a_recv_sem.at[j],
            device_id=(to, me_tm),
            device_id_type=MESH,
        )

    @pl.loop(1, devices)
    def _(j):
        pack(rest(devices, me_tile, j))
        a_copy(j).start()

    pack(me_tile)
    a_recv[me_tile] = a_send[me_tile]

    rate = rate_ref[...]

    def weight(part, t):
        step = (part * steps + t).astype(jnp.float32)
        return jnp.exp(rate * step / (steps * times))

    turn_centre = one_hot(
        width - 8, width, lambda row, column: column == width - ROWS - row
    )
    last = width // GSTEP * GSTEP - HMAX * 2

    def centre_pass(part, fresh):
        @pl.loop(0, share)
        def _(i):
            sums = [None] * GB
            for t in range(steps):
                turned = pick(turn_centre, centre[0, part, i, t]) * weight(part, t)
                straight = centre[1, part, i, t].astype(jnp.float32)
                for g in range(1, GB - 2):
                    back = last - GSTEP * g
                    ahead = GSTEP * (g - 1)
                    product = turned[back : back + SPAN] * straight[ahead : ahead + SPAN]
                    sums[g] = product if sums[g] is None else sums[g] + product
            for g in range(1, GB - 2):
                if fresh:
                    acc[i, g] = sums[g]
                else:
                    acc[i, g] += sums[g]

    for copy in own_copies:
        copy.wait()
    centre_pass(me_tm, True)

    @pl.loop(1, devices)
    def _(j):
        a_copy(j).wait()

    b_rims = 2 * share * steps * 2
    b_extra = b_send.shape[1] - b_rims

    def unpack(to):
        packed = None
        for i in range(share):
            tile = to * share + i
            for side in range(2):
                source = arrive_tab[0, 2 * tile + side]
                rank = arrive_tab[1, 2 * tile + side]
                rim = a_recv[source, pl.ds(rank * pieces, pieces)]
                for f in range(2):
                    for t in range(steps):
                        b_send[to, ((f * share + i) * steps + t) * 2 + side] = rim[f * steps + t]
            extra = a_recv[source, capacity * pieces :].reshape(a_extra * ROWS, depth)
            choose = one_hot(
                b_extra * ROWS,
                a_extra * ROWS,
                lambda row, column: (row >= i * pieces)
                & (row < (i + 1) * pieces)
                & (column == rank * pieces + row - i * pieces),
            )
            chosen = pick(choose, extra)
            packed = chosen if packed is None else packed + chosen
        b_send[to, b_rims:] = packed.astype(jnp.bfloat16).reshape(b_extra, ROWS, depth)

    def b_copy(j):
        to = rest(times, me_tm, j)
        return pltpu.make_async_remote_copy(
            src_ref=b_send.at[to],
            dst_ref=b_recv.at[me_tm],
            send_sem=b_send_sem.at[j],
            recv_sem=b_recv_sem.at[j],
            device_id=(me_tile, to),
            device_id_type=MESH,
        )

    @pl.loop(1, times)
    def _(j):
        unpack(rest(times, me_tm, j))
        b_copy(j).start()

    unpack(me_tm)
    b_recv[me_tm] = b_send[me_tm]

    def finish(gathers):
        @pl.loop(0, share)
        def _(i):
            extent = extent_ref[me_tm * share + i]
            cell = lax.broadcasted_iota(jnp.int32, (1, depth), 1)
            mask = (cell < extent).astype(jnp.float32)
            for g in gathers:
                out_ref[i, g] = (
                    acc[i, g][:OFFS] * (1.0 / math.sqrt(steps * times)) * mask
                )

    turn_first = one_hot(SPAN, 4 * ROWS, lambda row, column: column == OFFS - 1 - row)
    turn_last = one_hot(SPAN + ROWS, 4 * ROWS, lambda row, column: column == 4 * ROWS - row)
    wide = width - 3 * ROWS

    def edge_pass(part, fresh):
        @pl.loop(0, share)
        def _(i):
            extra = b_recv[part, b_rims:].reshape(b_extra * ROWS, depth)
            sums = [None] * 3
            for t in range(steps):
                scale = weight(part, t)
                place = i * pieces + t
                rims = (i * steps + t) * 2
                rims_rcv = ((share + i) * steps + t) * 2
                src_left = b_recv[part, rims]
                src_right = b_recv[part, rims + 1]
                rcv_left = b_recv[part, rims_rcv]
                rcv_right = b_recv[part, rims_rcv + 1]
                turned = pick(
                    turn_first,
                    jnp.concatenate([src_left, centre[0, part, i, t, : 3 * ROWS]], axis=0),
                )
                straight = jnp.concatenate(
                    [rcv_left, centre[1, part, i, t, : 3 * ROWS]], axis=0
                ).astype(jnp.float32)
                products = [turned * scale * straight[:SPAN]]
                turn_extra = one_hot(
                    SPAN + ROWS,
                    b_extra * ROWS,
                    lambda row, column: (row == 0) & (column == place),
                )
                turned = pick(
                    turn_last,
                    jnp.concatenate([centre[0, part, i, t, wide:], src_right], axis=0),
                ) + pick(turn_extra, extra)
                turned = turned * scale
                rcv_extra = pick(
                    one_hot(
                        8,
                        b_extra * ROWS,
                        lambda row, column: (row == 0) & (column == place + steps),
                    ),
                    extra,
                )
                straight = jnp.concatenate(
                    [
                        centre[1, part, i, t, wide:].astype(jnp.float32),
                        rcv_right.astype(jnp.float32),
                        rcv_extra,
                    ],
                    axis=0,
                )
                products.append(turned[ROWS:] * straight[:SPAN])
                products.append(turned[:SPAN] * straight[ROWS:])
                sums = [
                    product if total is None else total + product
                    for total, product in zip(sums, products)
                ]
            for g, total in zip((0, GB - 2, GB - 1), sums):
                if fresh:
                    acc[i, g] = total
                else:
                    acc[i, g] += total

    edge_pass(me_tm, True)
    for j in range(1, times):
        for f in range(2):
            main_copies[2 * (j - 1) + f].wait_recv()
        centre_pass(rest(times, me_tm, times - j), False)
    finish(range(1, GB - 2))
    for j in range(1, times):
        b_copy(j).wait_recv()
        edge_pass(rest(times, me_tm, times - j), False)
    finish((0, GB - 2, GB - 1))

    for copy in main_copies:
        copy.wait_send()
    for j in range(1, times):
        b_copy(j).wait_send()


def routes(nbr_device, nbr_index, devices, capacity, tiles):
    own = lax.axis_index("tile")
    count = 2 * tiles
    device = nbr_device.reshape(devices, count)
    index = nbr_index.reshape(devices, count)
    ids = jnp.arange(count, dtype=jnp.int32)
    earlier = ids[None, :] < ids[:, None]
    same = (device[:, :, None] == device[:, None, :]) & earlier[None]
    rank = jnp.sum(same.astype(jnp.int32), axis=2)
    slot = jnp.arange(capacity, dtype=jnp.int32)
    hit = ((device == own)[:, None, :] & (rank[:, None, :] == slot[None, :, None])).astype(jnp.int32)
    wanted = jnp.stack([index, jnp.broadcast_to((ids % 2)[None, :], index.shape)])
    send_tab = jnp.sum(hit[None] * wanted[:, :, None, :], axis=3)
    arrive = jnp.stack([device, rank])
    arrive_tab = lax.dynamic_slice_in_dim(arrive, own, 1, 1)[:, 0]
    return send_tab, arrive_tab


def local(src_snap, rcv_snap, q_rate, nbr_device, nbr_index, depth_extent):
    tiles, steps, width, depth = src_snap.shape
    devices = lax.axis_size("tile")
    times = lax.axis_size("tm")
    capacity = (2 * tiles + devices - 1) // devices + 1
    share = tiles // times
    send_tab, arrive_tab = routes(nbr_device, nbr_index, devices, capacity, tiles)
    pieces = 2 * steps
    a_blocks = capacity * pieces + -(-capacity * pieces // ROWS)
    b_blocks = 2 * share * steps * 2 + -(-share * pieces // ROWS)
    sizes = (tiles, steps, width, depth, devices, times, capacity, share)
    half = jnp.bfloat16
    products = share * GB * OFFS * depth * steps * times
    return pl.pallas_call(
        functools.partial(kernel, sizes),
        out_shape=jax.ShapeDtypeStruct((share, GB, OFFS, depth), jnp.float32),
        in_specs=[pl.BlockSpec(memory_space=pltpu.SMEM)] * 3
        + [pl.BlockSpec(memory_space=pltpu.VMEM)]
        + [pl.BlockSpec(memory_space=pl.ANY)] * 2,
        out_specs=pl.BlockSpec(memory_space=pltpu.VMEM),
        scratch_shapes=[
            pltpu.VMEM((2, 3, tiles, steps, ROWS, depth), half),
            pltpu.VMEM((devices, a_blocks, ROWS, depth), half),
            pltpu.VMEM((devices, a_blocks, ROWS, depth), half),
            pltpu.VMEM((times, b_blocks, ROWS, depth), half),
            pltpu.VMEM((times, b_blocks, ROWS, depth), half),
            pltpu.VMEM((2, times, share, steps, width, depth), half),
            pltpu.VMEM((share, GB, SPAN, depth), jnp.float32),
            pltpu.SemaphoreType.DMA((6,)),
            pltpu.SemaphoreType.DMA((2,)),
            pltpu.SemaphoreType.DMA((times, 2)),
            pltpu.SemaphoreType.DMA((times, 2)),
            pltpu.SemaphoreType.DMA((devices,)),
            pltpu.SemaphoreType.DMA((devices,)),
            pltpu.SemaphoreType.DMA((times,)),
            pltpu.SemaphoreType.DMA((times,)),
        ],
        compiler_params=pltpu.CompilerParams(
            collective_id=0, has_side_effects=True, vmem_limit_bytes=40 * 1024 * 1024
        ),
        cost_estimate=pl.CostEstimate(
            flops=3 * products, bytes_accessed=4 * tiles * steps * width * depth, transcendentals=0
        ),
    )(send_tab, arrive_tab, depth_extent, q_rate.reshape(1, depth), src_snap, rcv_snap)


def pair_kernel(
    sizes,
    device_tab,
    index_tab,
    extent_ref,
    rate_ref,
    src_ref,
    rcv_ref,
    out_ref,
    ranks,
    edge_cells,
    a_send,
    a_recv,
    b_own,
    b_send,
    b_recv,
    centre,
    acc,
    pc_send,
    pc_recv,
    pe_send,
    pe_recv,
    edge_sem,
    own_sem,
    main_send_sem,
    main_recv_sem,
    a_send_sem,
    a_recv_sem,
    b_send_sem,
    b_recv_sem,
    p_send_sem,
    p_recv_sem,
):
    tiles, steps, width, depth, devices, times, capacity, share = sizes
    half = share // 2
    pieces = 2 * steps
    fields = (src_ref, rcv_ref)
    me_tile = lax.axis_index("tile")
    me_tm = lax.axis_index("tm")
    low = lax.rem(me_tm, 2)
    high = lax.div(me_tm, 2)
    by_x = high * 2 + 1 - low
    by_y = (1 - high) * 2 + low
    across = (1 - high) * 2 + 1 - low

    owner = (by_y, by_x, me_tm, me_tm)
    partner = (by_x, by_y, by_x, by_y)
    owner_there = (across, across, by_x, by_y)
    offset = (0, half, 0, half)

    def first_tile(owners, w):
        return owners[w] * share + offset[w]

    edge_copies = []
    for f in range(2):
        for k, first in enumerate((width - ROWS, 0, ROWS)):
            copy = pltpu.make_async_copy(
                fields[f].at[:, :, pl.ds(first, ROWS), :],
                edge_cells.at[f, k],
                edge_sem.at[f * 3 + k],
            )
            copy.start()
            edge_copies.append(copy)

    barrier = pltpu.get_barrier_semaphore()
    for to in (by_x, by_y):
        pl.semaphore_signal(barrier, inc=1, device_id=(me_tile, to), device_id_type=MESH)
    for j in range(1, devices):
        pl.semaphore_signal(
            barrier, inc=1, device_id=(lax.rem(me_tile + j, devices), me_tm), device_id_type=MESH
        )
    pl.semaphore_wait(barrier, devices + 1)

    main_copies = []
    for w in range(4):
        copies = []
        for f in range(2):
            copy = pltpu.make_async_remote_copy(
                src_ref=fields[f].at[pl.ds(first_tile(owner_there, w), half)],
                dst_ref=centre.at[f, 1, w],
                send_sem=main_send_sem.at[w, f],
                recv_sem=main_recv_sem.at[w, f],
                device_id=(me_tile, partner[w]),
                device_id_type=MESH,
            )
            copy.start()
            copies.append(copy)
        main_copies.append(copies)
    own_copies = []
    for w in range(4):
        for f in range(2):
            copy = pltpu.make_async_copy(
                fields[f].at[pl.ds(first_tile(owner, w), half)],
                centre.at[f, 0, w],
                own_sem.at[w, f],
            )
            copy.start()
            own_copies.append(copy)

    for copy in edge_copies:
        copy.wait()

    a_extra = a_send.shape[1] - capacity * pieces
    compress = one_hot(
        a_extra * ROWS, capacity * pieces * ROWS, lambda row, column: column == row * ROWS
    )

    def pack(to):
        def scan(row, carry):
            count, codes = carry
            for side in range(2):
                hit = device_tab[side, to * tiles + row] == me_tile
                code = index_tab[side, to * tiles + row] * 2 + side
                codes = tuple(
                    jnp.where(hit & (count == k), code, codes[k]) for k in range(capacity)
                )
                count = count + hit.astype(jnp.int32)
            return count, codes

        zero = jnp.int32(0)
        _, codes = lax.fori_loop(0, tiles, scan, (zero, (zero,) * capacity))
        extra = []
        for k in range(capacity):
            index = lax.div(codes[k], 2)
            side = lax.rem(codes[k], 2)
            for f in range(2):
                first = k * pieces + f * steps
                a_send[to, first : first + steps] = edge_cells[f, side, index]
                extra.append(edge_cells[f, 2, index].reshape(steps * ROWS, depth))
        packed = pick(compress, jnp.concatenate(extra, axis=0))
        a_send[to, capacity * pieces :] = packed.astype(jnp.bfloat16).reshape(
            a_extra, ROWS, depth
        )

    def a_copy(j):
        to = lax.rem(me_tile + j, devices)
        return pltpu.make_async_remote_copy(
            src_ref=a_send.at[to],
            dst_ref=a_recv.at[me_tile],
            send_sem=a_send_sem.at[j],
            recv_sem=a_recv_sem.at[j],
            device_id=(to, me_tm),
            device_id_type=MESH,
        )

    @pl.loop(1, devices)
    def _(j):
        pack(lax.rem(me_tile + j, devices))
        a_copy(j).start()

    pack(me_tile)
    a_recv[me_tile] = a_send[me_tile]

    base = me_tile * tiles

    @pl.loop(0, tiles)
    def _(row):
        mine = [device_tab[side, base + row] for side in range(2)]

        def count(other, sums):
            theirs = [device_tab[side, base + other] for side in range(2)]
            return tuple(
                sums[side]
                + (theirs[0] == mine[side]).astype(jnp.int32)
                + (theirs[1] == mine[side]).astype(jnp.int32)
                for side in range(2)
            )

        found = lax.fori_loop(0, row, count, (jnp.int32(0), jnp.int32(0)))
        for side in range(2):
            ranks[side, row] = jnp.minimum(found[side], capacity - 1)

    rate = rate_ref[...]

    def weight(part, t):
        step = (part * steps + t).astype(jnp.float32)
        return jnp.exp(rate * step / (steps * times))

    inner = range(1, GB - 2)
    outer = (0, GB - 2, GB - 1)
    turn_centre = one_hot(
        width - 8, width, lambda row, column: column == width - ROWS - row
    )
    last = width // GSTEP * GSTEP - HMAX * 2

    def centre_sums(w, p, part, i):
        sums = [None] * GB
        for t in range(steps):
            turned = pick(turn_centre, centre[0, p, w, i, t]) * weight(part, t)
            straight = centre[1, p, w, i, t].astype(jnp.float32)
            for g in inner:
                back = last - GSTEP * g
                ahead = GSTEP * (g - 1)
                product = turned[back : back + SPAN] * straight[ahead : ahead + SPAN]
                sums[g] = product if sums[g] is None else sums[g] + product
        return sums

    turn_first = one_hot(SPAN, 4 * ROWS, lambda row, column: column == OFFS - 1 - row)
    turn_last = one_hot(SPAN + ROWS, 4 * ROWS, lambda row, column: column == 4 * ROWS - row)
    wide = width - 3 * ROWS
    b_rims = 2 * half * steps * 2
    b_extra = b_send.shape[1] - b_rims

    def edge_sums(rims_ref, w, p, part, i):
        extra = rims_ref[w, b_rims:].reshape(b_extra * ROWS, depth)
        sums = [None] * 3
        for t in range(steps):
            scale = weight(part, t)
            place = i * pieces + t
            rims = (i * steps + t) * 2
            rims_rcv = ((half + i) * steps + t) * 2
            turned = pick(
                turn_first,
                jnp.concatenate([rims_ref[w, rims], centre[0, p, w, i, t, : 3 * ROWS]], axis=0),
            )
            straight = jnp.concatenate(
                [rims_ref[w, rims_rcv], centre[1, p, w, i, t, : 3 * ROWS]], axis=0
            ).astype(jnp.float32)
            products = [turned * scale * straight[:SPAN]]
            turn_extra = one_hot(
                SPAN + ROWS,
                b_extra * ROWS,
                lambda row, column: (row == 0) & (column == place),
            )
            turned = pick(
                turn_last,
                jnp.concatenate(
                    [centre[0, p, w, i, t, wide:], rims_ref[w, rims + 1]], axis=0
                ),
            ) + pick(turn_extra, extra)
            turned = turned * scale
            rcv_extra = pick(
                one_hot(
                    8,
                    b_extra * ROWS,
                    lambda row, column: (row == 0) & (column == place + steps),
                ),
                extra,
            )
            straight = jnp.concatenate(
                [
                    centre[1, p, w, i, t, wide:].astype(jnp.float32),
                    rims_ref[w, rims_rcv + 1].astype(jnp.float32),
                    rcv_extra,
                ],
                axis=0,
            )
            products.append(turned[ROWS:] * straight[:SPAN])
            products.append(turned[:SPAN] * straight[ROWS:])
            sums = [
                product if total is None else total + product
                for total, product in zip(sums, products)
            ]
        return sums

    def own_centre(w):
        @pl.loop(0, half)
        def _(i):
            sums = centre_sums(w, 0, me_tm, i)
            for g in inner:
                acc[w, i, g] = sums[g]

    def own_edge(w):
        @pl.loop(0, half)
        def _(i):
            for g, total in zip(outer, edge_sums(b_own, w, 0, me_tm, i)):
                acc[w, i, g] = total

    def far_centre(w):
        for copy in main_copies[w]:
            copy.wait_recv()

        @pl.loop(0, half)
        def _(i):
            sums = centre_sums(w, 1, partner[w], i)
            for k, g in enumerate(inner):
                total = acc[w, i, g] + sums[g]
                if w < 2:
                    pc_send[w, i, OFFS * k : OFFS * (k + 1)] = total[:OFFS]
                else:
                    acc[w, i, g] = total

    def far_edge(w):
        b_copies[w].wait_recv()

        @pl.loop(0, half)
        def _(i):
            sums = edge_sums(b_recv, w, 1, partner[w], i)
            for k, g in enumerate(outer):
                total = acc[w, i, g] + sums[k]
                if w < 2:
                    pe_send[w, i, OFFS * k : OFFS * (k + 1)] = total[:OFFS]
                else:
                    acc[w, i, g] = total

    def partial_copy(w, send, recv, k):
        return pltpu.make_async_remote_copy(
            src_ref=send.at[w],
            dst_ref=recv.at[w],
            send_sem=p_send_sem.at[k, w],
            recv_sem=p_recv_sem.at[k, w],
            device_id=(me_tile, owner[w]),
            device_id_type=MESH,
        )

    def unpack(first, target, w):
        packed = None
        for i in range(half):
            tile = first + i
            for side in range(2):
                source = device_tab[side, base + tile]
                rank = ranks[side, tile]
                rim = a_recv[source, pl.ds(rank * pieces, pieces)]
                for f in range(2):
                    for t in range(steps):
                        target[w, ((f * half + i) * steps + t) * 2 + side] = rim[f * steps + t]
            extra = a_recv[source, capacity * pieces :].reshape(a_extra * ROWS, depth)
            choose = one_hot(
                b_extra * ROWS,
                a_extra * ROWS,
                lambda row, column: (row >= i * pieces)
                & (row < (i + 1) * pieces)
                & (column == rank * pieces + row - i * pieces),
            )
            chosen = pick(choose, extra)
            packed = chosen if packed is None else packed + chosen
        target[w, b_rims:] = packed.astype(jnp.bfloat16).reshape(b_extra, ROWS, depth)

    def finish(w, gathers, recv):
        @pl.loop(0, half)
        def _(i):
            tile = offset[w] + i
            extent = extent_ref[me_tm * share + tile]
            cell = lax.broadcasted_iota(jnp.int32, (1, depth), 1)
            mask = (cell < extent).astype(jnp.float32)
            for k, g in enumerate(gathers):
                total = acc[w, i, g][:OFFS] + recv[w - 2, i, OFFS * k : OFFS * (k + 1)]
                out_ref[tile, g] = total * (1.0 / math.sqrt(steps * times)) * mask

    for copy in own_copies:
        copy.wait()
    for w in range(4):
        own_centre(w)

    pc_copies = []
    for w in range(2):
        far_centre(w)
        copy = partial_copy(w, pc_send, pc_recv, 0)
        copy.start()
        pc_copies.append(copy)

    @pl.loop(1, devices)
    def _(j):
        a_copy(j).wait()

    b_copies = []
    for w in range(4):
        unpack(first_tile(owner_there, w), b_send, w)
        copy = pltpu.make_async_remote_copy(
            src_ref=b_send.at[w],
            dst_ref=b_recv.at[w],
            send_sem=b_send_sem.at[w],
            recv_sem=b_recv_sem.at[w],
            device_id=(me_tile, partner[w]),
            device_id_type=MESH,
        )
        copy.start()
        b_copies.append(copy)
    for w in range(4):
        unpack(first_tile(owner, w), b_own, w)
        own_edge(w)

    pe_copies = []
    for w in range(2):
        far_edge(w)
        copy = partial_copy(w, pe_send, pe_recv, 1)
        copy.start()
        pe_copies.append(copy)
    for w in (2, 3):
        far_centre(w)
    for w in (2, 3):
        far_edge(w)
    for w in (2, 3):
        pc_copies[w - 2].wait_recv()
        finish(w, inner, pc_recv)
    for w in (2, 3):
        pe_copies[w - 2].wait_recv()
        finish(w, outer, pe_recv)

    for copies in main_copies:
        for copy in copies:
            copy.wait_send()
    for copy in b_copies + pc_copies + pe_copies:
        copy.wait_send()


def paired(src_snap, rcv_snap, q_rate, nbr_device, nbr_index, depth_extent):
    tiles, steps, width, depth = src_snap.shape
    devices = lax.axis_size("tile")
    times = lax.axis_size("tm")
    capacity = (2 * tiles + devices - 1) // devices + 1
    share = tiles // times
    half = share // 2
    pieces = 2 * steps
    a_blocks = capacity * pieces + -(-capacity * pieces // ROWS)
    b_blocks = 2 * half * steps * 2 + -(-half * pieces // ROWS)
    inner_rows = -(-(GB - 3) * OFFS // 8) * 8
    outer_rows = -(-3 * OFFS // 8) * 8
    sizes = (tiles, steps, width, depth, devices, times, capacity, share)
    bf16, f32 = jnp.bfloat16, jnp.float32
    products = share * GB * OFFS * depth * steps * times
    return pl.pallas_call(
        functools.partial(pair_kernel, sizes),
        out_shape=jax.ShapeDtypeStruct((share, GB, OFFS, depth), f32),
        in_specs=[pl.BlockSpec(memory_space=pltpu.SMEM)] * 3
        + [pl.BlockSpec(memory_space=pltpu.VMEM)]
        + [pl.BlockSpec(memory_space=pl.ANY)] * 2,
        out_specs=pl.BlockSpec(memory_space=pltpu.VMEM),
        scratch_shapes=[
            pltpu.SMEM((2, tiles), jnp.int32),
            pltpu.VMEM((2, 3, tiles, steps, ROWS, depth), bf16),
            pltpu.VMEM((devices, a_blocks, ROWS, depth), bf16),
            pltpu.VMEM((devices, a_blocks, ROWS, depth), bf16),
            pltpu.VMEM((4, b_blocks, ROWS, depth), bf16),
            pltpu.VMEM((4, b_blocks, ROWS, depth), bf16),
            pltpu.VMEM((4, b_blocks, ROWS, depth), bf16),
            pltpu.VMEM((2, 2, 4, half, steps, width, depth), bf16),
            pltpu.VMEM((4, half, GB, SPAN, depth), f32),
            pltpu.VMEM((2, half, inner_rows, depth), f32),
            pltpu.VMEM((2, half, inner_rows, depth), f32),
            pltpu.VMEM((2, half, outer_rows, depth), f32),
            pltpu.VMEM((2, half, outer_rows, depth), f32),
            pltpu.SemaphoreType.DMA((6,)),
            pltpu.SemaphoreType.DMA((4, 2)),
            pltpu.SemaphoreType.DMA((4, 2)),
            pltpu.SemaphoreType.DMA((4, 2)),
            pltpu.SemaphoreType.DMA((devices,)),
            pltpu.SemaphoreType.DMA((devices,)),
            pltpu.SemaphoreType.DMA((4,)),
            pltpu.SemaphoreType.DMA((4,)),
            pltpu.SemaphoreType.DMA((2, 2)),
            pltpu.SemaphoreType.DMA((2, 2)),
        ],
        compiler_params=pltpu.CompilerParams(
            collective_id=1, has_side_effects=True, vmem_limit_bytes=60 * 1024 * 1024
        ),
        cost_estimate=pl.CostEstimate(
            flops=3 * products, bytes_accessed=4 * tiles * steps * width * depth, transcendentals=0
        ),
    )(nbr_device.T, nbr_index.T, depth_extent, q_rate.reshape(1, depth), src_snap, rcv_snap)


def solution(mesh):
    placed = (P("tile", "tm", None, None), P("tile", "tm", None, None), P(), P(), P(), P("tile"))
    body = paired if mesh.shape["tm"] == 4 else local
    return jax.shard_map(
        body,
        mesh=mesh,
        in_specs=placed,
        out_specs=P(("tile", "tm"), None, None, None),
        check_vma=False,
    )
```

```python
import functools
import math

import jax
import jax.numpy as jnp
from jax import lax
from jax.experimental import pallas as pl
from jax.experimental.pallas import tpu as pltpu
from jax.sharding import PartitionSpec as P

GSTEP = 16
HMAX = 24
GB = 8
OFFS = 49
RIM_L = 16
RIM_R = 17
ROWS = 16
SPAN = 56
MESH = pl.DeviceIdType.MESH


def one_hot(rows, columns, rule):
    row = lax.broadcasted_iota(jnp.int32, (rows, columns), 0)
    column = lax.broadcasted_iota(jnp.int32, (rows, columns), 1)
    return rule(row, column).astype(jnp.float32).astype(jnp.bfloat16)


def pick(matrix, values):
    return jnp.dot(matrix, values, preferred_element_type=jnp.float32)


def kernel(
    sizes,
    send_tab,
    arrive_tab,
    extent_ref,
    rate_ref,
    src_ref,
    rcv_ref,
    out_ref,
    edge_cells,
    a_send,
    a_recv,
    b_send,
    b_recv,
    centre,
    acc,
    edge_sem,
    own_sem,
    main_send_sem,
    main_recv_sem,
    a_send_sem,
    a_recv_sem,
    b_send_sem,
    b_recv_sem,
):
    tiles, steps, width, depth, devices, times, capacity, share = sizes
    pieces = 2 * steps
    fields = (src_ref, rcv_ref)
    me_tile = lax.axis_index("tile")
    me_tm = lax.axis_index("tm")

    def rest(count, me, j):
        return lax.rem(me + j, count)

    edge_copies = []
    for f in range(2):
        for k, first in enumerate((width - ROWS, 0, ROWS)):
            copy = pltpu.make_async_copy(
                fields[f].at[:, :, pl.ds(first, ROWS), :],
                edge_cells.at[f, k],
                edge_sem.at[f * 3 + k],
            )
            copy.start()
            edge_copies.append(copy)
    own_copies = []
    for f in range(2):
        copy = pltpu.make_async_copy(
            fields[f].at[pl.ds(me_tm * share, share)], centre.at[f, me_tm], own_sem.at[f]
        )
        copy.start()
        own_copies.append(copy)

    barrier = pltpu.get_barrier_semaphore()
    for j in range(1, times):
        pl.semaphore_signal(
            barrier, inc=1, device_id=(me_tile, rest(times, me_tm, j)), device_id_type=MESH
        )
    for j in range(1, devices):
        pl.semaphore_signal(
            barrier, inc=1, device_id=(rest(devices, me_tile, j), me_tm), device_id_type=MESH
        )
    pl.semaphore_wait(barrier, times + devices - 2)

    main_copies = []
    for j in range(1, times):
        to = rest(times, me_tm, j)
        for f in range(2):
            copy = pltpu.make_async_remote_copy(
                src_ref=fields[f].at[pl.ds(to * share, share)],
                dst_ref=centre.at[f, me_tm],
                send_sem=main_send_sem.at[j, f],
                recv_sem=main_recv_sem.at[j, f],
                device_id=(me_tile, to),
                device_id_type=MESH,
            )
            copy.start()
            main_copies.append(copy)

    for copy in edge_copies:
        copy.wait()

    a_extra = a_send.shape[1] - capacity * pieces
    compress = one_hot(
        a_extra * ROWS, capacity * pieces * ROWS, lambda row, column: column == row * ROWS
    )

    def pack(to):
        extra = []
        for k in range(capacity):
            index = send_tab[0, to, k]
            side = send_tab[1, to, k]
            for f in range(2):
                first = k * pieces + f * steps
                a_send[to, first : first + steps] = edge_cells[f, side, index]
                extra.append(edge_cells[f, 2, index].reshape(steps * ROWS, depth))
        packed = pick(compress, jnp.concatenate(extra, axis=0))
        a_send[to, capacity * pieces :] = packed.astype(jnp.bfloat16).reshape(
            a_extra, ROWS, depth
        )

    def a_copy(j):
        to = rest(devices, me_tile, j)
        return pltpu.make_async_remote_copy(
            src_ref=a_send.at[to],
            dst_ref=a_recv.at[me_tile],
            send_sem=a_send_sem.at[j],
            recv_sem=a_recv_sem.at[j],
            device_id=(to, me_tm),
            device_id_type=MESH,
        )

    @pl.loop(1, devices)
    def _(j):
        pack(rest(devices, me_tile, j))
        a_copy(j).start()

    pack(me_tile)
    a_recv[me_tile] = a_send[me_tile]

    rate = rate_ref[...]

    def weight(part, t):
        step = (part * steps + t).astype(jnp.float32)
        return jnp.exp(rate * step / (steps * times))

    turn_centre = one_hot(
        width - 8, width, lambda row, column: column == width - ROWS - row
    )
    last = width // GSTEP * GSTEP - HMAX * 2

    def centre_pass(part, fresh):
        @pl.loop(0, share)
        def _(i):
            sums = [None] * GB
            for t in range(steps):
                turned = pick(turn_centre, centre[0, part, i, t]) * weight(part, t)
                straight = centre[1, part, i, t].astype(jnp.float32)
                for g in range(1, GB - 2):
                    back = last - GSTEP * g
                    ahead = GSTEP * (g - 1)
                    product = turned[back : back + SPAN] * straight[ahead : ahead + SPAN]
                    sums[g] = product if sums[g] is None else sums[g] + product
            for g in range(1, GB - 2):
                if fresh:
                    acc[i, g] = sums[g]
                else:
                    acc[i, g] += sums[g]

    for copy in own_copies:
        copy.wait()
    centre_pass(me_tm, True)

    @pl.loop(1, devices)
    def _(j):
        a_copy(j).wait()

    b_rims = 2 * share * steps * 2
    b_extra = b_send.shape[1] - b_rims

    def unpack(to):
        packed = None
        for i in range(share):
            tile = to * share + i
            for side in range(2):
                source = arrive_tab[0, 2 * tile + side]
                rank = arrive_tab[1, 2 * tile + side]
                rim = a_recv[source, pl.ds(rank * pieces, pieces)]
                for f in range(2):
                    for t in range(steps):
                        b_send[to, ((f * share + i) * steps + t) * 2 + side] = rim[f * steps + t]
            extra = a_recv[source, capacity * pieces :].reshape(a_extra * ROWS, depth)
            choose = one_hot(
                b_extra * ROWS,
                a_extra * ROWS,
                lambda row, column: (row >= i * pieces)
                & (row < (i + 1) * pieces)
                & (column == rank * pieces + row - i * pieces),
            )
            chosen = pick(choose, extra)
            packed = chosen if packed is None else packed + chosen
        b_send[to, b_rims:] = packed.astype(jnp.bfloat16).reshape(b_extra, ROWS, depth)

    def b_copy(j):
        to = rest(times, me_tm, j)
        return pltpu.make_async_remote_copy(
            src_ref=b_send.at[to],
            dst_ref=b_recv.at[me_tm],
            send_sem=b_send_sem.at[j],
            recv_sem=b_recv_sem.at[j],
            device_id=(me_tile, to),
            device_id_type=MESH,
        )

    @pl.loop(1, times)
    def _(j):
        unpack(rest(times, me_tm, j))
        b_copy(j).start()

    unpack(me_tm)
    b_recv[me_tm] = b_send[me_tm]

    def finish(gathers):
        @pl.loop(0, share)
        def _(i):
            extent = extent_ref[me_tm * share + i]
            cell = lax.broadcasted_iota(jnp.int32, (1, depth), 1)
            mask = (cell < extent).astype(jnp.float32)
            for g in gathers:
                out_ref[i, g] = (
                    acc[i, g][:OFFS] * (1.0 / math.sqrt(steps * times)) * mask
                )

    turn_first = one_hot(SPAN, 4 * ROWS, lambda row, column: column == OFFS - 1 - row)
    turn_last = one_hot(SPAN + ROWS, 4 * ROWS, lambda row, column: column == 4 * ROWS - row)
    wide = width - 3 * ROWS

    def edge_pass(part, fresh):
        @pl.loop(0, share)
        def _(i):
            extra = b_recv[part, b_rims:].reshape(b_extra * ROWS, depth)
            sums = [None] * 3
            for t in range(steps):
                scale = weight(part, t)
                place = i * pieces + t
                rims = (i * steps + t) * 2
                rims_rcv = ((share + i) * steps + t) * 2
                src_left = b_recv[part, rims]
                src_right = b_recv[part, rims + 1]
                rcv_left = b_recv[part, rims_rcv]
                rcv_right = b_recv[part, rims_rcv + 1]
                turned = pick(
                    turn_first,
                    jnp.concatenate([src_left, centre[0, part, i, t, : 3 * ROWS]], axis=0),
                )
                straight = jnp.concatenate(
                    [rcv_left, centre[1, part, i, t, : 3 * ROWS]], axis=0
                ).astype(jnp.float32)
                products = [turned * scale * straight[:SPAN]]
                turn_extra = one_hot(
                    SPAN + ROWS,
                    b_extra * ROWS,
                    lambda row, column: (row == 0) & (column == place),
                )
                turned = pick(
                    turn_last,
                    jnp.concatenate([centre[0, part, i, t, wide:], src_right], axis=0),
                ) + pick(turn_extra, extra)
                turned = turned * scale
                rcv_extra = pick(
                    one_hot(
                        8,
                        b_extra * ROWS,
                        lambda row, column: (row == 0) & (column == place + steps),
                    ),
                    extra,
                )
                straight = jnp.concatenate(
                    [
                        centre[1, part, i, t, wide:].astype(jnp.float32),
                        rcv_right.astype(jnp.float32),
                        rcv_extra,
                    ],
                    axis=0,
                )
                products.append(turned[ROWS:] * straight[:SPAN])
                products.append(turned[:SPAN] * straight[ROWS:])
                sums = [
                    product if total is None else total + product
                    for total, product in zip(sums, products)
                ]
            for g, total in zip((0, GB - 2, GB - 1), sums):
                if fresh:
                    acc[i, g] = total
                else:
                    acc[i, g] += total

    edge_pass(me_tm, True)
    for j in range(1, times):
        for f in range(2):
            main_copies[2 * (j - 1) + f].wait_recv()
        centre_pass(rest(times, me_tm, times - j), False)
    finish(range(1, GB - 2))
    for j in range(1, times):
        b_copy(j).wait_recv()
        edge_pass(rest(times, me_tm, times - j), False)
    finish((0, GB - 2, GB - 1))

    for copy in main_copies:
        copy.wait_send()
    for j in range(1, times):
        b_copy(j).wait_send()


def routes(nbr_device, nbr_index, devices, capacity, tiles):
    own = lax.axis_index("tile")
    count = 2 * tiles
    device = nbr_device.reshape(devices, count)
    index = nbr_index.reshape(devices, count)
    ids = jnp.arange(count, dtype=jnp.int32)
    earlier = ids[None, :] < ids[:, None]
    same = (device[:, :, None] == device[:, None, :]) & earlier[None]
    rank = jnp.sum(same.astype(jnp.int32), axis=2)
    slot = jnp.arange(capacity, dtype=jnp.int32)
    hit = ((device == own)[:, None, :] & (rank[:, None, :] == slot[None, :, None])).astype(jnp.int32)
    wanted = jnp.stack([index, jnp.broadcast_to((ids % 2)[None, :], index.shape)])
    send_tab = jnp.sum(hit[None] * wanted[:, :, None, :], axis=3)
    arrive = jnp.stack([device, rank])
    arrive_tab = lax.dynamic_slice_in_dim(arrive, own, 1, 1)[:, 0]
    return send_tab, arrive_tab


def local(src_snap, rcv_snap, q_rate, nbr_device, nbr_index, depth_extent):
    tiles, steps, width, depth = src_snap.shape
    devices = lax.axis_size("tile")
    times = lax.axis_size("tm")
    capacity = (2 * tiles + devices - 1) // devices + 1
    share = tiles // times
    send_tab, arrive_tab = routes(nbr_device, nbr_index, devices, capacity, tiles)
    pieces = 2 * steps
    a_blocks = capacity * pieces + -(-capacity * pieces // ROWS)
    b_blocks = 2 * share * steps * 2 + -(-share * pieces // ROWS)
    sizes = (tiles, steps, width, depth, devices, times, capacity, share)
    half = jnp.bfloat16
    products = share * GB * OFFS * depth * steps * times
    return pl.pallas_call(
        functools.partial(kernel, sizes),
        out_shape=jax.ShapeDtypeStruct((share, GB, OFFS, depth), jnp.float32),
        in_specs=[pl.BlockSpec(memory_space=pltpu.SMEM)] * 3
        + [pl.BlockSpec(memory_space=pltpu.VMEM)]
        + [pl.BlockSpec(memory_space=pl.ANY)] * 2,
        out_specs=pl.BlockSpec(memory_space=pltpu.VMEM),
        scratch_shapes=[
            pltpu.VMEM((2, 3, tiles, steps, ROWS, depth), half),
            pltpu.VMEM((devices, a_blocks, ROWS, depth), half),
            pltpu.VMEM((devices, a_blocks, ROWS, depth), half),
            pltpu.VMEM((times, b_blocks, ROWS, depth), half),
            pltpu.VMEM((times, b_blocks, ROWS, depth), half),
            pltpu.VMEM((2, times, share, steps, width, depth), half),
            pltpu.VMEM((share, GB, SPAN, depth), jnp.float32),
            pltpu.SemaphoreType.DMA((6,)),
            pltpu.SemaphoreType.DMA((2,)),
            pltpu.SemaphoreType.DMA((times, 2)),
            pltpu.SemaphoreType.DMA((times, 2)),
            pltpu.SemaphoreType.DMA((devices,)),
            pltpu.SemaphoreType.DMA((devices,)),
            pltpu.SemaphoreType.DMA((times,)),
            pltpu.SemaphoreType.DMA((times,)),
        ],
        compiler_params=pltpu.CompilerParams(
            collective_id=0, has_side_effects=True, vmem_limit_bytes=40 * 1024 * 1024
        ),
        cost_estimate=pl.CostEstimate(
            flops=3 * products, bytes_accessed=4 * tiles * steps * width * depth, transcendentals=0
        ),
    )(send_tab, arrive_tab, depth_extent, q_rate.reshape(1, depth), src_snap, rcv_snap)


def pair_kernel(
    sizes,
    device_in,
    index_in,
    extent_in,
    rate_in,
    src_ref,
    rcv_ref,
    out_ref,
    device_tab,
    index_tab,
    extent_ref,
    rate_ref,
    ranks,
    edge_cells,
    a_send,
    a_recv,
    b_own,
    b_send,
    b_recv,
    centre,
    acc,
    turned_out,
    pc_send,
    pc_recv,
    pe_send,
    pe_recv,
    small_sem,
    edge_sem,
    own_sem,
    main_send_sem,
    main_recv_sem,
    a_send_sem,
    a_recv_sem,
    b_send_sem,
    b_recv_sem,
    p_send_sem,
    p_recv_sem,
):
    tiles, steps, width, depth, devices, times, capacity, share = sizes
    half = share // 2
    pieces = 2 * steps
    fields = (src_ref, rcv_ref)
    me_tile = lax.axis_index("tile")
    me_tm = lax.axis_index("tm")
    low = lax.rem(me_tm, 2)
    high = lax.div(me_tm, 2)
    by_x = high * 2 + 1 - low
    by_y = (1 - high) * 2 + low
    across = (1 - high) * 2 + 1 - low

    owner = (by_y, by_x, me_tm, me_tm)
    partner = (by_x, by_y, by_x, by_y)
    owner_there = (across, across, by_x, by_y)
    offset = (0, half, 0, half)

    def first_tile(owners, w):
        return owners[w] * share + offset[w]

    barrier = pltpu.get_barrier_semaphore()
    for to in (by_x, by_y):
        pl.semaphore_signal(barrier, inc=1, device_id=(me_tile, to), device_id_type=MESH)
    for j in range(1, devices):
        pl.semaphore_signal(
            barrier, inc=1, device_id=(lax.rem(me_tile + j, devices), me_tm), device_id_type=MESH
        )
    small_copies = []
    smalls = ((device_in, device_tab), (index_in, index_tab), (extent_in, extent_ref), (rate_in, rate_ref))
    for k, (source, target) in enumerate(smalls):
        copy = pltpu.make_async_copy(source, target, small_sem.at[k])
        copy.start()
        small_copies.append(copy)
    edge_copies = []
    for f in range(2):
        for k, first in enumerate((width - ROWS, 0, ROWS)):
            copy = pltpu.make_async_copy(
                fields[f].at[:, :, pl.ds(first, ROWS), :],
                edge_cells.at[f, k],
                edge_sem.at[f * 3 + k],
            )
            copy.start()
            edge_copies.append(copy)

    pl.semaphore_wait(barrier, devices + 1)

    main_copies = []

    def start_main(w):
        copies = []
        for f in range(2):
            copy = pltpu.make_async_remote_copy(
                src_ref=fields[f].at[pl.ds(first_tile(owner_there, w), half)],
                dst_ref=centre.at[f, 1, w],
                send_sem=main_send_sem.at[w, f],
                recv_sem=main_recv_sem.at[w, f],
                device_id=(me_tile, partner[w]),
                device_id_type=MESH,
            )
            copy.start()
            copies.append(copy)
        main_copies.append(copies)

    for w in range(2):
        start_main(w)
    own_copies = []
    for w in range(4):
        for f in range(2):
            copy = pltpu.make_async_copy(
                fields[f].at[pl.ds(first_tile(owner, w), half)],
                centre.at[f, 0, w],
                own_sem.at[w, f],
            )
            copy.start()
            own_copies.append(copy)

    for copy in small_copies + edge_copies:
        copy.wait()

    a_extra = a_send.shape[1] - capacity * pieces
    compress = one_hot(
        a_extra * ROWS, capacity * pieces * ROWS, lambda row, column: column == row * ROWS
    )

    def pack(to):
        def scan(row, carry):
            count, codes = carry
            for side in range(2):
                hit = device_tab[side, to * tiles + row] == me_tile
                code = index_tab[side, to * tiles + row] * 2 + side
                codes = tuple(
                    jnp.where(hit & (count == k), code, codes[k]) for k in range(capacity)
                )
                count = count + hit.astype(jnp.int32)
            return count, codes

        zero = jnp.int32(0)
        _, codes = lax.fori_loop(0, tiles, scan, (zero, (zero,) * capacity))
        extra = []
        for k in range(capacity):
            index = lax.div(codes[k], 2)
            side = lax.rem(codes[k], 2)
            for f in range(2):
                first = k * pieces + f * steps
                a_send[to, first : first + steps] = edge_cells[f, side, index]
                extra.append(edge_cells[f, 2, index].reshape(steps * ROWS, depth))
        packed = pick(compress, jnp.concatenate(extra, axis=0))
        a_send[to, capacity * pieces :] = packed.astype(jnp.bfloat16).reshape(
            a_extra, ROWS, depth
        )

    def other(j):
        total, unit = jnp.int32(0), 1
        while unit < devices:
            mine = lax.rem(lax.div(me_tile, unit), 2)
            flip = lax.rem(lax.div(j, unit), 2)
            total = total + (mine + flip - 2 * mine * flip) * unit
            unit *= 2
        return total

    def a_copy(j):
        to = other(j)
        return pltpu.make_async_remote_copy(
            src_ref=a_send.at[to],
            dst_ref=a_recv.at[me_tile],
            send_sem=a_send_sem.at[j],
            recv_sem=a_recv_sem.at[j],
            device_id=(to, me_tm),
            device_id_type=MESH,
        )

    @pl.loop(1, devices)
    def _(back):
        j = devices - back
        pack(other(j))
        a_copy(j).start()

    for w in (2, 3):
        start_main(w)
    pack(me_tile)
    a_recv[me_tile] = a_send[me_tile]

    base = me_tile * tiles

    @pl.loop(0, tiles)
    def _(row):
        mine = [device_tab[side, base + row] for side in range(2)]

        def count(other, sums):
            theirs = [device_tab[side, base + other] for side in range(2)]
            return tuple(
                sums[side]
                + (theirs[0] == mine[side]).astype(jnp.int32)
                + (theirs[1] == mine[side]).astype(jnp.int32)
                for side in range(2)
            )

        found = lax.fori_loop(0, row, count, (jnp.int32(0), jnp.int32(0)))
        for side in range(2):
            ranks[side, row] = jnp.minimum(found[side], capacity - 1)

    rate = rate_ref[...]

    def weight(part, t):
        step = (part * steps + t).astype(jnp.float32)
        return jnp.exp(rate * step / (steps * times))

    inner = range(1, GB - 2)
    outer = (0, GB - 2, GB - 1)
    turn_centre = one_hot(
        width - 8, width, lambda row, column: column == width - ROWS - row
    )
    last = width // GSTEP * GSTEP - HMAX * 2

    def centre_sums(w, p, part, i):
        sums = [None] * GB
        for t in range(steps):
            turned = pick(turn_centre, centre[0, p, w, i, t]) * weight(part, t)
            straight = centre[1, p, w, i, t].astype(jnp.float32)
            for g in inner:
                back = last - GSTEP * g
                ahead = GSTEP * (g - 1)
                product = turned[back : back + SPAN] * straight[ahead : ahead + SPAN]
                sums[g] = product if sums[g] is None else sums[g] + product
        return sums

    turn_first = one_hot(SPAN, 4 * ROWS, lambda row, column: column == OFFS - 1 - row)
    turn_last = one_hot(SPAN + ROWS, 4 * ROWS, lambda row, column: column == 4 * ROWS - row)
    wide = width - 3 * ROWS
    b_rims = 2 * half * steps * 2
    b_extra = b_send.shape[1] - b_rims

    def edge_sums(rims_ref, w, p, part, i):
        extra = rims_ref[w, b_rims:].reshape(b_extra * ROWS, depth)
        sums = [None] * 3
        for t in range(steps):
            scale = weight(part, t)
            place = i * pieces + t
            rims = (i * steps + t) * 2
            rims_rcv = ((half + i) * steps + t) * 2
            turned = pick(
                turn_first,
                jnp.concatenate([rims_ref[w, rims], centre[0, p, w, i, t, : 3 * ROWS]], axis=0),
            )
            straight = jnp.concatenate(
                [rims_ref[w, rims_rcv], centre[1, p, w, i, t, : 3 * ROWS]], axis=0
            ).astype(jnp.float32)
            products = [turned * scale * straight[:SPAN]]
            turn_extra = one_hot(
                SPAN + ROWS,
                b_extra * ROWS,
                lambda row, column: (row == 0) & (column == place),
            )
            turned = pick(
                turn_last,
                jnp.concatenate(
                    [centre[0, p, w, i, t, wide:], rims_ref[w, rims + 1]], axis=0
                ),
            ) + pick(turn_extra, extra)
            turned = turned * scale
            rcv_extra = pick(
                one_hot(
                    8,
                    b_extra * ROWS,
                    lambda row, column: (row == 0) & (column == place + steps),
                ),
                extra,
            )
            straight = jnp.concatenate(
                [
                    centre[1, p, w, i, t, wide:].astype(jnp.float32),
                    rims_ref[w, rims_rcv + 1].astype(jnp.float32),
                    rcv_extra,
                ],
                axis=0,
            )
            products.append(turned[ROWS:] * straight[:SPAN])
            products.append(turned[:SPAN] * straight[ROWS:])
            sums = [
                product if total is None else total + product
                for total, product in zip(sums, products)
            ]
        return sums

    def own_centre(w):
        @pl.loop(0, half)
        def _(i):
            sums = centre_sums(w, 0, me_tm, i)
            for g in inner:
                acc[w, i, g] = sums[g]

    def own_edge(w):
        @pl.loop(0, half)
        def _(i):
            for g, total in zip(outer, edge_sums(b_own, w, 0, me_tm, i)):
                acc[w, i, g] = total

    def far_centre(w):
        for copy in main_copies[w]:
            copy.wait_recv()

        @pl.loop(0, half)
        def _(i):
            sums = centre_sums(w, 1, partner[w], i)
            for k, g in enumerate(inner):
                total = acc[w, i, g] + sums[g]
                if w < 2:
                    pc_send[w, i, OFFS * k : OFFS * (k + 1)] = total[:OFFS]
                else:
                    acc[w, i, g] = total

    def far_edge(w):
        b_copies[w].wait_recv()

        @pl.loop(0, half)
        def _(i):
            sums = edge_sums(b_recv, w, 1, partner[w], i)
            for k, g in enumerate(outer):
                total = acc[w, i, g] + sums[k]
                if w < 2:
                    pe_send[w, i, OFFS * k : OFFS * (k + 1)] = total[:OFFS]
                else:
                    acc[w, i, g] = total

    def partial_copy(w, send, recv, k):
        return pltpu.make_async_remote_copy(
            src_ref=send.at[w],
            dst_ref=recv.at[w],
            send_sem=p_send_sem.at[k, w],
            recv_sem=p_recv_sem.at[k, w],
            device_id=(me_tile, owner[w]),
            device_id_type=MESH,
        )

    def unpack(first, target, w):
        packed = None
        for i in range(half):
            tile = first + i
            for side in range(2):
                source = device_tab[side, base + tile]
                rank = ranks[side, tile]
                rim = a_recv[source, pl.ds(rank * pieces, pieces)]
                for f in range(2):
                    for t in range(steps):
                        target[w, ((f * half + i) * steps + t) * 2 + side] = rim[f * steps + t]
            extra = a_recv[source, capacity * pieces :].reshape(a_extra * ROWS, depth)
            choose = one_hot(
                b_extra * ROWS,
                a_extra * ROWS,
                lambda row, column: (row >= i * pieces)
                & (row < (i + 1) * pieces)
                & (column == rank * pieces + row - i * pieces),
            )
            chosen = pick(choose, extra)
            packed = chosen if packed is None else packed + chosen
        target[w, b_rims:] = packed.astype(jnp.bfloat16).reshape(b_extra, ROWS, depth)

    def finish(w, gathers, recv):
        @pl.loop(0, half)
        def _(i):
            tile = offset[w] + i
            for k, g in enumerate(gathers):
                total = acc[w, i, g][:OFFS] + recv[w - 2, i, OFFS * k : OFFS * (k + 1)]
                for part in range(depth // 128):
                    turned_out[tile, part, pl.ds(g, OFFS, stride=GB), :] = total[
                        :, 128 * part : 128 * (part + 1)
                    ]
            if gathers != outer:
                return
            extent = extent_ref[me_tm * share + tile]
            cell = lax.broadcasted_iota(jnp.int32, (1, 128), 1)
            for part in range(depth // 128):
                mask = (cell + 128 * part < extent).astype(jnp.float32)
                out_ref[tile, :, 128 * part : 128 * (part + 1)] = (
                    turned_out[tile, part] * (1.0 / math.sqrt(steps * times)) * mask
                )

    for copy in own_copies:
        copy.wait()
    for w in range(4):
        own_centre(w)

    pc_copies = []
    for w in range(2):
        far_centre(w)
        copy = partial_copy(w, pc_send, pc_recv, 0)
        copy.start()
        pc_copies.append(copy)
    for w in (2, 3):
        far_centre(w)

    @pl.loop(1, devices)
    def _(j):
        a_copy(j).wait()

    b_copies = []
    for w in range(4):
        unpack(first_tile(owner_there, w), b_send, w)
        copy = pltpu.make_async_remote_copy(
            src_ref=b_send.at[w],
            dst_ref=b_recv.at[w],
            send_sem=b_send_sem.at[w],
            recv_sem=b_recv_sem.at[w],
            device_id=(me_tile, partner[w]),
            device_id_type=MESH,
        )
        copy.start()
        b_copies.append(copy)
    for w in range(2):
        unpack(first_tile(owner, w), b_own, w)
        own_edge(w)

    pe_copies = []
    for w in range(2):
        far_edge(w)
        copy = partial_copy(w, pe_send, pe_recv, 1)
        copy.start()
        pe_copies.append(copy)
    for w in (2, 3):
        unpack(first_tile(owner, w), b_own, w)
        own_edge(w)
        far_edge(w)
    for w in (2, 3):
        pc_copies[w - 2].wait_recv()
        finish(w, inner, pc_recv)
    for w in (2, 3):
        pe_copies[w - 2].wait_recv()
        finish(w, outer, pe_recv)

    for copies in main_copies:
        for copy in copies:
            copy.wait_send()
    for copy in b_copies + pc_copies + pe_copies:
        copy.wait_send()


def paired(src_snap, rcv_snap, q_rate, nbr_device, nbr_index, depth_extent):
    tiles, steps, width, depth = src_snap.shape
    devices = lax.axis_size("tile")
    times = lax.axis_size("tm")
    capacity = (2 * tiles + devices - 1) // devices + 1
    share = tiles // times
    half = share // 2
    pieces = 2 * steps
    a_blocks = capacity * pieces + -(-capacity * pieces // ROWS)
    b_blocks = 2 * half * steps * 2 + -(-half * pieces // ROWS)
    inner_rows = -(-(GB - 3) * OFFS // 8) * 8
    outer_rows = -(-3 * OFFS // 8) * 8
    sizes = (tiles, steps, width, depth, devices, times, capacity, share)
    bf16, f32 = jnp.bfloat16, jnp.float32
    products = share * GB * OFFS * depth * steps * times
    image = pl.pallas_call(
        functools.partial(pair_kernel, sizes),
        out_shape=jax.ShapeDtypeStruct((share, OFFS * GB, depth), f32),
        in_specs=[pl.BlockSpec(memory_space=pltpu.HBM)] * 6,
        out_specs=pl.BlockSpec(memory_space=pltpu.VMEM),
        scratch_shapes=[
            pltpu.SMEM(nbr_device.shape[::-1], jnp.int32),
            pltpu.SMEM(nbr_index.shape[::-1], jnp.int32),
            pltpu.SMEM(depth_extent.shape, jnp.int32),
            pltpu.VMEM((1, depth), f32),
            pltpu.SMEM((2, tiles), jnp.int32),
            pltpu.VMEM((2, 3, tiles, steps, ROWS, depth), bf16),
            pltpu.VMEM((devices, a_blocks, ROWS, depth), bf16),
            pltpu.VMEM((devices, a_blocks, ROWS, depth), bf16),
            pltpu.VMEM((4, b_blocks, ROWS, depth), bf16),
            pltpu.VMEM((4, b_blocks, ROWS, depth), bf16),
            pltpu.VMEM((4, b_blocks, ROWS, depth), bf16),
            pltpu.VMEM((2, 2, 4, half, steps, width, depth), bf16),
            pltpu.VMEM((4, half, GB, SPAN, depth), f32),
            pltpu.VMEM((share, depth // 128, OFFS * GB, 128), f32),
            pltpu.VMEM((2, half, inner_rows, depth), f32),
            pltpu.VMEM((2, half, inner_rows, depth), f32),
            pltpu.VMEM((2, half, outer_rows, depth), f32),
            pltpu.VMEM((2, half, outer_rows, depth), f32),
            pltpu.SemaphoreType.DMA((4,)),
            pltpu.SemaphoreType.DMA((6,)),
            pltpu.SemaphoreType.DMA((4, 2)),
            pltpu.SemaphoreType.DMA((4, 2)),
            pltpu.SemaphoreType.DMA((4, 2)),
            pltpu.SemaphoreType.DMA((devices,)),
            pltpu.SemaphoreType.DMA((devices,)),
            pltpu.SemaphoreType.DMA((4,)),
            pltpu.SemaphoreType.DMA((4,)),
            pltpu.SemaphoreType.DMA((2, 2)),
            pltpu.SemaphoreType.DMA((2, 2)),
        ],
        compiler_params=pltpu.CompilerParams(
            collective_id=1, has_side_effects=True, vmem_limit_bytes=60 * 1024 * 1024
        ),
        cost_estimate=pl.CostEstimate(
            flops=3 * products, bytes_accessed=4 * tiles * steps * width * depth, transcendentals=0
        ),
    )(nbr_device.T, nbr_index.T, depth_extent, q_rate.reshape(1, depth), src_snap, rcv_snap)
    return image.reshape(share, OFFS, GB, depth).transpose(0, 2, 1, 3)


def solution(mesh):
    placed = (P("tile", "tm", None, None), P("tile", "tm", None, None), P(), P(), P(), P("tile"))
    body = paired if mesh.shape["tm"] == 4 else local
    return jax.shard_map(
        body,
        mesh=mesh,
        in_specs=placed,
        out_specs=P(("tile", "tm"), None, None, None),
        check_vma=False,
    )
```

```python
import functools
import math

import jax
import jax.numpy as jnp
from jax import lax
from jax.experimental import pallas as pl
from jax.experimental.pallas import tpu as pltpu
from jax.sharding import PartitionSpec as P

GSTEP = 16
HMAX = 24
GB = 8
OFFS = 49
RIM_L = 16
RIM_R = 17
ROWS = 16
SPAN = 56
MESH = pl.DeviceIdType.MESH


def one_hot(rows, columns, rule):
    row = lax.broadcasted_iota(jnp.int32, (rows, columns), 0)
    column = lax.broadcasted_iota(jnp.int32, (rows, columns), 1)
    return rule(row, column).astype(jnp.float32).astype(jnp.bfloat16)


def pick(matrix, values):
    return jnp.dot(matrix, values, preferred_element_type=jnp.float32)


def kernel(
    sizes,
    send_tab,
    arrive_tab,
    extent_ref,
    rate_ref,
    src_ref,
    rcv_ref,
    out_ref,
    edge_cells,
    a_send,
    a_recv,
    b_send,
    b_recv,
    centre,
    acc,
    edge_sem,
    own_sem,
    main_send_sem,
    main_recv_sem,
    a_send_sem,
    a_recv_sem,
    b_send_sem,
    b_recv_sem,
):
    tiles, steps, width, depth, devices, times, capacity, share = sizes
    pieces = 2 * steps
    fields = (src_ref, rcv_ref)
    me_tile = lax.axis_index("tile")
    me_tm = lax.axis_index("tm")

    def rest(count, me, j):
        return lax.rem(me + j, count)

    edge_copies = []
    for f in range(2):
        for k, first in enumerate((width - ROWS, 0, ROWS)):
            copy = pltpu.make_async_copy(
                fields[f].at[:, :, pl.ds(first, ROWS), :],
                edge_cells.at[f, k],
                edge_sem.at[f * 3 + k],
            )
            copy.start()
            edge_copies.append(copy)
    own_copies = []
    for f in range(2):
        copy = pltpu.make_async_copy(
            fields[f].at[pl.ds(me_tm * share, share)], centre.at[f, me_tm], own_sem.at[f]
        )
        copy.start()
        own_copies.append(copy)

    barrier = pltpu.get_barrier_semaphore()
    for j in range(1, times):
        pl.semaphore_signal(
            barrier, inc=1, device_id=(me_tile, rest(times, me_tm, j)), device_id_type=MESH
        )
    for j in range(1, devices):
        pl.semaphore_signal(
            barrier, inc=1, device_id=(rest(devices, me_tile, j), me_tm), device_id_type=MESH
        )
    pl.semaphore_wait(barrier, times + devices - 2)

    main_copies = []
    for j in range(1, times):
        to = rest(times, me_tm, j)
        for f in range(2):
            copy = pltpu.make_async_remote_copy(
                src_ref=fields[f].at[pl.ds(to * share, share)],
                dst_ref=centre.at[f, me_tm],
                send_sem=main_send_sem.at[j, f],
                recv_sem=main_recv_sem.at[j, f],
                device_id=(me_tile, to),
                device_id_type=MESH,
            )
            copy.start()
            main_copies.append(copy)

    for copy in edge_copies:
        copy.wait()

    a_extra = a_send.shape[1] - capacity * pieces
    compress = one_hot(
        a_extra * ROWS, capacity * pieces * ROWS, lambda row, column: column == row * ROWS
    )

    def pack(to):
        extra = []
        for k in range(capacity):
            index = send_tab[0, to, k]
            side = send_tab[1, to, k]
            for f in range(2):
                first = k * pieces + f * steps
                a_send[to, first : first + steps] = edge_cells[f, side, index]
                extra.append(edge_cells[f, 2, index].reshape(steps * ROWS, depth))
        packed = pick(compress, jnp.concatenate(extra, axis=0))
        a_send[to, capacity * pieces :] = packed.astype(jnp.bfloat16).reshape(
            a_extra, ROWS, depth
        )

    def a_copy(j):
        to = rest(devices, me_tile, j)
        return pltpu.make_async_remote_copy(
            src_ref=a_send.at[to],
            dst_ref=a_recv.at[me_tile],
            send_sem=a_send_sem.at[j],
            recv_sem=a_recv_sem.at[j],
            device_id=(to, me_tm),
            device_id_type=MESH,
        )

    @pl.loop(1, devices)
    def _(j):
        pack(rest(devices, me_tile, j))
        a_copy(j).start()

    pack(me_tile)
    a_recv[me_tile] = a_send[me_tile]

    rate = rate_ref[...]

    def weight(part, t):
        step = (part * steps + t).astype(jnp.float32)
        return jnp.exp(rate * step / (steps * times))

    turn_centre = one_hot(
        width - 8, width, lambda row, column: column == width - ROWS - row
    )
    last = width // GSTEP * GSTEP - HMAX * 2

    def centre_pass(part, fresh):
        @pl.loop(0, share)
        def _(i):
            sums = [None] * GB
            for t in range(steps):
                turned = pick(turn_centre, centre[0, part, i, t]) * weight(part, t)
                straight = centre[1, part, i, t].astype(jnp.float32)
                for g in range(1, GB - 2):
                    back = last - GSTEP * g
                    ahead = GSTEP * (g - 1)
                    product = turned[back : back + SPAN] * straight[ahead : ahead + SPAN]
                    sums[g] = product if sums[g] is None else sums[g] + product
            for g in range(1, GB - 2):
                if fresh:
                    acc[i, g] = sums[g]
                else:
                    acc[i, g] += sums[g]

    for copy in own_copies:
        copy.wait()
    centre_pass(me_tm, True)

    @pl.loop(1, devices)
    def _(j):
        a_copy(j).wait()

    b_rims = 2 * share * steps * 2
    b_extra = b_send.shape[1] - b_rims

    def unpack(to):
        packed = None
        for i in range(share):
            tile = to * share + i
            for side in range(2):
                source = arrive_tab[0, 2 * tile + side]
                rank = arrive_tab[1, 2 * tile + side]
                rim = a_recv[source, pl.ds(rank * pieces, pieces)]
                for f in range(2):
                    for t in range(steps):
                        b_send[to, ((f * share + i) * steps + t) * 2 + side] = rim[f * steps + t]
            extra = a_recv[source, capacity * pieces :].reshape(a_extra * ROWS, depth)
            choose = one_hot(
                b_extra * ROWS,
                a_extra * ROWS,
                lambda row, column: (row >= i * pieces)
                & (row < (i + 1) * pieces)
                & (column == rank * pieces + row - i * pieces),
            )
            chosen = pick(choose, extra)
            packed = chosen if packed is None else packed + chosen
        b_send[to, b_rims:] = packed.astype(jnp.bfloat16).reshape(b_extra, ROWS, depth)

    def b_copy(j):
        to = rest(times, me_tm, j)
        return pltpu.make_async_remote_copy(
            src_ref=b_send.at[to],
            dst_ref=b_recv.at[me_tm],
            send_sem=b_send_sem.at[j],
            recv_sem=b_recv_sem.at[j],
            device_id=(me_tile, to),
            device_id_type=MESH,
        )

    @pl.loop(1, times)
    def _(j):
        unpack(rest(times, me_tm, j))
        b_copy(j).start()

    unpack(me_tm)
    b_recv[me_tm] = b_send[me_tm]

    def finish(gathers):
        @pl.loop(0, share)
        def _(i):
            extent = extent_ref[me_tm * share + i]
            cell = lax.broadcasted_iota(jnp.int32, (1, depth), 1)
            mask = (cell < extent).astype(jnp.float32)
            for g in gathers:
                out_ref[i, g] = (
                    acc[i, g][:OFFS] * (1.0 / math.sqrt(steps * times)) * mask
                )

    turn_first = one_hot(SPAN, 4 * ROWS, lambda row, column: column == OFFS - 1 - row)
    turn_last = one_hot(SPAN + ROWS, 4 * ROWS, lambda row, column: column == 4 * ROWS - row)
    wide = width - 3 * ROWS

    def edge_pass(part, fresh):
        @pl.loop(0, share)
        def _(i):
            extra = b_recv[part, b_rims:].reshape(b_extra * ROWS, depth)
            sums = [None] * 3
            for t in range(steps):
                scale = weight(part, t)
                place = i * pieces + t
                rims = (i * steps + t) * 2
                rims_rcv = ((share + i) * steps + t) * 2
                src_left = b_recv[part, rims]
                src_right = b_recv[part, rims + 1]
                rcv_left = b_recv[part, rims_rcv]
                rcv_right = b_recv[part, rims_rcv + 1]
                turned = pick(
                    turn_first,
                    jnp.concatenate([src_left, centre[0, part, i, t, : 3 * ROWS]], axis=0),
                )
                straight = jnp.concatenate(
                    [rcv_left, centre[1, part, i, t, : 3 * ROWS]], axis=0
                ).astype(jnp.float32)
                products = [turned * scale * straight[:SPAN]]
                turn_extra = one_hot(
                    SPAN + ROWS,
                    b_extra * ROWS,
                    lambda row, column: (row == 0) & (column == place),
                )
                turned = pick(
                    turn_last,
                    jnp.concatenate([centre[0, part, i, t, wide:], src_right], axis=0),
                ) + pick(turn_extra, extra)
                turned = turned * scale
                rcv_extra = pick(
                    one_hot(
                        8,
                        b_extra * ROWS,
                        lambda row, column: (row == 0) & (column == place + steps),
                    ),
                    extra,
                )
                straight = jnp.concatenate(
                    [
                        centre[1, part, i, t, wide:].astype(jnp.float32),
                        rcv_right.astype(jnp.float32),
                        rcv_extra,
                    ],
                    axis=0,
                )
                products.append(turned[ROWS:] * straight[:SPAN])
                products.append(turned[:SPAN] * straight[ROWS:])
                sums = [
                    product if total is None else total + product
                    for total, product in zip(sums, products)
                ]
            for g, total in zip((0, GB - 2, GB - 1), sums):
                if fresh:
                    acc[i, g] = total
                else:
                    acc[i, g] += total

    edge_pass(me_tm, True)
    for j in range(1, times):
        for f in range(2):
            main_copies[2 * (j - 1) + f].wait_recv()
        centre_pass(rest(times, me_tm, times - j), False)
    finish(range(1, GB - 2))
    for j in range(1, times):
        b_copy(j).wait_recv()
        edge_pass(rest(times, me_tm, times - j), False)
    finish((0, GB - 2, GB - 1))

    for copy in main_copies:
        copy.wait_send()
    for j in range(1, times):
        b_copy(j).wait_send()


def routes(nbr_device, nbr_index, devices, capacity, tiles):
    own = lax.axis_index("tile")
    count = 2 * tiles
    device = nbr_device.reshape(devices, count)
    index = nbr_index.reshape(devices, count)
    ids = jnp.arange(count, dtype=jnp.int32)
    earlier = ids[None, :] < ids[:, None]
    same = (device[:, :, None] == device[:, None, :]) & earlier[None]
    rank = jnp.sum(same.astype(jnp.int32), axis=2)
    slot = jnp.arange(capacity, dtype=jnp.int32)
    hit = ((device == own)[:, None, :] & (rank[:, None, :] == slot[None, :, None])).astype(jnp.int32)
    wanted = jnp.stack([index, jnp.broadcast_to((ids % 2)[None, :], index.shape)])
    send_tab = jnp.sum(hit[None] * wanted[:, :, None, :], axis=3)
    arrive = jnp.stack([device, rank])
    arrive_tab = lax.dynamic_slice_in_dim(arrive, own, 1, 1)[:, 0]
    return send_tab, arrive_tab


def local(src_snap, rcv_snap, q_rate, nbr_device, nbr_index, depth_extent):
    tiles, steps, width, depth = src_snap.shape
    devices = lax.axis_size("tile")
    times = lax.axis_size("tm")
    capacity = (2 * tiles + devices - 1) // devices + 1
    share = tiles // times
    send_tab, arrive_tab = routes(nbr_device, nbr_index, devices, capacity, tiles)
    pieces = 2 * steps
    a_blocks = capacity * pieces + -(-capacity * pieces // ROWS)
    b_blocks = 2 * share * steps * 2 + -(-share * pieces // ROWS)
    sizes = (tiles, steps, width, depth, devices, times, capacity, share)
    half = jnp.bfloat16
    products = share * GB * OFFS * depth * steps * times
    return pl.pallas_call(
        functools.partial(kernel, sizes),
        out_shape=jax.ShapeDtypeStruct((share, GB, OFFS, depth), jnp.float32),
        in_specs=[pl.BlockSpec(memory_space=pltpu.SMEM)] * 3
        + [pl.BlockSpec(memory_space=pltpu.VMEM)]
        + [pl.BlockSpec(memory_space=pl.ANY)] * 2,
        out_specs=pl.BlockSpec(memory_space=pltpu.VMEM),
        scratch_shapes=[
            pltpu.VMEM((2, 3, tiles, steps, ROWS, depth), half),
            pltpu.VMEM((devices, a_blocks, ROWS, depth), half),
            pltpu.VMEM((devices, a_blocks, ROWS, depth), half),
            pltpu.VMEM((times, b_blocks, ROWS, depth), half),
            pltpu.VMEM((times, b_blocks, ROWS, depth), half),
            pltpu.VMEM((2, times, share, steps, width, depth), half),
            pltpu.VMEM((share, GB, SPAN, depth), jnp.float32),
            pltpu.SemaphoreType.DMA((6,)),
            pltpu.SemaphoreType.DMA((2,)),
            pltpu.SemaphoreType.DMA((times, 2)),
            pltpu.SemaphoreType.DMA((times, 2)),
            pltpu.SemaphoreType.DMA((devices,)),
            pltpu.SemaphoreType.DMA((devices,)),
            pltpu.SemaphoreType.DMA((times,)),
            pltpu.SemaphoreType.DMA((times,)),
        ],
        compiler_params=pltpu.CompilerParams(
            collective_id=0, has_side_effects=True, vmem_limit_bytes=40 * 1024 * 1024
        ),
        cost_estimate=pl.CostEstimate(
            flops=3 * products, bytes_accessed=4 * tiles * steps * width * depth, transcendentals=0
        ),
    )(send_tab, arrive_tab, depth_extent, q_rate.reshape(1, depth), src_snap, rcv_snap)


def pair_kernel(
    sizes,
    device_in,
    index_in,
    extent_in,
    rate_in,
    src_ref,
    rcv_ref,
    out_ref,
    device_tab,
    index_tab,
    extent_ref,
    rate_ref,
    ranks,
    edge_cells,
    a_send,
    a_recv,
    b_own,
    b_send,
    b_recv,
    centre,
    acc,
    acc_mid,
    turned_out,
    pc_send,
    pc_recv,
    pe_send,
    pe_recv,
    small_sem,
    edge_sem,
    own_sem,
    main_send_sem,
    main_recv_sem,
    a_send_sem,
    a_recv_sem,
    b_send_sem,
    b_recv_sem,
    p_send_sem,
    p_recv_sem,
):
    tiles, steps, width, depth, devices, times, capacity, share = sizes
    half = share // 2
    pieces = 2 * steps
    fields = (src_ref, rcv_ref)
    me_tile = lax.axis_index("tile")
    me_tm = lax.axis_index("tm")
    low = lax.rem(me_tm, 2)
    high = lax.div(me_tm, 2)
    by_x = high * 2 + 1 - low
    by_y = (1 - high) * 2 + low
    across = (1 - high) * 2 + 1 - low

    owner = (by_y, by_x, me_tm, me_tm)
    partner = (by_x, by_y, by_x, by_y)
    owner_there = (across, across, by_x, by_y)
    offset = (0, half, 0, half)

    def first_tile(owners, w):
        return owners[w] * share + offset[w]

    barrier = pltpu.get_barrier_semaphore()
    for to in (by_x, by_y):
        pl.semaphore_signal(barrier, inc=1, device_id=(me_tile, to), device_id_type=MESH)
    for j in range(1, devices):
        pl.semaphore_signal(
            barrier, inc=1, device_id=(lax.rem(me_tile + j, devices), me_tm), device_id_type=MESH
        )
    small_copies = []
    smalls = ((device_in, device_tab), (index_in, index_tab), (extent_in, extent_ref), (rate_in, rate_ref))
    for k, (source, target) in enumerate(smalls):
        copy = pltpu.make_async_copy(source, target, small_sem.at[k])
        copy.start()
        small_copies.append(copy)
    edge_copies = []
    for f in range(2):
        for k, first in enumerate((width - ROWS, 0, ROWS)):
            copy = pltpu.make_async_copy(
                fields[f].at[:, :, pl.ds(first, ROWS), :],
                edge_cells.at[f, k],
                edge_sem.at[f * 3 + k],
            )
            copy.start()
            edge_copies.append(copy)

    pl.semaphore_wait(barrier, devices + 1)

    main_copies = []

    def start_main(w):
        copies = []
        for f in range(2):
            copy = pltpu.make_async_remote_copy(
                src_ref=fields[f].at[pl.ds(first_tile(owner_there, w), half)],
                dst_ref=centre.at[f, 1, w],
                send_sem=main_send_sem.at[w, f],
                recv_sem=main_recv_sem.at[w, f],
                device_id=(me_tile, partner[w]),
                device_id_type=MESH,
            )
            copy.start()
            copies.append(copy)
        main_copies.append(copies)

    for w in range(2):
        start_main(w)
    own_copies = []
    for w in range(4):
        for f in range(2):
            copy = pltpu.make_async_copy(
                fields[f].at[pl.ds(first_tile(owner, w), half)],
                centre.at[f, 0, w],
                own_sem.at[w, f],
            )
            copy.start()
            own_copies.append(copy)

    for copy in small_copies + edge_copies:
        copy.wait()

    a_extra = a_send.shape[1] - capacity * pieces
    compress = one_hot(
        a_extra * ROWS, capacity * pieces * ROWS, lambda row, column: column == row * ROWS
    )

    def pack(to):
        def scan(row, carry):
            count, codes = carry
            for side in range(2):
                hit = device_tab[side, to * tiles + row] == me_tile
                code = index_tab[side, to * tiles + row] * 2 + side
                codes = tuple(
                    jnp.where(hit & (count == k), code, codes[k]) for k in range(capacity)
                )
                count = count + hit.astype(jnp.int32)
            return count, codes

        zero = jnp.int32(0)
        _, codes = lax.fori_loop(0, tiles, scan, (zero, (zero,) * capacity))
        extra = []
        for k in range(capacity):
            index = lax.div(codes[k], 2)
            side = lax.rem(codes[k], 2)
            for f in range(2):
                first = k * pieces + f * steps
                a_send[to, first : first + steps] = edge_cells[f, side, index]
                extra.append(edge_cells[f, 2, index].reshape(steps * ROWS, depth))
        packed = pick(compress, jnp.concatenate(extra, axis=0))
        a_send[to, capacity * pieces :] = packed.astype(jnp.bfloat16).reshape(
            a_extra, ROWS, depth
        )

    def other(j):
        total, unit = jnp.int32(0), 1
        while unit < devices:
            mine = lax.rem(lax.div(me_tile, unit), 2)
            flip = lax.rem(lax.div(j, unit), 2)
            total = total + (mine + flip - 2 * mine * flip) * unit
            unit *= 2
        return total

    def a_copy(j):
        to = other(j)
        return pltpu.make_async_remote_copy(
            src_ref=a_send.at[to],
            dst_ref=a_recv.at[me_tile],
            send_sem=a_send_sem.at[j],
            recv_sem=a_recv_sem.at[j],
            device_id=(to, me_tm),
            device_id_type=MESH,
        )

    @pl.loop(1, devices)
    def _(back):
        j = devices - back
        pack(other(j))
        a_copy(j).start()

    for w in (2, 3):
        start_main(w)
    pack(me_tile)
    a_recv[me_tile] = a_send[me_tile]

    base = me_tile * tiles

    @pl.loop(0, tiles)
    def _(row):
        mine = [device_tab[side, base + row] for side in range(2)]

        def count(other, sums):
            theirs = [device_tab[side, base + other] for side in range(2)]
            return tuple(
                sums[side]
                + (theirs[0] == mine[side]).astype(jnp.int32)
                + (theirs[1] == mine[side]).astype(jnp.int32)
                for side in range(2)
            )

        found = lax.fori_loop(0, row, count, (jnp.int32(0), jnp.int32(0)))
        for side in range(2):
            ranks[side, row] = jnp.minimum(found[side], capacity - 1)

    rate = rate_ref[...]

    def weight(part, t):
        step = (part * steps + t).astype(jnp.float32)
        return jnp.exp(rate * step / (steps * times))

    inner = range(1, GB - 2)
    outer = (0, GB - 2, GB - 1)
    middle = ((0, 16, 17, 0), (GB - 2, 1, 47, 25), (GB - 1, 17, 15, 73))
    border = (
        (0, 0, 16),
        (0, 33, 16),
        (GB - 1, 0, 17),
        (GB - 1, 32, 17),
        (GB - 2, 0, 1),
        (GB - 2, 48, 1),
    )
    turn_centre = one_hot(width + 8, width, lambda row, column: column == width - row)
    last = width // GSTEP * GSTEP + ROWS - HMAX * 2

    def centre_sums(w, p, part, i):
        sums = [None] * GB
        mids = [None] * 3
        for t in range(steps):
            turned = pick(turn_centre, centre[0, p, w, i, t]) * weight(part, t)
            straight = centre[1, p, w, i, t].astype(jnp.float32)
            products = (
                turned[width - ROWS :] * straight[:24],
                turned[: 3 * ROWS] * straight[width - 3 * ROWS :],
                turned[:ROWS] * straight[width - ROWS :],
            )
            mids = [
                product if total is None else total + product
                for total, product in zip(mids, products)
            ]
            for g in inner:
                back = last - GSTEP * g
                ahead = GSTEP * (g - 1)
                product = turned[back : back + SPAN] * straight[ahead : ahead + SPAN]
                sums[g] = product if sums[g] is None else sums[g] + product
        return sums, jnp.concatenate(mids, axis=0)

    turn_first = one_hot(SPAN, 4 * ROWS, lambda row, column: column == OFFS - 1 - row)
    turn_last = one_hot(SPAN + ROWS, 4 * ROWS, lambda row, column: column == 4 * ROWS - row)
    wide = width - 3 * ROWS
    b_rims = 2 * half * steps * 2
    b_extra = b_send.shape[1] - b_rims

    def edge_sums(rims_ref, w, p, part, i):
        extra = rims_ref[w, b_rims:].reshape(b_extra * ROWS, depth)
        sums = [None] * 3
        for t in range(steps):
            scale = weight(part, t)
            place = i * pieces + t
            rims = (i * steps + t) * 2
            rims_rcv = ((half + i) * steps + t) * 2
            turned = pick(
                turn_first,
                jnp.concatenate([rims_ref[w, rims], centre[0, p, w, i, t, : 3 * ROWS]], axis=0),
            )
            straight = jnp.concatenate(
                [rims_ref[w, rims_rcv], centre[1, p, w, i, t, : 3 * ROWS]], axis=0
            ).astype(jnp.float32)
            products = [turned * scale * straight[:SPAN]]
            turn_extra = one_hot(
                SPAN + ROWS,
                b_extra * ROWS,
                lambda row, column: (row == 0) & (column == place),
            )
            turned = pick(
                turn_last,
                jnp.concatenate(
                    [centre[0, p, w, i, t, wide:], rims_ref[w, rims + 1]], axis=0
                ),
            ) + pick(turn_extra, extra)
            turned = turned * scale
            rcv_extra = pick(
                one_hot(
                    8,
                    b_extra * ROWS,
                    lambda row, column: (row == 0) & (column == place + steps),
                ),
                extra,
            )
            straight = jnp.concatenate(
                [
                    centre[1, p, w, i, t, wide:].astype(jnp.float32),
                    rims_ref[w, rims_rcv + 1].astype(jnp.float32),
                    rcv_extra,
                ],
                axis=0,
            )
            products.append(turned[ROWS:] * straight[:SPAN])
            products.append(turned[:SPAN] * straight[ROWS:])
            sums = [
                product if total is None else total + product
                for total, product in zip(sums, products)
            ]
        return sums

    def own_centre(w):
        @pl.loop(0, half)
        def _(i):
            sums, mids = centre_sums(w, 0, me_tm, i)
            for g in inner:
                acc[w, i, g] = sums[g]
            acc_mid[w, i] = mids

    def own_edge(w):
        @pl.loop(0, half)
        def _(i):
            for g, total in zip(outer, edge_sums(b_own, w, 0, me_tm, i)):
                acc[w, i, g] = total

    def far_centre(w):
        for copy in main_copies[w]:
            copy.wait_recv()

        @pl.loop(0, half)
        def _(i):
            sums, mids = centre_sums(w, 1, partner[w], i)
            mids = acc_mid[w, i] + mids
            if w < 2:
                first = OFFS * len(inner)
                for _, _, count, place in middle:
                    pc_send[w, i, first : first + count] = mids[place : place + count]
                    first += count
            else:
                acc_mid[w, i] = mids
            for k, g in enumerate(inner):
                total = acc[w, i, g] + sums[g]
                if w < 2:
                    pc_send[w, i, OFFS * k : OFFS * (k + 1)] = total[:OFFS]
                else:
                    acc[w, i, g] = total

    def far_edge(w):
        b_copies[w].wait_recv()

        @pl.loop(0, half)
        def _(i):
            sums = edge_sums(b_recv, w, 1, partner[w], i)
            totals = {g: acc[w, i, g] + sums[k] for k, g in enumerate(outer)}
            if w < 2:
                first = 0
                for g, offs, count in border:
                    pe_send[w, i, first : first + count] = totals[g][offs : offs + count]
                    first += count
            else:
                for g in outer:
                    acc[w, i, g] = totals[g]

    def partial_copy(w, send, recv, k):
        return pltpu.make_async_remote_copy(
            src_ref=send.at[w],
            dst_ref=recv.at[w],
            send_sem=p_send_sem.at[k, w],
            recv_sem=p_recv_sem.at[k, w],
            device_id=(me_tile, owner[w]),
            device_id_type=MESH,
        )

    def unpack(first, target, w):
        packed = None
        for i in range(half):
            tile = first + i
            for side in range(2):
                source = device_tab[side, base + tile]
                rank = ranks[side, tile]
                rim = a_recv[source, pl.ds(rank * pieces, pieces)]
                for f in range(2):
                    for t in range(steps):
                        target[w, ((f * half + i) * steps + t) * 2 + side] = rim[f * steps + t]
            extra = a_recv[source, capacity * pieces :].reshape(a_extra * ROWS, depth)
            choose = one_hot(
                b_extra * ROWS,
                a_extra * ROWS,
                lambda row, column: (row >= i * pieces)
                & (row < (i + 1) * pieces)
                & (column == rank * pieces + row - i * pieces),
            )
            chosen = pick(choose, extra)
            packed = chosen if packed is None else packed + chosen
        target[w, b_rims:] = packed.astype(jnp.bfloat16).reshape(b_extra, ROWS, depth)

    def place_rows(tile, g, offs, count, rows):
        for part in range(depth // 128):
            turned_out[tile, part, pl.ds(offs * GB + g, count, stride=GB), :] = rows[
                :, 128 * part : 128 * (part + 1)
            ]

    def finish_early(w):
        @pl.loop(0, half)
        def _(i):
            tile = offset[w] + i
            first = 0
            for g in inner:
                got = pc_recv[w - 2, i, first : first + OFFS]
                place_rows(tile, g, 0, OFFS, acc[w, i, g][:OFFS] + got)
                first += OFFS
            mids = acc_mid[w, i]
            for g, offs, count, place in middle:
                got = pc_recv[w - 2, i, first : first + count]
                place_rows(tile, g, offs, count, mids[place : place + count] + got)
                first += count

    def finish_late(w):
        @pl.loop(0, half)
        def _(i):
            tile = offset[w] + i
            first = 0
            for g, offs, count in border:
                got = pe_recv[w - 2, i, first : first + count]
                place_rows(tile, g, offs, count, acc[w, i, g][offs : offs + count] + got)
                first += count
            extent = extent_ref[me_tm * share + tile]
            cell = lax.broadcasted_iota(jnp.int32, (1, 128), 1)
            for part in range(depth // 128):
                mask = (cell + 128 * part < extent).astype(jnp.float32)
                out_ref[tile, :, 128 * part : 128 * (part + 1)] = (
                    turned_out[tile, part] * (1.0 / math.sqrt(steps * times)) * mask
                )

    for copy in own_copies:
        copy.wait()
    for w in range(4):
        own_centre(w)

    pc_copies = []
    for w in range(2):
        far_centre(w)
        copy = partial_copy(w, pc_send, pc_recv, 0)
        copy.start()
        pc_copies.append(copy)
    for w in (2, 3):
        far_centre(w)

    @pl.loop(1, devices)
    def _(j):
        a_copy(j).wait()

    b_copies = []
    for w in range(4):
        unpack(first_tile(owner_there, w), b_send, w)
        copy = pltpu.make_async_remote_copy(
            src_ref=b_send.at[w],
            dst_ref=b_recv.at[w],
            send_sem=b_send_sem.at[w],
            recv_sem=b_recv_sem.at[w],
            device_id=(me_tile, partner[w]),
            device_id_type=MESH,
        )
        copy.start()
        b_copies.append(copy)
    for w in range(2):
        unpack(first_tile(owner, w), b_own, w)
        own_edge(w)

    pe_copies = []
    for w in range(2):
        far_edge(w)
        copy = partial_copy(w, pe_send, pe_recv, 1)
        copy.start()
        pe_copies.append(copy)
    for w in (2, 3):
        unpack(first_tile(owner, w), b_own, w)
        own_edge(w)
        far_edge(w)
    for w in (2, 3):
        pc_copies[w - 2].wait_recv()
        finish_early(w)
    for w in (2, 3):
        pe_copies[w - 2].wait_recv()
        finish_late(w)

    for copies in main_copies:
        for copy in copies:
            copy.wait_send()
    for copy in b_copies + pc_copies + pe_copies:
        copy.wait_send()


def paired(src_snap, rcv_snap, q_rate, nbr_device, nbr_index, depth_extent):
    tiles, steps, width, depth = src_snap.shape
    devices = lax.axis_size("tile")
    times = lax.axis_size("tm")
    capacity = (2 * tiles + devices - 1) // devices + 1
    share = tiles // times
    half = share // 2
    pieces = 2 * steps
    a_blocks = capacity * pieces + -(-capacity * pieces // ROWS)
    b_blocks = 2 * half * steps * 2 + -(-half * pieces // ROWS)
    inner_rows = 328
    outer_rows = 72
    sizes = (tiles, steps, width, depth, devices, times, capacity, share)
    bf16, f32 = jnp.bfloat16, jnp.float32
    products = share * GB * OFFS * depth * steps * times
    image = pl.pallas_call(
        functools.partial(pair_kernel, sizes),
        out_shape=jax.ShapeDtypeStruct((share, OFFS * GB, depth), f32),
        in_specs=[pl.BlockSpec(memory_space=pltpu.HBM)] * 6,
        out_specs=pl.BlockSpec(memory_space=pltpu.VMEM),
        scratch_shapes=[
            pltpu.SMEM(nbr_device.shape[::-1], jnp.int32),
            pltpu.SMEM(nbr_index.shape[::-1], jnp.int32),
            pltpu.SMEM(depth_extent.shape, jnp.int32),
            pltpu.VMEM((1, depth), f32),
            pltpu.SMEM((2, tiles), jnp.int32),
            pltpu.VMEM((2, 3, tiles, steps, ROWS, depth), bf16),
            pltpu.VMEM((devices, a_blocks, ROWS, depth), bf16),
            pltpu.VMEM((devices, a_blocks, ROWS, depth), bf16),
            pltpu.VMEM((4, b_blocks, ROWS, depth), bf16),
            pltpu.VMEM((4, b_blocks, ROWS, depth), bf16),
            pltpu.VMEM((4, b_blocks, ROWS, depth), bf16),
            pltpu.VMEM((2, 2, 4, half, steps, width, depth), bf16),
            pltpu.VMEM((4, half, GB, SPAN, depth), f32),
            pltpu.VMEM((4, half, 88, depth), f32),
            pltpu.VMEM((share, depth // 128, OFFS * GB, 128), f32),
            pltpu.VMEM((2, half, inner_rows, depth), f32),
            pltpu.VMEM((2, half, inner_rows, depth), f32),
            pltpu.VMEM((2, half, outer_rows, depth), f32),
            pltpu.VMEM((2, half, outer_rows, depth), f32),
            pltpu.SemaphoreType.DMA((4,)),
            pltpu.SemaphoreType.DMA((6,)),
            pltpu.SemaphoreType.DMA((4, 2)),
            pltpu.SemaphoreType.DMA((4, 2)),
            pltpu.SemaphoreType.DMA((4, 2)),
            pltpu.SemaphoreType.DMA((devices,)),
            pltpu.SemaphoreType.DMA((devices,)),
            pltpu.SemaphoreType.DMA((4,)),
            pltpu.SemaphoreType.DMA((4,)),
            pltpu.SemaphoreType.DMA((2, 2)),
            pltpu.SemaphoreType.DMA((2, 2)),
        ],
        compiler_params=pltpu.CompilerParams(
            collective_id=1, has_side_effects=True, vmem_limit_bytes=60 * 1024 * 1024
        ),
        cost_estimate=pl.CostEstimate(
            flops=3 * products, bytes_accessed=4 * tiles * steps * width * depth, transcendentals=0
        ),
    )(nbr_device.T, nbr_index.T, depth_extent, q_rate.reshape(1, depth), src_snap, rcv_snap)
    return image.reshape(share, OFFS, GB, depth).transpose(0, 2, 1, 3)


def solution(mesh):
    placed = (P("tile", "tm", None, None), P("tile", "tm", None, None), P(), P(), P(), P("tile"))
    body = paired if mesh.shape["tm"] == 4 else local
    return jax.shard_map(
        body,
        mesh=mesh,
        in_specs=placed,
        out_specs=P(("tile", "tm"), None, None, None),
        check_vma=False,
    )
```

```python
import functools
import math

import jax
import jax.numpy as jnp
from jax import lax
from jax.experimental import pallas as pl
from jax.experimental.pallas import tpu as pltpu
from jax.sharding import PartitionSpec as P

GSTEP = 16
HMAX = 24
GB = 8
OFFS = 49
RIM_L = 16
RIM_R = 17
ROWS = 16
SPAN = 56
MESH = pl.DeviceIdType.MESH


def one_hot(rows, columns, rule):
    row = lax.broadcasted_iota(jnp.int32, (rows, columns), 0)
    column = lax.broadcasted_iota(jnp.int32, (rows, columns), 1)
    return rule(row, column).astype(jnp.float32).astype(jnp.bfloat16)


def pick(matrix, values):
    return jnp.dot(matrix, values, preferred_element_type=jnp.float32)


def kernel(
    sizes,
    send_tab,
    arrive_tab,
    extent_ref,
    rate_ref,
    src_ref,
    rcv_ref,
    out_ref,
    edge_cells,
    a_send,
    a_recv,
    b_send,
    b_recv,
    centre,
    acc,
    edge_sem,
    own_sem,
    main_send_sem,
    main_recv_sem,
    a_send_sem,
    a_recv_sem,
    b_send_sem,
    b_recv_sem,
):
    tiles, steps, width, depth, devices, times, capacity, share = sizes
    pieces = 2 * steps
    fields = (src_ref, rcv_ref)
    me_tile = lax.axis_index("tile")
    me_tm = lax.axis_index("tm")

    def rest(count, me, j):
        return lax.rem(me + j, count)

    edge_copies = []
    for f in range(2):
        for k, first in enumerate((width - ROWS, 0, ROWS)):
            copy = pltpu.make_async_copy(
                fields[f].at[:, :, pl.ds(first, ROWS), :],
                edge_cells.at[f, k],
                edge_sem.at[f * 3 + k],
            )
            copy.start()
            edge_copies.append(copy)
    own_copies = []
    for f in range(2):
        copy = pltpu.make_async_copy(
            fields[f].at[pl.ds(me_tm * share, share)], centre.at[f, me_tm], own_sem.at[f]
        )
        copy.start()
        own_copies.append(copy)

    barrier = pltpu.get_barrier_semaphore()
    for j in range(1, times):
        pl.semaphore_signal(
            barrier, inc=1, device_id=(me_tile, rest(times, me_tm, j)), device_id_type=MESH
        )
    for j in range(1, devices):
        pl.semaphore_signal(
            barrier, inc=1, device_id=(rest(devices, me_tile, j), me_tm), device_id_type=MESH
        )
    pl.semaphore_wait(barrier, times + devices - 2)

    main_copies = []
    for j in range(1, times):
        to = rest(times, me_tm, j)
        for f in range(2):
            copy = pltpu.make_async_remote_copy(
                src_ref=fields[f].at[pl.ds(to * share, share)],
                dst_ref=centre.at[f, me_tm],
                send_sem=main_send_sem.at[j, f],
                recv_sem=main_recv_sem.at[j, f],
                device_id=(me_tile, to),
                device_id_type=MESH,
            )
            copy.start()
            main_copies.append(copy)

    for copy in edge_copies:
        copy.wait()

    a_extra = a_send.shape[1] - capacity * pieces
    compress = one_hot(
        a_extra * ROWS, capacity * pieces * ROWS, lambda row, column: column == row * ROWS
    )

    def pack(to):
        extra = []
        for k in range(capacity):
            index = send_tab[0, to, k]
            side = send_tab[1, to, k]
            for f in range(2):
                first = k * pieces + f * steps
                a_send[to, first : first + steps] = edge_cells[f, side, index]
                extra.append(edge_cells[f, 2, index].reshape(steps * ROWS, depth))
        packed = pick(compress, jnp.concatenate(extra, axis=0))
        a_send[to, capacity * pieces :] = packed.astype(jnp.bfloat16).reshape(
            a_extra, ROWS, depth
        )

    def a_copy(j):
        to = rest(devices, me_tile, j)
        return pltpu.make_async_remote_copy(
            src_ref=a_send.at[to],
            dst_ref=a_recv.at[me_tile],
            send_sem=a_send_sem.at[j],
            recv_sem=a_recv_sem.at[j],
            device_id=(to, me_tm),
            device_id_type=MESH,
        )

    @pl.loop(1, devices)
    def _(j):
        pack(rest(devices, me_tile, j))
        a_copy(j).start()

    pack(me_tile)
    a_recv[me_tile] = a_send[me_tile]

    rate = rate_ref[...]

    def weight(part, t):
        step = (part * steps + t).astype(jnp.float32)
        return jnp.exp(rate * step / (steps * times))

    turn_centre = one_hot(
        width - 8, width, lambda row, column: column == width - ROWS - row
    )
    last = width // GSTEP * GSTEP - HMAX * 2

    def centre_pass(part, fresh):
        @pl.loop(0, share)
        def _(i):
            sums = [None] * GB
            for t in range(steps):
                turned = pick(turn_centre, centre[0, part, i, t]) * weight(part, t)
                straight = centre[1, part, i, t].astype(jnp.float32)
                for g in range(1, GB - 2):
                    back = last - GSTEP * g
                    ahead = GSTEP * (g - 1)
                    product = turned[back : back + SPAN] * straight[ahead : ahead + SPAN]
                    sums[g] = product if sums[g] is None else sums[g] + product
            for g in range(1, GB - 2):
                if fresh:
                    acc[i, g] = sums[g]
                else:
                    acc[i, g] += sums[g]

    for copy in own_copies:
        copy.wait()
    centre_pass(me_tm, True)

    @pl.loop(1, devices)
    def _(j):
        a_copy(j).wait()

    b_rims = 2 * share * steps * 2
    b_extra = b_send.shape[1] - b_rims

    def unpack(to):
        packed = None
        for i in range(share):
            tile = to * share + i
            for side in range(2):
                source = arrive_tab[0, 2 * tile + side]
                rank = arrive_tab[1, 2 * tile + side]
                rim = a_recv[source, pl.ds(rank * pieces, pieces)]
                for f in range(2):
                    for t in range(steps):
                        b_send[to, ((f * share + i) * steps + t) * 2 + side] = rim[f * steps + t]
            extra = a_recv[source, capacity * pieces :].reshape(a_extra * ROWS, depth)
            choose = one_hot(
                b_extra * ROWS,
                a_extra * ROWS,
                lambda row, column: (row >= i * pieces)
                & (row < (i + 1) * pieces)
                & (column == rank * pieces + row - i * pieces),
            )
            chosen = pick(choose, extra)
            packed = chosen if packed is None else packed + chosen
        b_send[to, b_rims:] = packed.astype(jnp.bfloat16).reshape(b_extra, ROWS, depth)

    def b_copy(j):
        to = rest(times, me_tm, j)
        return pltpu.make_async_remote_copy(
            src_ref=b_send.at[to],
            dst_ref=b_recv.at[me_tm],
            send_sem=b_send_sem.at[j],
            recv_sem=b_recv_sem.at[j],
            device_id=(me_tile, to),
            device_id_type=MESH,
        )

    @pl.loop(1, times)
    def _(j):
        unpack(rest(times, me_tm, j))
        b_copy(j).start()

    unpack(me_tm)
    b_recv[me_tm] = b_send[me_tm]

    def finish(gathers):
        @pl.loop(0, share)
        def _(i):
            extent = extent_ref[me_tm * share + i]
            cell = lax.broadcasted_iota(jnp.int32, (1, depth), 1)
            mask = (cell < extent).astype(jnp.float32)
            for g in gathers:
                out_ref[i, g] = (
                    acc[i, g][:OFFS] * (1.0 / math.sqrt(steps * times)) * mask
                )

    turn_first = one_hot(SPAN, 4 * ROWS, lambda row, column: column == OFFS - 1 - row)
    turn_last = one_hot(SPAN + ROWS, 4 * ROWS, lambda row, column: column == 4 * ROWS - row)
    wide = width - 3 * ROWS

    def edge_pass(part, fresh):
        @pl.loop(0, share)
        def _(i):
            extra = b_recv[part, b_rims:].reshape(b_extra * ROWS, depth)
            sums = [None] * 3
            for t in range(steps):
                scale = weight(part, t)
                place = i * pieces + t
                rims = (i * steps + t) * 2
                rims_rcv = ((share + i) * steps + t) * 2
                src_left = b_recv[part, rims]
                src_right = b_recv[part, rims + 1]
                rcv_left = b_recv[part, rims_rcv]
                rcv_right = b_recv[part, rims_rcv + 1]
                turned = pick(
                    turn_first,
                    jnp.concatenate([src_left, centre[0, part, i, t, : 3 * ROWS]], axis=0),
                )
                straight = jnp.concatenate(
                    [rcv_left, centre[1, part, i, t, : 3 * ROWS]], axis=0
                ).astype(jnp.float32)
                products = [turned * scale * straight[:SPAN]]
                turn_extra = one_hot(
                    SPAN + ROWS,
                    b_extra * ROWS,
                    lambda row, column: (row == 0) & (column == place),
                )
                turned = pick(
                    turn_last,
                    jnp.concatenate([centre[0, part, i, t, wide:], src_right], axis=0),
                ) + pick(turn_extra, extra)
                turned = turned * scale
                rcv_extra = pick(
                    one_hot(
                        8,
                        b_extra * ROWS,
                        lambda row, column: (row == 0) & (column == place + steps),
                    ),
                    extra,
                )
                straight = jnp.concatenate(
                    [
                        centre[1, part, i, t, wide:].astype(jnp.float32),
                        rcv_right.astype(jnp.float32),
                        rcv_extra,
                    ],
                    axis=0,
                )
                products.append(turned[ROWS:] * straight[:SPAN])
                products.append(turned[:SPAN] * straight[ROWS:])
                sums = [
                    product if total is None else total + product
                    for total, product in zip(sums, products)
                ]
            for g, total in zip((0, GB - 2, GB - 1), sums):
                if fresh:
                    acc[i, g] = total
                else:
                    acc[i, g] += total

    edge_pass(me_tm, True)
    for j in range(1, times):
        for f in range(2):
            main_copies[2 * (j - 1) + f].wait_recv()
        centre_pass(rest(times, me_tm, times - j), False)
    finish(range(1, GB - 2))
    for j in range(1, times):
        b_copy(j).wait_recv()
        edge_pass(rest(times, me_tm, times - j), False)
    finish((0, GB - 2, GB - 1))

    for copy in main_copies:
        copy.wait_send()
    for j in range(1, times):
        b_copy(j).wait_send()


def routes(nbr_device, nbr_index, devices, capacity, tiles):
    own = lax.axis_index("tile")
    count = 2 * tiles
    device = nbr_device.reshape(devices, count)
    index = nbr_index.reshape(devices, count)
    ids = jnp.arange(count, dtype=jnp.int32)
    earlier = ids[None, :] < ids[:, None]
    same = (device[:, :, None] == device[:, None, :]) & earlier[None]
    rank = jnp.sum(same.astype(jnp.int32), axis=2)
    slot = jnp.arange(capacity, dtype=jnp.int32)
    hit = ((device == own)[:, None, :] & (rank[:, None, :] == slot[None, :, None])).astype(jnp.int32)
    wanted = jnp.stack([index, jnp.broadcast_to((ids % 2)[None, :], index.shape)])
    send_tab = jnp.sum(hit[None] * wanted[:, :, None, :], axis=3)
    arrive = jnp.stack([device, rank])
    arrive_tab = lax.dynamic_slice_in_dim(arrive, own, 1, 1)[:, 0]
    return send_tab, arrive_tab


def local(src_snap, rcv_snap, q_rate, nbr_device, nbr_index, depth_extent):
    tiles, steps, width, depth = src_snap.shape
    devices = lax.axis_size("tile")
    times = lax.axis_size("tm")
    capacity = (2 * tiles + devices - 1) // devices + 1
    share = tiles // times
    send_tab, arrive_tab = routes(nbr_device, nbr_index, devices, capacity, tiles)
    pieces = 2 * steps
    a_blocks = capacity * pieces + -(-capacity * pieces // ROWS)
    b_blocks = 2 * share * steps * 2 + -(-share * pieces // ROWS)
    sizes = (tiles, steps, width, depth, devices, times, capacity, share)
    half = jnp.bfloat16
    products = share * GB * OFFS * depth * steps * times
    return pl.pallas_call(
        functools.partial(kernel, sizes),
        out_shape=jax.ShapeDtypeStruct((share, GB, OFFS, depth), jnp.float32),
        in_specs=[pl.BlockSpec(memory_space=pltpu.SMEM)] * 3
        + [pl.BlockSpec(memory_space=pltpu.VMEM)]
        + [pl.BlockSpec(memory_space=pl.ANY)] * 2,
        out_specs=pl.BlockSpec(memory_space=pltpu.VMEM),
        scratch_shapes=[
            pltpu.VMEM((2, 3, tiles, steps, ROWS, depth), half),
            pltpu.VMEM((devices, a_blocks, ROWS, depth), half),
            pltpu.VMEM((devices, a_blocks, ROWS, depth), half),
            pltpu.VMEM((times, b_blocks, ROWS, depth), half),
            pltpu.VMEM((times, b_blocks, ROWS, depth), half),
            pltpu.VMEM((2, times, share, steps, width, depth), half),
            pltpu.VMEM((share, GB, SPAN, depth), jnp.float32),
            pltpu.SemaphoreType.DMA((6,)),
            pltpu.SemaphoreType.DMA((2,)),
            pltpu.SemaphoreType.DMA((times, 2)),
            pltpu.SemaphoreType.DMA((times, 2)),
            pltpu.SemaphoreType.DMA((devices,)),
            pltpu.SemaphoreType.DMA((devices,)),
            pltpu.SemaphoreType.DMA((times,)),
            pltpu.SemaphoreType.DMA((times,)),
        ],
        compiler_params=pltpu.CompilerParams(
            collective_id=0, has_side_effects=True, vmem_limit_bytes=40 * 1024 * 1024
        ),
        cost_estimate=pl.CostEstimate(
            flops=3 * products, bytes_accessed=4 * tiles * steps * width * depth, transcendentals=0
        ),
    )(send_tab, arrive_tab, depth_extent, q_rate.reshape(1, depth), src_snap, rcv_snap)


def pair_kernel(
    sizes,
    device_in,
    index_in,
    extent_in,
    rate_in,
    src_ref,
    rcv_ref,
    out_ref,
    device_tab,
    index_tab,
    extent_ref,
    rate_ref,
    ranks,
    edge_cells,
    a_send,
    a_recv,
    b_own,
    b_send,
    b_recv,
    centre,
    acc,
    acc_mid,
    acc_edge,
    kept,
    turned_out,
    pc_send,
    pc_recv,
    pe_send,
    pe_recv,
    small_sem,
    edge_sem,
    own_sem,
    main_send_sem,
    main_recv_sem,
    a_send_sem,
    a_recv_sem,
    b_send_sem,
    b_recv_sem,
    p_send_sem,
    p_recv_sem,
):
    tiles, steps, width, depth, devices, times, capacity, share = sizes
    half = share // 2
    pieces = 2 * steps
    fields = (src_ref, rcv_ref)
    me_tile = lax.axis_index("tile")
    me_tm = lax.axis_index("tm")
    low = lax.rem(me_tm, 2)
    high = lax.div(me_tm, 2)
    by_x = high * 2 + 1 - low
    by_y = (1 - high) * 2 + low
    across = (1 - high) * 2 + 1 - low

    owner = (by_y, by_x, me_tm, me_tm)
    partner = (by_x, by_y, by_x, by_y)
    owner_there = (across, across, by_x, by_y)
    offset = (0, half, 0, half)

    def first_tile(owners, w):
        return owners[w] * share + offset[w]

    barrier = pltpu.get_barrier_semaphore()
    for to in (by_x, by_y):
        pl.semaphore_signal(barrier, inc=1, device_id=(me_tile, to), device_id_type=MESH)
    for j in range(1, devices):
        pl.semaphore_signal(
            barrier, inc=1, device_id=(lax.rem(me_tile + j, devices), me_tm), device_id_type=MESH
        )
    small_copies = []
    smalls = ((device_in, device_tab), (index_in, index_tab), (extent_in, extent_ref), (rate_in, rate_ref))
    for k, (source, target) in enumerate(smalls):
        copy = pltpu.make_async_copy(source, target, small_sem.at[k])
        copy.start()
        small_copies.append(copy)
    edge_copies = []
    for f in range(2):
        for k, first in enumerate((width - ROWS, 0, ROWS)):
            copy = pltpu.make_async_copy(
                fields[f].at[:, :, pl.ds(first, ROWS), :],
                edge_cells.at[f, k],
                edge_sem.at[f * 3 + k],
            )
            copy.start()
            edge_copies.append(copy)

    pl.semaphore_wait(barrier, devices + 1)

    main_copies = []

    def start_main(w):
        copies = []
        for f in range(2):
            copy = pltpu.make_async_remote_copy(
                src_ref=fields[f].at[pl.ds(first_tile(owner_there, w), half)],
                dst_ref=centre.at[f, 1, w],
                send_sem=main_send_sem.at[w, f],
                recv_sem=main_recv_sem.at[w, f],
                device_id=(me_tile, partner[w]),
                device_id_type=MESH,
            )
            copy.start()
            copies.append(copy)
        main_copies.append(copies)

    for w in range(2):
        start_main(w)
    own_copies = []
    for w in range(4):
        for f in range(2):
            copy = pltpu.make_async_copy(
                fields[f].at[pl.ds(first_tile(owner, w), half)],
                centre.at[f, 0, w],
                own_sem.at[w, f],
            )
            copy.start()
            own_copies.append(copy)

    for copy in small_copies + edge_copies:
        copy.wait()

    a_extra = a_send.shape[1] - capacity * pieces
    compress = one_hot(
        a_extra * ROWS, capacity * pieces * ROWS, lambda row, column: column == row * ROWS
    )

    def pack(to):
        def scan(row, carry):
            count, codes = carry
            for side in range(2):
                hit = device_tab[side, to * tiles + row] == me_tile
                code = index_tab[side, to * tiles + row] * 2 + side
                codes = tuple(
                    jnp.where(hit & (count == k), code, codes[k]) for k in range(capacity)
                )
                count = count + hit.astype(jnp.int32)
            return count, codes

        zero = jnp.int32(0)
        _, codes = lax.fori_loop(0, tiles, scan, (zero, (zero,) * capacity))
        extra = []
        for k in range(capacity):
            index = lax.div(codes[k], 2)
            side = lax.rem(codes[k], 2)
            for f in range(2):
                first = k * pieces + f * steps
                a_send[to, first : first + steps] = edge_cells[f, side, index]
                extra.append(edge_cells[f, 2, index].reshape(steps * ROWS, depth))
        packed = pick(compress, jnp.concatenate(extra, axis=0))
        a_send[to, capacity * pieces :] = packed.astype(jnp.bfloat16).reshape(
            a_extra, ROWS, depth
        )

    def other(j):
        total, unit = jnp.int32(0), 1
        while unit < devices:
            mine = lax.rem(lax.div(me_tile, unit), 2)
            flip = lax.rem(lax.div(j, unit), 2)
            total = total + (mine + flip - 2 * mine * flip) * unit
            unit *= 2
        return total

    def a_copy(j):
        to = other(j)
        return pltpu.make_async_remote_copy(
            src_ref=a_send.at[to],
            dst_ref=a_recv.at[me_tile],
            send_sem=a_send_sem.at[j],
            recv_sem=a_recv_sem.at[j],
            device_id=(to, me_tm),
            device_id_type=MESH,
        )

    @pl.loop(1, devices)
    def _(back):
        j = devices - back
        pack(other(j))
        a_copy(j).start()

    for w in (2, 3):
        start_main(w)
    pack(me_tile)
    a_recv[me_tile] = a_send[me_tile]

    base = me_tile * tiles

    @pl.loop(0, tiles)
    def _(row):
        mine = [device_tab[side, base + row] for side in range(2)]

        def count(other, sums):
            theirs = [device_tab[side, base + other] for side in range(2)]
            return tuple(
                sums[side]
                + (theirs[0] == mine[side]).astype(jnp.int32)
                + (theirs[1] == mine[side]).astype(jnp.int32)
                for side in range(2)
            )

        found = lax.fori_loop(0, row, count, (jnp.int32(0), jnp.int32(0)))
        for side in range(2):
            ranks[side, row] = jnp.minimum(found[side], capacity - 1)

    rate = rate_ref[...]

    def weight(part, t):
        step = (part * steps + t).astype(jnp.float32)
        return jnp.exp(rate * step / (steps * times))

    weights = [[weight(part, t) for t in range(steps)] for part in (me_tm, by_x, by_y)]

    def weights_of(p, w):
        return weights[0] if p == 0 else weights[1 + w % 2]

    inner = range(1, GB - 2)
    middle = ((0, 16, 17, 0), (GB - 2, 1, 47, 25), (GB - 1, 17, 15, 73))
    border = (
        (0, 0, 16),
        (0, 33, 16),
        (GB - 1, 1, 16),
        (GB - 1, 32, 16),
        (GB - 1, 0, 1),
        (GB - 1, 48, 1),
        (GB - 2, 0, 1),
        (GB - 2, 48, 1),
    )
    turn_centre = one_hot(width + 8, width, lambda row, column: column == width - row)
    last = width // GSTEP * GSTEP + ROWS - HMAX * 2

    def centre_sums(w, p, i):
        sums = [None] * GB
        mids = [None] * 3
        for t in range(steps):
            turned = pick(turn_centre, centre[0, p, w, i, t]) * weights_of(p, w)[t]
            kept[p, w, i, t, : 3 * ROWS] = turned[ROWS : 4 * ROWS]
            kept[p, w, i, t, 3 * ROWS :] = turned[6 * ROWS : 7 * ROWS]
            straight = centre[1, p, w, i, t].astype(jnp.float32)
            products = (
                turned[width - ROWS :] * straight[:24],
                turned[: 3 * ROWS] * straight[width - 3 * ROWS :],
                turned[:ROWS] * straight[width - ROWS :],
            )
            mids = [
                product if total is None else total + product
                for total, product in zip(mids, products)
            ]
            for g in inner:
                back = last - GSTEP * g
                ahead = GSTEP * (g - 1)
                product = turned[back : back + SPAN] * straight[ahead : ahead + SPAN]
                sums[g] = product if sums[g] is None else sums[g] + product
        return sums, jnp.concatenate(mids, axis=0)

    b_rims = 2 * half * steps * 2
    b_extra = b_send.shape[1] - b_rims
    rim_rows = b_rims // 2 * ROWS
    turn_rims = one_hot(
        rim_rows,
        rim_rows,
        lambda row, column: column == row // ROWS * (2 * ROWS) + ROWS - 1 - row,
    )

    def edge_sums(rims_ref, w, p):
        extra = rims_ref[w, b_rims:].reshape(b_extra * ROWS, depth).astype(jnp.float32)
        turned_rims = pick(turn_rims, rims_ref[w, : b_rims // 2].reshape(rim_rows, depth))
        found = []
        for i in range(half):
            total = None
            for t in range(steps):
                scale = weights_of(p, w)[t]
                place = i * pieces + t
                block = (i * steps + t) * 2
                left = turned_rims[block * ROWS : (block + 1) * ROWS] * scale
                right = turned_rims[(block + 1) * ROWS : (block + 2) * ROWS] * scale
                rims_rcv = b_rims // 2 + block
                rcv_left = rims_ref[w, rims_rcv].astype(jnp.float32)
                rcv_right = rims_ref[w, rims_rcv + 1].astype(jnp.float32)
                turned = kept[p, w, i, t]
                near = centre[1, p, w, i, t, ROWS : 3 * ROWS].astype(jnp.float32)
                far = centre[1, p, w, i, t, width - 3 * ROWS :].astype(jnp.float32)
                src_extra = extra[place : place + 1] * scale
                rcv_extra = extra[place + steps : place + steps + 1]
                product = jnp.concatenate(
                    [
                        turned[3 * ROWS :] * rcv_left,
                        left * near[1 : ROWS + 1],
                        right * far[ROWS + 1 : 2 * ROWS + 1],
                        turned[:ROWS] * rcv_right,
                        src_extra * far[ROWS : ROWS + 1],
                        turned[ROWS : ROWS + 1] * rcv_extra,
                        right[ROWS - 1 :] * far[:1],
                        turned[2 * ROWS : 2 * ROWS + 1] * rcv_right[:1],
                        jnp.zeros((4, depth), jnp.float32),
                    ],
                    axis=0,
                )
                total = product if total is None else total + product
            found.append(total)
        return found

    def own_centre(w):
        @pl.loop(0, half)
        def _(i):
            sums, mids = centre_sums(w, 0, i)
            for g in inner:
                acc[w, i, g] = sums[g]
            acc_mid[w, i] = mids

    def own_edge(w):
        for i, total in enumerate(edge_sums(b_own, w, 0)):
            acc_edge[w, i] = total

    def far_centre(w):
        for copy in main_copies[w]:
            copy.wait_recv()

        @pl.loop(0, half)
        def _(i):
            sums, mids = centre_sums(w, 1, i)
            mids = acc_mid[w, i] + mids
            if w < 2:
                first = OFFS * len(inner)
                for _, _, count, place in middle:
                    pc_send[w, i, first : first + count] = mids[place : place + count]
                    first += count
            else:
                acc_mid[w, i] = mids
            for k, g in enumerate(inner):
                total = acc[w, i, g] + sums[g]
                if w < 2:
                    pc_send[w, i, OFFS * k : OFFS * (k + 1)] = total[:OFFS]
                else:
                    acc[w, i, g] = total

    def far_edge(w):
        b_copies[w].wait_recv()
        target = pe_send if w < 2 else acc_edge
        for i, total in enumerate(edge_sums(b_recv, w, 1)):
            target[w, i] = acc_edge[w, i] + total

    def partial_copy(w, send, recv, k):
        return pltpu.make_async_remote_copy(
            src_ref=send.at[w],
            dst_ref=recv.at[w],
            send_sem=p_send_sem.at[k, w],
            recv_sem=p_recv_sem.at[k, w],
            device_id=(me_tile, owner[w]),
            device_id_type=MESH,
        )

    def unpack(first, target, w):
        row = lax.broadcasted_iota(jnp.int32, (b_extra * ROWS, half * a_extra * ROWS), 0)
        column = lax.broadcasted_iota(jnp.int32, (b_extra * ROWS, half * a_extra * ROWS), 1)
        chosen = jnp.full(row.shape, False)
        extras = []
        for i in range(half):
            tile = first + i
            for side in range(2):
                source = device_tab[side, base + tile]
                rank = ranks[side, tile]
                rim = a_recv[source, pl.ds(rank * pieces, pieces)]
                for f in range(2):
                    for t in range(steps):
                        target[w, ((f * half + i) * steps + t) * 2 + side] = rim[f * steps + t]
            extras.append(
                a_recv[source, capacity * pieces :].reshape(a_extra * ROWS, depth)
            )
            chosen = chosen | (
                (row >= i * pieces)
                & (row < (i + 1) * pieces)
                & (column == i * a_extra * ROWS + rank * pieces + row - i * pieces)
            )
        packed = pick(
            chosen.astype(jnp.float32).astype(jnp.bfloat16), jnp.concatenate(extras, axis=0)
        )
        target[w, b_rims:] = packed.astype(jnp.bfloat16).reshape(b_extra, ROWS, depth)

    def place_rows(tile, g, offs, count, rows):
        for part in range(depth // 128):
            turned_out[tile, part, pl.ds(offs * GB + g, count, stride=GB), :] = rows[
                :, 128 * part : 128 * (part + 1)
            ]

    def finish_early(w):
        @pl.loop(0, half)
        def _(i):
            tile = offset[w] + i
            first = 0
            for g in inner:
                got = pc_recv[w - 2, i, first : first + OFFS]
                place_rows(tile, g, 0, OFFS, acc[w, i, g][:OFFS] + got)
                first += OFFS
            mids = acc_mid[w, i]
            for g, offs, count, place in middle:
                got = pc_recv[w - 2, i, first : first + count]
                place_rows(tile, g, offs, count, mids[place : place + count] + got)
                first += count

    def finish_late(w):
        @pl.loop(0, half)
        def _(i):
            tile = offset[w] + i
            first = 0
            for g, offs, count in border:
                got = pe_recv[w - 2, i, first : first + count]
                place_rows(tile, g, offs, count, acc_edge[w, i, first : first + count] + got)
                first += count
            extent = extent_ref[me_tm * share + tile]
            cell = lax.broadcasted_iota(jnp.int32, (1, 128), 1)
            for part in range(depth // 128):
                mask = (cell + 128 * part < extent).astype(jnp.float32)
                out_ref[tile, :, 128 * part : 128 * (part + 1)] = (
                    turned_out[tile, part] * (1.0 / math.sqrt(steps * times)) * mask
                )

    for copy in own_copies:
        copy.wait()
    for w in range(4):
        own_centre(w)

    pc_copies = []
    for w in range(2):
        far_centre(w)
        copy = partial_copy(w, pc_send, pc_recv, 0)
        copy.start()
        pc_copies.append(copy)
    for w in (2, 3):
        far_centre(w)

    @pl.loop(1, devices)
    def _(j):
        a_copy(j).wait()

    b_copies = []
    for w in range(4):
        unpack(first_tile(owner_there, w), b_send, w)
        copy = pltpu.make_async_remote_copy(
            src_ref=b_send.at[w],
            dst_ref=b_recv.at[w],
            send_sem=b_send_sem.at[w],
            recv_sem=b_recv_sem.at[w],
            device_id=(me_tile, partner[w]),
            device_id_type=MESH,
        )
        copy.start()
        b_copies.append(copy)
    for w in range(2):
        unpack(first_tile(owner, w), b_own, w)
        own_edge(w)

    pe_copies = []
    for w in range(2):
        far_edge(w)
        copy = partial_copy(w, pe_send, pe_recv, 1)
        copy.start()
        pe_copies.append(copy)
    for w in (2, 3):
        unpack(first_tile(owner, w), b_own, w)
        own_edge(w)
        far_edge(w)
    for w in (2, 3):
        pc_copies[w - 2].wait_recv()
        finish_early(w)
    for w in (2, 3):
        pe_copies[w - 2].wait_recv()
        finish_late(w)

    for copies in main_copies:
        for copy in copies:
            copy.wait_send()
    for copy in b_copies + pc_copies + pe_copies:
        copy.wait_send()


def paired(src_snap, rcv_snap, q_rate, nbr_device, nbr_index, depth_extent):
    tiles, steps, width, depth = src_snap.shape
    devices = lax.axis_size("tile")
    times = lax.axis_size("tm")
    capacity = (2 * tiles + devices - 1) // devices + 1
    share = tiles // times
    half = share // 2
    pieces = 2 * steps
    a_blocks = capacity * pieces + -(-capacity * pieces // ROWS)
    b_blocks = 2 * half * steps * 2 + -(-half * pieces // ROWS)
    inner_rows = 328
    outer_rows = 72
    sizes = (tiles, steps, width, depth, devices, times, capacity, share)
    bf16, f32 = jnp.bfloat16, jnp.float32
    products = share * GB * OFFS * depth * steps * times
    image = pl.pallas_call(
        functools.partial(pair_kernel, sizes),
        out_shape=jax.ShapeDtypeStruct((share, OFFS * GB, depth), f32),
        in_specs=[pl.BlockSpec(memory_space=pltpu.HBM)] * 6,
        out_specs=pl.BlockSpec(memory_space=pltpu.VMEM),
        scratch_shapes=[
            pltpu.SMEM(nbr_device.shape[::-1], jnp.int32),
            pltpu.SMEM(nbr_index.shape[::-1], jnp.int32),
            pltpu.SMEM(depth_extent.shape, jnp.int32),
            pltpu.VMEM((1, depth), f32),
            pltpu.SMEM((2, tiles), jnp.int32),
            pltpu.VMEM((2, 3, tiles, steps, ROWS, depth), bf16),
            pltpu.VMEM((devices, a_blocks, ROWS, depth), bf16),
            pltpu.VMEM((devices, a_blocks, ROWS, depth), bf16),
            pltpu.VMEM((4, b_blocks, ROWS, depth), bf16),
            pltpu.VMEM((4, b_blocks, ROWS, depth), bf16),
            pltpu.VMEM((4, b_blocks, ROWS, depth), bf16),
            pltpu.VMEM((2, 2, 4, half, steps, width, depth), bf16),
            pltpu.VMEM((4, half, GB, SPAN, depth), f32),
            pltpu.VMEM((4, half, 88, depth), f32),
            pltpu.VMEM((4, half, outer_rows, depth), f32),
            pltpu.VMEM((2, 4, half, steps, 4 * ROWS, depth), f32),
            pltpu.VMEM((share, depth // 128, OFFS * GB, 128), f32),
            pltpu.VMEM((2, half, inner_rows, depth), f32),
            pltpu.VMEM((2, half, inner_rows, depth), f32),
            pltpu.VMEM((2, half, outer_rows, depth), f32),
            pltpu.VMEM((2, half, outer_rows, depth), f32),
            pltpu.SemaphoreType.DMA((4,)),
            pltpu.SemaphoreType.DMA((6,)),
            pltpu.SemaphoreType.DMA((4, 2)),
            pltpu.SemaphoreType.DMA((4, 2)),
            pltpu.SemaphoreType.DMA((4, 2)),
            pltpu.SemaphoreType.DMA((devices,)),
            pltpu.SemaphoreType.DMA((devices,)),
            pltpu.SemaphoreType.DMA((4,)),
            pltpu.SemaphoreType.DMA((4,)),
            pltpu.SemaphoreType.DMA((2, 2)),
            pltpu.SemaphoreType.DMA((2, 2)),
        ],
        compiler_params=pltpu.CompilerParams(
            collective_id=1, has_side_effects=True, vmem_limit_bytes=60 * 1024 * 1024
        ),
        cost_estimate=pl.CostEstimate(
            flops=3 * products, bytes_accessed=4 * tiles * steps * width * depth, transcendentals=0
        ),
    )(nbr_device.T, nbr_index.T, depth_extent, q_rate.reshape(1, depth), src_snap, rcv_snap)
    return image.reshape(share, OFFS, GB, depth).transpose(0, 2, 1, 3)


def solution(mesh):
    placed = (P("tile", "tm", None, None), P("tile", "tm", None, None), P(), P(), P(), P("tile"))
    body = paired if mesh.shape["tm"] == 4 else local
    return jax.shard_map(
        body,
        mesh=mesh,
        in_specs=placed,
        out_specs=P(("tile", "tm"), None, None, None),
        check_vma=False,
    )
```

```python
import functools
import math

import jax
import jax.numpy as jnp
from jax import lax
from jax.experimental import pallas as pl
from jax.experimental.pallas import tpu as pltpu
from jax.sharding import PartitionSpec as P

GSTEP = 16
HMAX = 24
GB = 8
OFFS = 49
RIM_L = 16
RIM_R = 17
ROWS = 16
SPAN = 56
MESH = pl.DeviceIdType.MESH


def one_hot(rows, columns, rule):
    row = lax.broadcasted_iota(jnp.int32, (rows, columns), 0)
    column = lax.broadcasted_iota(jnp.int32, (rows, columns), 1)
    return rule(row, column).astype(jnp.float32).astype(jnp.bfloat16)


def pick(matrix, values):
    return jnp.dot(matrix, values, preferred_element_type=jnp.float32)


def kernel(
    sizes,
    send_tab,
    arrive_tab,
    extent_ref,
    rate_ref,
    src_ref,
    rcv_ref,
    out_ref,
    edge_cells,
    a_send,
    a_recv,
    b_send,
    b_recv,
    centre,
    acc,
    edge_sem,
    own_sem,
    main_send_sem,
    main_recv_sem,
    a_send_sem,
    a_recv_sem,
    b_send_sem,
    b_recv_sem,
):
    tiles, steps, width, depth, devices, times, capacity, share = sizes
    pieces = 2 * steps
    fields = (src_ref, rcv_ref)
    me_tile = lax.axis_index("tile")
    me_tm = lax.axis_index("tm")

    def rest(count, me, j):
        return lax.rem(me + j, count)

    edge_copies = []
    for f in range(2):
        for k, first in enumerate((width - ROWS, 0, ROWS)):
            copy = pltpu.make_async_copy(
                fields[f].at[:, :, pl.ds(first, ROWS), :],
                edge_cells.at[f, k],
                edge_sem.at[f * 3 + k],
            )
            copy.start()
            edge_copies.append(copy)
    own_copies = []
    for f in range(2):
        copy = pltpu.make_async_copy(
            fields[f].at[pl.ds(me_tm * share, share)], centre.at[f, me_tm], own_sem.at[f]
        )
        copy.start()
        own_copies.append(copy)

    barrier = pltpu.get_barrier_semaphore()
    for j in range(1, times):
        pl.semaphore_signal(
            barrier, inc=1, device_id=(me_tile, rest(times, me_tm, j)), device_id_type=MESH
        )
    for j in range(1, devices):
        pl.semaphore_signal(
            barrier, inc=1, device_id=(rest(devices, me_tile, j), me_tm), device_id_type=MESH
        )
    pl.semaphore_wait(barrier, times + devices - 2)

    main_copies = []
    for j in range(1, times):
        to = rest(times, me_tm, j)
        for f in range(2):
            copy = pltpu.make_async_remote_copy(
                src_ref=fields[f].at[pl.ds(to * share, share)],
                dst_ref=centre.at[f, me_tm],
                send_sem=main_send_sem.at[j, f],
                recv_sem=main_recv_sem.at[j, f],
                device_id=(me_tile, to),
                device_id_type=MESH,
            )
            copy.start()
            main_copies.append(copy)

    for copy in edge_copies:
        copy.wait()

    a_extra = a_send.shape[1] - capacity * pieces
    compress = one_hot(
        a_extra * ROWS, capacity * pieces * ROWS, lambda row, column: column == row * ROWS
    )

    def pack(to):
        extra = []
        for k in range(capacity):
            index = send_tab[0, to, k]
            side = send_tab[1, to, k]
            for f in range(2):
                first = k * pieces + f * steps
                a_send[to, first : first + steps] = edge_cells[f, side, index]
                extra.append(edge_cells[f, 2, index].reshape(steps * ROWS, depth))
        packed = pick(compress, jnp.concatenate(extra, axis=0))
        a_send[to, capacity * pieces :] = packed.astype(jnp.bfloat16).reshape(
            a_extra, ROWS, depth
        )

    def a_copy(j):
        to = rest(devices, me_tile, j)
        return pltpu.make_async_remote_copy(
            src_ref=a_send.at[to],
            dst_ref=a_recv.at[me_tile],
            send_sem=a_send_sem.at[j],
            recv_sem=a_recv_sem.at[j],
            device_id=(to, me_tm),
            device_id_type=MESH,
        )

    @pl.loop(1, devices)
    def _(j):
        pack(rest(devices, me_tile, j))
        a_copy(j).start()

    pack(me_tile)
    a_recv[me_tile] = a_send[me_tile]

    rate = rate_ref[...]

    def weight(part, t):
        step = (part * steps + t).astype(jnp.float32)
        return jnp.exp(rate * step / (steps * times))

    turn_centre = one_hot(
        width - 8, width, lambda row, column: column == width - ROWS - row
    )
    last = width // GSTEP * GSTEP - HMAX * 2

    def centre_pass(part, fresh):
        @pl.loop(0, share)
        def _(i):
            sums = [None] * GB
            for t in range(steps):
                turned = pick(turn_centre, centre[0, part, i, t]) * weight(part, t)
                straight = centre[1, part, i, t].astype(jnp.float32)
                for g in range(1, GB - 2):
                    back = last - GSTEP * g
                    ahead = GSTEP * (g - 1)
                    product = turned[back : back + SPAN] * straight[ahead : ahead + SPAN]
                    sums[g] = product if sums[g] is None else sums[g] + product
            for g in range(1, GB - 2):
                if fresh:
                    acc[i, g] = sums[g]
                else:
                    acc[i, g] += sums[g]

    for copy in own_copies:
        copy.wait()
    centre_pass(me_tm, True)

    @pl.loop(1, devices)
    def _(j):
        a_copy(j).wait()

    b_rims = 2 * share * steps * 2
    b_extra = b_send.shape[1] - b_rims

    def unpack(to):
        packed = None
        for i in range(share):
            tile = to * share + i
            for side in range(2):
                source = arrive_tab[0, 2 * tile + side]
                rank = arrive_tab[1, 2 * tile + side]
                rim = a_recv[source, pl.ds(rank * pieces, pieces)]
                for f in range(2):
                    for t in range(steps):
                        b_send[to, ((f * share + i) * steps + t) * 2 + side] = rim[f * steps + t]
            extra = a_recv[source, capacity * pieces :].reshape(a_extra * ROWS, depth)
            choose = one_hot(
                b_extra * ROWS,
                a_extra * ROWS,
                lambda row, column: (row >= i * pieces)
                & (row < (i + 1) * pieces)
                & (column == rank * pieces + row - i * pieces),
            )
            chosen = pick(choose, extra)
            packed = chosen if packed is None else packed + chosen
        b_send[to, b_rims:] = packed.astype(jnp.bfloat16).reshape(b_extra, ROWS, depth)

    def b_copy(j):
        to = rest(times, me_tm, j)
        return pltpu.make_async_remote_copy(
            src_ref=b_send.at[to],
            dst_ref=b_recv.at[me_tm],
            send_sem=b_send_sem.at[j],
            recv_sem=b_recv_sem.at[j],
            device_id=(me_tile, to),
            device_id_type=MESH,
        )

    @pl.loop(1, times)
    def _(j):
        unpack(rest(times, me_tm, j))
        b_copy(j).start()

    unpack(me_tm)
    b_recv[me_tm] = b_send[me_tm]

    def finish(gathers):
        @pl.loop(0, share)
        def _(i):
            extent = extent_ref[me_tm * share + i]
            cell = lax.broadcasted_iota(jnp.int32, (1, depth), 1)
            mask = (cell < extent).astype(jnp.float32)
            for g in gathers:
                out_ref[i, g] = (
                    acc[i, g][:OFFS] * (1.0 / math.sqrt(steps * times)) * mask
                )

    turn_first = one_hot(SPAN, 4 * ROWS, lambda row, column: column == OFFS - 1 - row)
    turn_last = one_hot(SPAN + ROWS, 4 * ROWS, lambda row, column: column == 4 * ROWS - row)
    wide = width - 3 * ROWS

    def edge_pass(part, fresh):
        @pl.loop(0, share)
        def _(i):
            extra = b_recv[part, b_rims:].reshape(b_extra * ROWS, depth)
            sums = [None] * 3
            for t in range(steps):
                scale = weight(part, t)
                place = i * pieces + t
                rims = (i * steps + t) * 2
                rims_rcv = ((share + i) * steps + t) * 2
                src_left = b_recv[part, rims]
                src_right = b_recv[part, rims + 1]
                rcv_left = b_recv[part, rims_rcv]
                rcv_right = b_recv[part, rims_rcv + 1]
                turned = pick(
                    turn_first,
                    jnp.concatenate([src_left, centre[0, part, i, t, : 3 * ROWS]], axis=0),
                )
                straight = jnp.concatenate(
                    [rcv_left, centre[1, part, i, t, : 3 * ROWS]], axis=0
                ).astype(jnp.float32)
                products = [turned * scale * straight[:SPAN]]
                turn_extra = one_hot(
                    SPAN + ROWS,
                    b_extra * ROWS,
                    lambda row, column: (row == 0) & (column == place),
                )
                turned = pick(
                    turn_last,
                    jnp.concatenate([centre[0, part, i, t, wide:], src_right], axis=0),
                ) + pick(turn_extra, extra)
                turned = turned * scale
                rcv_extra = pick(
                    one_hot(
                        8,
                        b_extra * ROWS,
                        lambda row, column: (row == 0) & (column == place + steps),
                    ),
                    extra,
                )
                straight = jnp.concatenate(
                    [
                        centre[1, part, i, t, wide:].astype(jnp.float32),
                        rcv_right.astype(jnp.float32),
                        rcv_extra,
                    ],
                    axis=0,
                )
                products.append(turned[ROWS:] * straight[:SPAN])
                products.append(turned[:SPAN] * straight[ROWS:])
                sums = [
                    product if total is None else total + product
                    for total, product in zip(sums, products)
                ]
            for g, total in zip((0, GB - 2, GB - 1), sums):
                if fresh:
                    acc[i, g] = total
                else:
                    acc[i, g] += total

    edge_pass(me_tm, True)
    for j in range(1, times):
        for f in range(2):
            main_copies[2 * (j - 1) + f].wait_recv()
        centre_pass(rest(times, me_tm, times - j), False)
    finish(range(1, GB - 2))
    for j in range(1, times):
        b_copy(j).wait_recv()
        edge_pass(rest(times, me_tm, times - j), False)
    finish((0, GB - 2, GB - 1))

    for copy in main_copies:
        copy.wait_send()
    for j in range(1, times):
        b_copy(j).wait_send()


def routes(nbr_device, nbr_index, devices, capacity, tiles):
    own = lax.axis_index("tile")
    count = 2 * tiles
    device = nbr_device.reshape(devices, count)
    index = nbr_index.reshape(devices, count)
    ids = jnp.arange(count, dtype=jnp.int32)
    earlier = ids[None, :] < ids[:, None]
    same = (device[:, :, None] == device[:, None, :]) & earlier[None]
    rank = jnp.sum(same.astype(jnp.int32), axis=2)
    slot = jnp.arange(capacity, dtype=jnp.int32)
    hit = ((device == own)[:, None, :] & (rank[:, None, :] == slot[None, :, None])).astype(jnp.int32)
    wanted = jnp.stack([index, jnp.broadcast_to((ids % 2)[None, :], index.shape)])
    send_tab = jnp.sum(hit[None] * wanted[:, :, None, :], axis=3)
    arrive = jnp.stack([device, rank])
    arrive_tab = lax.dynamic_slice_in_dim(arrive, own, 1, 1)[:, 0]
    return send_tab, arrive_tab


def local(src_snap, rcv_snap, q_rate, nbr_device, nbr_index, depth_extent):
    tiles, steps, width, depth = src_snap.shape
    devices = lax.axis_size("tile")
    times = lax.axis_size("tm")
    capacity = (2 * tiles + devices - 1) // devices + 1
    share = tiles // times
    send_tab, arrive_tab = routes(nbr_device, nbr_index, devices, capacity, tiles)
    pieces = 2 * steps
    a_blocks = capacity * pieces + -(-capacity * pieces // ROWS)
    b_blocks = 2 * share * steps * 2 + -(-share * pieces // ROWS)
    sizes = (tiles, steps, width, depth, devices, times, capacity, share)
    half = jnp.bfloat16
    products = share * GB * OFFS * depth * steps * times
    return pl.pallas_call(
        functools.partial(kernel, sizes),
        out_shape=jax.ShapeDtypeStruct((share, GB, OFFS, depth), jnp.float32),
        in_specs=[pl.BlockSpec(memory_space=pltpu.SMEM)] * 3
        + [pl.BlockSpec(memory_space=pltpu.VMEM)]
        + [pl.BlockSpec(memory_space=pl.ANY)] * 2,
        out_specs=pl.BlockSpec(memory_space=pltpu.VMEM),
        scratch_shapes=[
            pltpu.VMEM((2, 3, tiles, steps, ROWS, depth), half),
            pltpu.VMEM((devices, a_blocks, ROWS, depth), half),
            pltpu.VMEM((devices, a_blocks, ROWS, depth), half),
            pltpu.VMEM((times, b_blocks, ROWS, depth), half),
            pltpu.VMEM((times, b_blocks, ROWS, depth), half),
            pltpu.VMEM((2, times, share, steps, width, depth), half),
            pltpu.VMEM((share, GB, SPAN, depth), jnp.float32),
            pltpu.SemaphoreType.DMA((6,)),
            pltpu.SemaphoreType.DMA((2,)),
            pltpu.SemaphoreType.DMA((times, 2)),
            pltpu.SemaphoreType.DMA((times, 2)),
            pltpu.SemaphoreType.DMA((devices,)),
            pltpu.SemaphoreType.DMA((devices,)),
            pltpu.SemaphoreType.DMA((times,)),
            pltpu.SemaphoreType.DMA((times,)),
        ],
        compiler_params=pltpu.CompilerParams(
            collective_id=0, has_side_effects=True, vmem_limit_bytes=40 * 1024 * 1024
        ),
        cost_estimate=pl.CostEstimate(
            flops=3 * products, bytes_accessed=4 * tiles * steps * width * depth, transcendentals=0
        ),
    )(send_tab, arrive_tab, depth_extent, q_rate.reshape(1, depth), src_snap, rcv_snap)


def mask_kernel(scale, extent_ref, sums_ref, image_ref):
    tile = pl.program_id(0)
    extent = extent_ref[lax.axis_index("tm") * pl.num_programs(0) + tile]
    cell = lax.broadcasted_iota(jnp.int32, (1, 128), 1)
    for part in range(sums_ref.shape[1]):
        mask = (cell + 128 * part < extent).astype(jnp.float32)
        image_ref[0, :, 128 * part : 128 * (part + 1)] = sums_ref[0, part] * scale * mask


def pair_kernel(
    sizes,
    device_in,
    index_in,
    rate_in,
    src_ref,
    rcv_ref,
    out_ref,
    device_tab,
    index_tab,
    rate_ref,
    ranks,
    edge_cells,
    a_send,
    a_recv,
    b_own,
    b_send,
    b_recv,
    centre,
    acc,
    acc_mid,
    acc_edge,
    kept,
    pc_send,
    pc_recv,
    pe_send,
    pe_recv,
    small_sem,
    edge_sem,
    own_sem,
    main_send_sem,
    main_recv_sem,
    a_send_sem,
    a_recv_sem,
    b_send_sem,
    b_recv_sem,
    p_send_sem,
    p_recv_sem,
):
    tiles, steps, width, depth, devices, times, capacity, share = sizes
    half = share // 2
    pieces = 2 * steps
    fields = (src_ref, rcv_ref)
    me_tile = lax.axis_index("tile")
    me_tm = lax.axis_index("tm")
    low = lax.rem(me_tm, 2)
    high = lax.div(me_tm, 2)
    by_x = high * 2 + 1 - low
    by_y = (1 - high) * 2 + low
    across = (1 - high) * 2 + 1 - low

    owner = (by_y, by_x, me_tm, me_tm)
    partner = (by_x, by_y, by_x, by_y)
    owner_there = (across, across, by_x, by_y)
    offset = (0, half, 0, half)

    def first_tile(owners, w):
        return owners[w] * share + offset[w]

    barrier = pltpu.get_barrier_semaphore()
    for to in (by_x, by_y):
        pl.semaphore_signal(barrier, inc=1, device_id=(me_tile, to), device_id_type=MESH)
    for j in range(1, devices):
        pl.semaphore_signal(
            barrier, inc=1, device_id=(lax.rem(me_tile + j, devices), me_tm), device_id_type=MESH
        )
    small_copies = []
    smalls = ((device_in, device_tab), (index_in, index_tab), (rate_in, rate_ref))
    for k, (source, target) in enumerate(smalls):
        copy = pltpu.make_async_copy(source, target, small_sem.at[k])
        copy.start()
        small_copies.append(copy)
    edge_copies = []
    for f in range(2):
        for k, first in enumerate((width - ROWS, 0, ROWS)):
            copy = pltpu.make_async_copy(
                fields[f].at[:, :, pl.ds(first, ROWS), :],
                edge_cells.at[f, k],
                edge_sem.at[f * 3 + k],
            )
            copy.start()
            edge_copies.append(copy)

    pl.semaphore_wait(barrier, devices + 1)

    main_copies = []

    def start_main(w):
        copies = []
        for f in range(2):
            copy = pltpu.make_async_remote_copy(
                src_ref=fields[f].at[pl.ds(first_tile(owner_there, w), half)],
                dst_ref=centre.at[f, 1, w],
                send_sem=main_send_sem.at[w, f],
                recv_sem=main_recv_sem.at[w, f],
                device_id=(me_tile, partner[w]),
                device_id_type=MESH,
            )
            copy.start()
            copies.append(copy)
        main_copies.append(copies)

    for w in range(2):
        start_main(w)
    own_copies = []
    for w in range(4):
        for f in range(2):
            copy = pltpu.make_async_copy(
                fields[f].at[pl.ds(first_tile(owner, w), half)],
                centre.at[f, 0, w],
                own_sem.at[w, f],
            )
            copy.start()
            own_copies.append(copy)

    for copy in small_copies + edge_copies:
        copy.wait()

    a_extra = a_send.shape[1] - capacity * pieces
    compress = one_hot(
        a_extra * ROWS, capacity * pieces * ROWS, lambda row, column: column == row * ROWS
    )

    def pack(to):
        def scan(row, carry):
            count, codes = carry
            for side in range(2):
                hit = device_tab[side, to * tiles + row] == me_tile
                code = index_tab[side, to * tiles + row] * 2 + side
                codes = tuple(
                    jnp.where(hit & (count == k), code, codes[k]) for k in range(capacity)
                )
                count = count + hit.astype(jnp.int32)
            return count, codes

        zero = jnp.int32(0)
        _, codes = lax.fori_loop(0, tiles, scan, (zero, (zero,) * capacity))
        extra = []
        for k in range(capacity):
            index = lax.div(codes[k], 2)
            side = lax.rem(codes[k], 2)
            for f in range(2):
                first = k * pieces + f * steps
                a_send[to, first : first + steps] = edge_cells[f, side, index]
                extra.append(edge_cells[f, 2, index].reshape(steps * ROWS, depth))
        packed = pick(compress, jnp.concatenate(extra, axis=0))
        a_send[to, capacity * pieces :] = packed.astype(jnp.bfloat16).reshape(
            a_extra, ROWS, depth
        )

    def other(j):
        total, unit = jnp.int32(0), 1
        while unit < devices:
            mine = lax.rem(lax.div(me_tile, unit), 2)
            flip = lax.rem(lax.div(j, unit), 2)
            total = total + (mine + flip - 2 * mine * flip) * unit
            unit *= 2
        return total

    def a_copy(j):
        to = other(j)
        return pltpu.make_async_remote_copy(
            src_ref=a_send.at[to],
            dst_ref=a_recv.at[me_tile],
            send_sem=a_send_sem.at[j],
            recv_sem=a_recv_sem.at[j],
            device_id=(to, me_tm),
            device_id_type=MESH,
        )

    @pl.loop(1, devices)
    def _(back):
        j = devices - back
        pack(other(j))
        a_copy(j).start()

    for w in (2, 3):
        start_main(w)
    pack(me_tile)
    a_recv[me_tile] = a_send[me_tile]

    base = me_tile * tiles

    @pl.loop(0, tiles)
    def _(row):
        mine = [device_tab[side, base + row] for side in range(2)]

        def count(other, sums):
            theirs = [device_tab[side, base + other] for side in range(2)]
            return tuple(
                sums[side]
                + (theirs[0] == mine[side]).astype(jnp.int32)
                + (theirs[1] == mine[side]).astype(jnp.int32)
                for side in range(2)
            )

        found = lax.fori_loop(0, row, count, (jnp.int32(0), jnp.int32(0)))
        for side in range(2):
            ranks[side, row] = jnp.minimum(found[side], capacity - 1)

    rate = rate_ref[...]

    def weight(part, t):
        step = (part * steps + t).astype(jnp.float32)
        return jnp.exp(rate * step / (steps * times))

    weights = [[weight(part, t) for t in range(steps)] for part in (me_tm, by_x, by_y)]

    def weights_of(p, w):
        return weights[0] if p == 0 else weights[1 + w % 2]

    inner = range(1, GB - 2)
    middle = ((0, 16, 17, 0), (GB - 2, 1, 47, 25), (GB - 1, 17, 15, 73))
    border = (
        (0, 0, 16),
        (0, 33, 16),
        (GB - 1, 1, 16),
        (GB - 1, 32, 16),
        (GB - 1, 0, 1),
        (GB - 1, 48, 1),
        (GB - 2, 0, 1),
        (GB - 2, 48, 1),
    )
    turn_centre = one_hot(width + 8, width, lambda row, column: column == width - row)
    last = width // GSTEP * GSTEP + ROWS - HMAX * 2

    def centre_sums(w, p, i):
        sums = [None] * GB
        mids = [None] * 3
        for t in range(steps):
            turned = pick(turn_centre, centre[0, p, w, i, t]) * weights_of(p, w)[t]
            kept[p, w, i, t, : 3 * ROWS] = turned[ROWS : 4 * ROWS]
            kept[p, w, i, t, 3 * ROWS :] = turned[6 * ROWS : 7 * ROWS]
            straight = centre[1, p, w, i, t].astype(jnp.float32)
            products = (
                turned[width - ROWS :] * straight[:24],
                turned[: 3 * ROWS] * straight[width - 3 * ROWS :],
                turned[:ROWS] * straight[width - ROWS :],
            )
            mids = [
                product if total is None else total + product
                for total, product in zip(mids, products)
            ]
            for g in inner:
                back = last - GSTEP * g
                ahead = GSTEP * (g - 1)
                product = turned[back : back + SPAN] * straight[ahead : ahead + SPAN]
                sums[g] = product if sums[g] is None else sums[g] + product
        return sums, jnp.concatenate(mids, axis=0)

    b_rims = 2 * half * steps * 2
    b_extra = b_send.shape[1] - b_rims
    rim_rows = b_rims // 2 * ROWS
    turn_rims = one_hot(
        rim_rows,
        rim_rows,
        lambda row, column: column == row // ROWS * (2 * ROWS) + ROWS - 1 - row,
    )

    def edge_sums(rims_ref, w, p):
        extra = rims_ref[w, b_rims:].reshape(b_extra * ROWS, depth).astype(jnp.float32)
        turned_rims = pick(turn_rims, rims_ref[w, : b_rims // 2].reshape(rim_rows, depth))
        found = []
        for i in range(half):
            total = None
            for t in range(steps):
                scale = weights_of(p, w)[t]
                place = i * pieces + t
                block = (i * steps + t) * 2
                left = turned_rims[block * ROWS : (block + 1) * ROWS] * scale
                right = turned_rims[(block + 1) * ROWS : (block + 2) * ROWS] * scale
                rims_rcv = b_rims // 2 + block
                rcv_left = rims_ref[w, rims_rcv].astype(jnp.float32)
                rcv_right = rims_ref[w, rims_rcv + 1].astype(jnp.float32)
                turned = kept[p, w, i, t]
                near = centre[1, p, w, i, t, ROWS : 3 * ROWS].astype(jnp.float32)
                far = centre[1, p, w, i, t, width - 3 * ROWS :].astype(jnp.float32)
                src_extra = extra[place : place + 1] * scale
                rcv_extra = extra[place + steps : place + steps + 1]
                product = jnp.concatenate(
                    [
                        turned[3 * ROWS :] * rcv_left,
                        left * near[1 : ROWS + 1],
                        right * far[ROWS + 1 : 2 * ROWS + 1],
                        turned[:ROWS] * rcv_right,
                        src_extra * far[ROWS : ROWS + 1],
                        turned[ROWS : ROWS + 1] * rcv_extra,
                        right[ROWS - 1 :] * far[:1],
                        turned[2 * ROWS : 2 * ROWS + 1] * rcv_right[:1],
                        jnp.zeros((4, depth), jnp.float32),
                    ],
                    axis=0,
                )
                total = product if total is None else total + product
            found.append(total)
        return found

    def own_centre(w):
        @pl.loop(0, half)
        def _(i):
            sums, mids = centre_sums(w, 0, i)
            for g in inner:
                acc[w, i, g] = sums[g]
            acc_mid[w, i] = mids

    def own_edge(w):
        for i, total in enumerate(edge_sums(b_own, w, 0)):
            acc_edge[w, i] = total

    def far_centre(w):
        for copy in main_copies[w]:
            copy.wait_recv()

        @pl.loop(0, half)
        def _(i):
            sums, mids = centre_sums(w, 1, i)
            mids = acc_mid[w, i] + mids
            if w < 2:
                first = OFFS * len(inner)
                for _, _, count, place in middle:
                    pc_send[w, i, first : first + count] = mids[place : place + count]
                    first += count
            else:
                acc_mid[w, i] = mids
            for k, g in enumerate(inner):
                total = acc[w, i, g] + sums[g]
                if w < 2:
                    pc_send[w, i, OFFS * k : OFFS * (k + 1)] = total[:OFFS]
                else:
                    acc[w, i, g] = total

    def far_edge(w):
        b_copies[w].wait_recv()
        target = pe_send if w < 2 else acc_edge
        for i, total in enumerate(edge_sums(b_recv, w, 1)):
            target[w, i] = acc_edge[w, i] + total

    def partial_copy(w, send, recv, k):
        return pltpu.make_async_remote_copy(
            src_ref=send.at[w],
            dst_ref=recv.at[w],
            send_sem=p_send_sem.at[k, w],
            recv_sem=p_recv_sem.at[k, w],
            device_id=(me_tile, owner[w]),
            device_id_type=MESH,
        )

    def unpack(first, target, w):
        row = lax.broadcasted_iota(jnp.int32, (b_extra * ROWS, half * a_extra * ROWS), 0)
        column = lax.broadcasted_iota(jnp.int32, (b_extra * ROWS, half * a_extra * ROWS), 1)
        chosen = jnp.full(row.shape, False)
        extras = []
        for i in range(half):
            tile = first + i
            for side in range(2):
                source = device_tab[side, base + tile]
                rank = ranks[side, tile]
                rim = a_recv[source, pl.ds(rank * pieces, pieces)]
                for f in range(2):
                    for t in range(steps):
                        target[w, ((f * half + i) * steps + t) * 2 + side] = rim[f * steps + t]
            extras.append(
                a_recv[source, capacity * pieces :].reshape(a_extra * ROWS, depth)
            )
            chosen = chosen | (
                (row >= i * pieces)
                & (row < (i + 1) * pieces)
                & (column == i * a_extra * ROWS + rank * pieces + row - i * pieces)
            )
        packed = pick(
            chosen.astype(jnp.float32).astype(jnp.bfloat16), jnp.concatenate(extras, axis=0)
        )
        target[w, b_rims:] = packed.astype(jnp.bfloat16).reshape(b_extra, ROWS, depth)

    def place_rows(tile, g, offs, count, rows):
        for part in range(depth // 128):
            out_ref[tile, part, pl.ds(offs * GB + g, count, stride=GB), :] = rows[
                :, 128 * part : 128 * (part + 1)
            ]

    def finish_early(w):
        @pl.loop(0, half)
        def _(i):
            tile = offset[w] + i
            first = 0
            for g in inner:
                got = pc_recv[w - 2, i, first : first + OFFS]
                place_rows(tile, g, 0, OFFS, acc[w, i, g][:OFFS] + got)
                first += OFFS
            mids = acc_mid[w, i]
            for g, offs, count, place in middle:
                got = pc_recv[w - 2, i, first : first + count]
                place_rows(tile, g, offs, count, mids[place : place + count] + got)
                first += count

    def finish_late(w):
        @pl.loop(0, half)
        def _(i):
            tile = offset[w] + i
            first = 0
            for g, offs, count in border:
                got = pe_recv[w - 2, i, first : first + count]
                place_rows(tile, g, offs, count, acc_edge[w, i, first : first + count] + got)
                first += count

    for copy in own_copies:
        copy.wait()
    for w in range(4):
        own_centre(w)

    pc_copies = []
    for w in range(2):
        far_centre(w)
        copy = partial_copy(w, pc_send, pc_recv, 0)
        copy.start()
        pc_copies.append(copy)
    for w in (2, 3):
        far_centre(w)

    @pl.loop(1, devices)
    def _(j):
        a_copy(j).wait()

    b_copies = []
    for w in range(4):
        unpack(first_tile(owner_there, w), b_send, w)
        copy = pltpu.make_async_remote_copy(
            src_ref=b_send.at[w],
            dst_ref=b_recv.at[w],
            send_sem=b_send_sem.at[w],
            recv_sem=b_recv_sem.at[w],
            device_id=(me_tile, partner[w]),
            device_id_type=MESH,
        )
        copy.start()
        b_copies.append(copy)
    for w in range(2):
        unpack(first_tile(owner, w), b_own, w)
        own_edge(w)

    pe_copies = []
    for w in range(2):
        far_edge(w)
        copy = partial_copy(w, pe_send, pe_recv, 1)
        copy.start()
        pe_copies.append(copy)
    for w in (2, 3):
        unpack(first_tile(owner, w), b_own, w)
        own_edge(w)
        far_edge(w)
    for w in (2, 3):
        pc_copies[w - 2].wait_recv()
        finish_early(w)
    for w in (2, 3):
        pe_copies[w - 2].wait_recv()
        finish_late(w)

    for copies in main_copies:
        for copy in copies:
            copy.wait_send()
    for copy in b_copies + pc_copies + pe_copies:
        copy.wait_send()


def paired(src_snap, rcv_snap, q_rate, nbr_device, nbr_index, depth_extent):
    tiles, steps, width, depth = src_snap.shape
    devices = lax.axis_size("tile")
    times = lax.axis_size("tm")
    capacity = (2 * tiles + devices - 1) // devices + 1
    share = tiles // times
    half = share // 2
    pieces = 2 * steps
    a_blocks = capacity * pieces + -(-capacity * pieces // ROWS)
    b_blocks = 2 * half * steps * 2 + -(-half * pieces // ROWS)
    inner_rows = 328
    outer_rows = 72
    sizes = (tiles, steps, width, depth, devices, times, capacity, share)
    bf16, f32 = jnp.bfloat16, jnp.float32
    products = share * GB * OFFS * depth * steps * times
    parts = depth // 128
    sums = pl.pallas_call(
        functools.partial(pair_kernel, sizes),
        out_shape=jax.ShapeDtypeStruct((share, parts, OFFS * GB, 128), f32),
        in_specs=[pl.BlockSpec(memory_space=pltpu.HBM)] * 5,
        out_specs=pl.BlockSpec(memory_space=pltpu.VMEM),
        scratch_shapes=[
            pltpu.SMEM(nbr_device.shape[::-1], jnp.int32),
            pltpu.SMEM(nbr_index.shape[::-1], jnp.int32),
            pltpu.VMEM((1, depth), f32),
            pltpu.SMEM((2, tiles), jnp.int32),
            pltpu.VMEM((2, 3, tiles, steps, ROWS, depth), bf16),
            pltpu.VMEM((devices, a_blocks, ROWS, depth), bf16),
            pltpu.VMEM((devices, a_blocks, ROWS, depth), bf16),
            pltpu.VMEM((4, b_blocks, ROWS, depth), bf16),
            pltpu.VMEM((4, b_blocks, ROWS, depth), bf16),
            pltpu.VMEM((4, b_blocks, ROWS, depth), bf16),
            pltpu.VMEM((2, 2, 4, half, steps, width, depth), bf16),
            pltpu.VMEM((4, half, GB, SPAN, depth), f32),
            pltpu.VMEM((4, half, 88, depth), f32),
            pltpu.VMEM((4, half, outer_rows, depth), f32),
            pltpu.VMEM((2, 4, half, steps, 4 * ROWS, depth), f32),
            pltpu.VMEM((2, half, inner_rows, depth), f32),
            pltpu.VMEM((2, half, inner_rows, depth), f32),
            pltpu.VMEM((2, half, outer_rows, depth), f32),
            pltpu.VMEM((2, half, outer_rows, depth), f32),
            pltpu.SemaphoreType.DMA((3,)),
            pltpu.SemaphoreType.DMA((6,)),
            pltpu.SemaphoreType.DMA((4, 2)),
            pltpu.SemaphoreType.DMA((4, 2)),
            pltpu.SemaphoreType.DMA((4, 2)),
            pltpu.SemaphoreType.DMA((devices,)),
            pltpu.SemaphoreType.DMA((devices,)),
            pltpu.SemaphoreType.DMA((4,)),
            pltpu.SemaphoreType.DMA((4,)),
            pltpu.SemaphoreType.DMA((2, 2)),
            pltpu.SemaphoreType.DMA((2, 2)),
        ],
        compiler_params=pltpu.CompilerParams(
            collective_id=1, has_side_effects=True, vmem_limit_bytes=60 * 1024 * 1024
        ),
        cost_estimate=pl.CostEstimate(
            flops=3 * products, bytes_accessed=4 * tiles * steps * width * depth, transcendentals=0
        ),
    )(nbr_device.T, nbr_index.T, q_rate.reshape(1, depth), src_snap, rcv_snap)
    image = pl.pallas_call(
        functools.partial(mask_kernel, 1.0 / math.sqrt(steps * times)),
        out_shape=jax.ShapeDtypeStruct((share, OFFS * GB, depth), f32),
        grid=(share,),
        in_specs=[
            pl.BlockSpec(memory_space=pltpu.SMEM),
            pl.BlockSpec((1, parts, OFFS * GB, 128), lambda i: (i, 0, 0, 0)),
        ],
        out_specs=pl.BlockSpec((1, OFFS * GB, depth), lambda i: (i, 0, 0)),
        compiler_params=pltpu.CompilerParams(vmem_limit_bytes=60 * 1024 * 1024),
    )(depth_extent, sums)
    return image.reshape(share, OFFS, GB, depth).transpose(0, 2, 1, 3)


def solution(mesh):
    placed = (P("tile", "tm", None, None), P("tile", "tm", None, None), P(), P(), P(), P("tile"))
    body = paired if mesh.shape["tm"] == 4 else local
    return jax.shard_map(
        body,
        mesh=mesh,
        in_specs=placed,
        out_specs=P(("tile", "tm"), None, None, None),
        check_vma=False,
    )
```

```python
import functools
import math

import jax
import jax.numpy as jnp
from jax import lax
from jax.experimental import pallas as pl
from jax.experimental.pallas import tpu as pltpu
from jax.sharding import PartitionSpec as P

GSTEP = 16
HMAX = 24
GB = 8
OFFS = 49
RIM_L = 16
RIM_R = 17
ROWS = 16
SPAN = 56
MESH = pl.DeviceIdType.MESH


def one_hot(rows, columns, rule):
    row = lax.broadcasted_iota(jnp.int32, (rows, columns), 0)
    column = lax.broadcasted_iota(jnp.int32, (rows, columns), 1)
    return rule(row, column).astype(jnp.float32).astype(jnp.bfloat16)


def pick(matrix, values):
    return jnp.dot(matrix, values, preferred_element_type=jnp.float32)


def kernel(
    sizes,
    send_tab,
    arrive_tab,
    extent_ref,
    rate_ref,
    src_ref,
    rcv_ref,
    out_ref,
    edge_cells,
    a_send,
    a_recv,
    b_send,
    b_recv,
    centre,
    acc,
    edge_sem,
    own_sem,
    main_send_sem,
    main_recv_sem,
    a_send_sem,
    a_recv_sem,
    b_send_sem,
    b_recv_sem,
):
    tiles, steps, width, depth, devices, times, capacity, share = sizes
    pieces = 2 * steps
    fields = (src_ref, rcv_ref)
    me_tile = lax.axis_index("tile")
    me_tm = lax.axis_index("tm")

    def rest(count, me, j):
        return lax.rem(me + j, count)

    edge_copies = []
    for f in range(2):
        for k, first in enumerate((width - ROWS, 0, ROWS)):
            copy = pltpu.make_async_copy(
                fields[f].at[:, :, pl.ds(first, ROWS), :],
                edge_cells.at[f, k],
                edge_sem.at[f * 3 + k],
            )
            copy.start()
            edge_copies.append(copy)
    own_copies = []
    for f in range(2):
        copy = pltpu.make_async_copy(
            fields[f].at[pl.ds(me_tm * share, share)], centre.at[f, me_tm], own_sem.at[f]
        )
        copy.start()
        own_copies.append(copy)

    barrier = pltpu.get_barrier_semaphore()
    for j in range(1, times):
        pl.semaphore_signal(
            barrier, inc=1, device_id=(me_tile, rest(times, me_tm, j)), device_id_type=MESH
        )
    for j in range(1, devices):
        pl.semaphore_signal(
            barrier, inc=1, device_id=(rest(devices, me_tile, j), me_tm), device_id_type=MESH
        )
    pl.semaphore_wait(barrier, times + devices - 2)

    main_copies = []
    for j in range(1, times):
        to = rest(times, me_tm, j)
        for f in range(2):
            copy = pltpu.make_async_remote_copy(
                src_ref=fields[f].at[pl.ds(to * share, share)],
                dst_ref=centre.at[f, me_tm],
                send_sem=main_send_sem.at[j, f],
                recv_sem=main_recv_sem.at[j, f],
                device_id=(me_tile, to),
                device_id_type=MESH,
            )
            copy.start()
            main_copies.append(copy)

    for copy in edge_copies:
        copy.wait()

    a_extra = a_send.shape[1] - capacity * pieces
    compress = one_hot(
        a_extra * ROWS, capacity * pieces * ROWS, lambda row, column: column == row * ROWS
    )

    def pack(to):
        extra = []
        for k in range(capacity):
            index = send_tab[0, to, k]
            side = send_tab[1, to, k]
            for f in range(2):
                first = k * pieces + f * steps
                a_send[to, first : first + steps] = edge_cells[f, side, index]
                extra.append(edge_cells[f, 2, index].reshape(steps * ROWS, depth))
        packed = pick(compress, jnp.concatenate(extra, axis=0))
        a_send[to, capacity * pieces :] = packed.astype(jnp.bfloat16).reshape(
            a_extra, ROWS, depth
        )

    def a_copy(j):
        to = rest(devices, me_tile, j)
        return pltpu.make_async_remote_copy(
            src_ref=a_send.at[to],
            dst_ref=a_recv.at[me_tile],
            send_sem=a_send_sem.at[j],
            recv_sem=a_recv_sem.at[j],
            device_id=(to, me_tm),
            device_id_type=MESH,
        )

    @pl.loop(1, devices)
    def _(j):
        pack(rest(devices, me_tile, j))
        a_copy(j).start()

    pack(me_tile)
    a_recv[me_tile] = a_send[me_tile]

    rate = rate_ref[...]

    def weight(part, t):
        step = (part * steps + t).astype(jnp.float32)
        return jnp.exp(rate * step / (steps * times))

    turn_centre = one_hot(
        width - 8, width, lambda row, column: column == width - ROWS - row
    )
    last = width // GSTEP * GSTEP - HMAX * 2

    def centre_pass(part, fresh):
        @pl.loop(0, share)
        def _(i):
            sums = [None] * GB
            for t in range(steps):
                turned = pick(turn_centre, centre[0, part, i, t]) * weight(part, t)
                straight = centre[1, part, i, t].astype(jnp.float32)
                for g in range(1, GB - 2):
                    back = last - GSTEP * g
                    ahead = GSTEP * (g - 1)
                    product = turned[back : back + SPAN] * straight[ahead : ahead + SPAN]
                    sums[g] = product if sums[g] is None else sums[g] + product
            for g in range(1, GB - 2):
                if fresh:
                    acc[i, g] = sums[g]
                else:
                    acc[i, g] += sums[g]

    for copy in own_copies:
        copy.wait()
    centre_pass(me_tm, True)

    @pl.loop(1, devices)
    def _(j):
        a_copy(j).wait()

    b_rims = 2 * share * steps * 2
    b_extra = b_send.shape[1] - b_rims

    def unpack(to):
        packed = None
        for i in range(share):
            tile = to * share + i
            for side in range(2):
                source = arrive_tab[0, 2 * tile + side]
                rank = arrive_tab[1, 2 * tile + side]
                rim = a_recv[source, pl.ds(rank * pieces, pieces)]
                for f in range(2):
                    for t in range(steps):
                        b_send[to, ((f * share + i) * steps + t) * 2 + side] = rim[f * steps + t]
            extra = a_recv[source, capacity * pieces :].reshape(a_extra * ROWS, depth)
            choose = one_hot(
                b_extra * ROWS,
                a_extra * ROWS,
                lambda row, column: (row >= i * pieces)
                & (row < (i + 1) * pieces)
                & (column == rank * pieces + row - i * pieces),
            )
            chosen = pick(choose, extra)
            packed = chosen if packed is None else packed + chosen
        b_send[to, b_rims:] = packed.astype(jnp.bfloat16).reshape(b_extra, ROWS, depth)

    def b_copy(j):
        to = rest(times, me_tm, j)
        return pltpu.make_async_remote_copy(
            src_ref=b_send.at[to],
            dst_ref=b_recv.at[me_tm],
            send_sem=b_send_sem.at[j],
            recv_sem=b_recv_sem.at[j],
            device_id=(me_tile, to),
            device_id_type=MESH,
        )

    @pl.loop(1, times)
    def _(j):
        unpack(rest(times, me_tm, j))
        b_copy(j).start()

    unpack(me_tm)
    b_recv[me_tm] = b_send[me_tm]

    def finish(gathers):
        @pl.loop(0, share)
        def _(i):
            extent = extent_ref[me_tm * share + i]
            cell = lax.broadcasted_iota(jnp.int32, (1, depth), 1)
            mask = (cell < extent).astype(jnp.float32)
            for g in gathers:
                out_ref[i, g] = (
                    acc[i, g][:OFFS] * (1.0 / math.sqrt(steps * times)) * mask
                )

    turn_first = one_hot(SPAN, 4 * ROWS, lambda row, column: column == OFFS - 1 - row)
    turn_last = one_hot(SPAN + ROWS, 4 * ROWS, lambda row, column: column == 4 * ROWS - row)
    wide = width - 3 * ROWS

    def edge_pass(part, fresh):
        @pl.loop(0, share)
        def _(i):
            extra = b_recv[part, b_rims:].reshape(b_extra * ROWS, depth)
            sums = [None] * 3
            for t in range(steps):
                scale = weight(part, t)
                place = i * pieces + t
                rims = (i * steps + t) * 2
                rims_rcv = ((share + i) * steps + t) * 2
                src_left = b_recv[part, rims]
                src_right = b_recv[part, rims + 1]
                rcv_left = b_recv[part, rims_rcv]
                rcv_right = b_recv[part, rims_rcv + 1]
                turned = pick(
                    turn_first,
                    jnp.concatenate([src_left, centre[0, part, i, t, : 3 * ROWS]], axis=0),
                )
                straight = jnp.concatenate(
                    [rcv_left, centre[1, part, i, t, : 3 * ROWS]], axis=0
                ).astype(jnp.float32)
                products = [turned * scale * straight[:SPAN]]
                turn_extra = one_hot(
                    SPAN + ROWS,
                    b_extra * ROWS,
                    lambda row, column: (row == 0) & (column == place),
                )
                turned = pick(
                    turn_last,
                    jnp.concatenate([centre[0, part, i, t, wide:], src_right], axis=0),
                ) + pick(turn_extra, extra)
                turned = turned * scale
                rcv_extra = pick(
                    one_hot(
                        8,
                        b_extra * ROWS,
                        lambda row, column: (row == 0) & (column == place + steps),
                    ),
                    extra,
                )
                straight = jnp.concatenate(
                    [
                        centre[1, part, i, t, wide:].astype(jnp.float32),
                        rcv_right.astype(jnp.float32),
                        rcv_extra,
                    ],
                    axis=0,
                )
                products.append(turned[ROWS:] * straight[:SPAN])
                products.append(turned[:SPAN] * straight[ROWS:])
                sums = [
                    product if total is None else total + product
                    for total, product in zip(sums, products)
                ]
            for g, total in zip((0, GB - 2, GB - 1), sums):
                if fresh:
                    acc[i, g] = total
                else:
                    acc[i, g] += total

    edge_pass(me_tm, True)
    for j in range(1, times):
        for f in range(2):
            main_copies[2 * (j - 1) + f].wait_recv()
        centre_pass(rest(times, me_tm, times - j), False)
    finish(range(1, GB - 2))
    for j in range(1, times):
        b_copy(j).wait_recv()
        edge_pass(rest(times, me_tm, times - j), False)
    finish((0, GB - 2, GB - 1))

    for copy in main_copies:
        copy.wait_send()
    for j in range(1, times):
        b_copy(j).wait_send()


def routes(nbr_device, nbr_index, devices, capacity, tiles):
    own = lax.axis_index("tile")
    count = 2 * tiles
    device = nbr_device.reshape(devices, count)
    index = nbr_index.reshape(devices, count)
    ids = jnp.arange(count, dtype=jnp.int32)
    earlier = ids[None, :] < ids[:, None]
    same = (device[:, :, None] == device[:, None, :]) & earlier[None]
    rank = jnp.sum(same.astype(jnp.int32), axis=2)
    slot = jnp.arange(capacity, dtype=jnp.int32)
    hit = ((device == own)[:, None, :] & (rank[:, None, :] == slot[None, :, None])).astype(jnp.int32)
    wanted = jnp.stack([index, jnp.broadcast_to((ids % 2)[None, :], index.shape)])
    send_tab = jnp.sum(hit[None] * wanted[:, :, None, :], axis=3)
    arrive = jnp.stack([device, rank])
    arrive_tab = lax.dynamic_slice_in_dim(arrive, own, 1, 1)[:, 0]
    return send_tab, arrive_tab


def local(src_snap, rcv_snap, q_rate, nbr_device, nbr_index, depth_extent):
    tiles, steps, width, depth = src_snap.shape
    devices = lax.axis_size("tile")
    times = lax.axis_size("tm")
    capacity = (2 * tiles + devices - 1) // devices + 1
    share = tiles // times
    send_tab, arrive_tab = routes(nbr_device, nbr_index, devices, capacity, tiles)
    pieces = 2 * steps
    a_blocks = capacity * pieces + -(-capacity * pieces // ROWS)
    b_blocks = 2 * share * steps * 2 + -(-share * pieces // ROWS)
    sizes = (tiles, steps, width, depth, devices, times, capacity, share)
    half = jnp.bfloat16
    products = share * GB * OFFS * depth * steps * times
    return pl.pallas_call(
        functools.partial(kernel, sizes),
        out_shape=jax.ShapeDtypeStruct((share, GB, OFFS, depth), jnp.float32),
        in_specs=[pl.BlockSpec(memory_space=pltpu.SMEM)] * 3
        + [pl.BlockSpec(memory_space=pltpu.VMEM)]
        + [pl.BlockSpec(memory_space=pl.ANY)] * 2,
        out_specs=pl.BlockSpec(memory_space=pltpu.VMEM),
        scratch_shapes=[
            pltpu.VMEM((2, 3, tiles, steps, ROWS, depth), half),
            pltpu.VMEM((devices, a_blocks, ROWS, depth), half),
            pltpu.VMEM((devices, a_blocks, ROWS, depth), half),
            pltpu.VMEM((times, b_blocks, ROWS, depth), half),
            pltpu.VMEM((times, b_blocks, ROWS, depth), half),
            pltpu.VMEM((2, times, share, steps, width, depth), half),
            pltpu.VMEM((share, GB, SPAN, depth), jnp.float32),
            pltpu.SemaphoreType.DMA((6,)),
            pltpu.SemaphoreType.DMA((2,)),
            pltpu.SemaphoreType.DMA((times, 2)),
            pltpu.SemaphoreType.DMA((times, 2)),
            pltpu.SemaphoreType.DMA((devices,)),
            pltpu.SemaphoreType.DMA((devices,)),
            pltpu.SemaphoreType.DMA((times,)),
            pltpu.SemaphoreType.DMA((times,)),
        ],
        compiler_params=pltpu.CompilerParams(
            collective_id=0, has_side_effects=True, vmem_limit_bytes=40 * 1024 * 1024
        ),
        cost_estimate=pl.CostEstimate(
            flops=3 * products, bytes_accessed=4 * tiles * steps * width * depth, transcendentals=0
        ),
    )(send_tab, arrive_tab, depth_extent, q_rate.reshape(1, depth), src_snap, rcv_snap)


def pair_kernel(
    sizes,
    device_in,
    index_in,
    extent_in,
    rate_in,
    src_ref,
    rcv_ref,
    out_ref,
    device_tab,
    index_tab,
    extent_ref,
    rate_ref,
    ranks,
    edge_cells,
    a_send,
    a_recv,
    b_own,
    b_send,
    b_recv,
    centre,
    acc,
    acc_mid,
    acc_edge,
    kept,
    turned_out,
    pc_send,
    pc_recv,
    pe_send,
    pe_recv,
    small_sem,
    edge_sem,
    own_sem,
    main_send_sem,
    main_recv_sem,
    a_send_sem,
    a_recv_sem,
    b_send_sem,
    b_recv_sem,
    p_send_sem,
    p_recv_sem,
):
    tiles, steps, width, depth, devices, times, capacity, share = sizes
    half = share // 2
    pieces = 2 * steps
    fields = (src_ref, rcv_ref)
    me_tile = lax.axis_index("tile")
    me_tm = lax.axis_index("tm")
    low = lax.rem(me_tm, 2)
    high = lax.div(me_tm, 2)
    by_x = high * 2 + 1 - low
    by_y = (1 - high) * 2 + low
    across = (1 - high) * 2 + 1 - low

    owner = (by_y, by_x, me_tm, me_tm)
    partner = (by_x, by_y, by_x, by_y)
    owner_there = (across, across, by_x, by_y)
    offset = (0, half, 0, half)

    def first_tile(owners, w):
        return owners[w] * share + offset[w]

    barrier = pltpu.get_barrier_semaphore()
    for to in (by_x, by_y):
        pl.semaphore_signal(barrier, inc=1, device_id=(me_tile, to), device_id_type=MESH)
    for j in range(1, devices):
        pl.semaphore_signal(
            barrier, inc=1, device_id=(lax.rem(me_tile + j, devices), me_tm), device_id_type=MESH
        )
    small_copies = []
    smalls = ((device_in, device_tab), (index_in, index_tab), (extent_in, extent_ref), (rate_in, rate_ref))
    for k, (source, target) in enumerate(smalls):
        copy = pltpu.make_async_copy(source, target, small_sem.at[k])
        copy.start()
        small_copies.append(copy)
    edge_copies = []
    for f in range(2):
        for k, first in enumerate((width - ROWS, 0, ROWS)):
            copy = pltpu.make_async_copy(
                fields[f].at[:, :, pl.ds(first, ROWS), :],
                edge_cells.at[f, k],
                edge_sem.at[f * 3 + k],
            )
            copy.start()
            edge_copies.append(copy)

    pl.semaphore_wait(barrier, devices + 1)

    main_copies = []

    def start_main(w):
        copies = []
        for f in range(2):
            copy = pltpu.make_async_remote_copy(
                src_ref=fields[f].at[pl.ds(first_tile(owner_there, w), half)],
                dst_ref=centre.at[f, 1, w],
                send_sem=main_send_sem.at[w, f],
                recv_sem=main_recv_sem.at[w, f],
                device_id=(me_tile, partner[w]),
                device_id_type=MESH,
            )
            copy.start()
            copies.append(copy)
        main_copies.append(copies)

    for w in range(2):
        start_main(w)
    own_copies = []
    for w in range(4):
        for f in range(2):
            copy = pltpu.make_async_copy(
                fields[f].at[pl.ds(first_tile(owner, w), half)],
                centre.at[f, 0, w],
                own_sem.at[w, f],
            )
            copy.start()
            own_copies.append(copy)

    for copy in small_copies + edge_copies:
        copy.wait()

    a_extra = a_send.shape[1] - capacity * pieces
    compress = one_hot(
        a_extra * ROWS, capacity * pieces * ROWS, lambda row, column: column == row * ROWS
    )

    def pack(to):
        def scan(row, carry):
            count, codes = carry
            for side in range(2):
                hit = device_tab[side, to * tiles + row] == me_tile
                code = index_tab[side, to * tiles + row] * 2 + side
                codes = tuple(
                    jnp.where(hit & (count == k), code, codes[k]) for k in range(capacity)
                )
                count = count + hit.astype(jnp.int32)
            return count, codes

        zero = jnp.int32(0)
        _, codes = lax.fori_loop(0, tiles, scan, (zero, (zero,) * capacity))
        extra = []
        for k in range(capacity):
            index = lax.div(codes[k], 2)
            side = lax.rem(codes[k], 2)
            for f in range(2):
                first = k * pieces + f * steps
                a_send[to, first : first + steps] = edge_cells[f, side, index]
                extra.append(edge_cells[f, 2, index].reshape(steps * ROWS, depth))
        packed = pick(compress, jnp.concatenate(extra, axis=0))
        a_send[to, capacity * pieces :] = packed.astype(jnp.bfloat16).reshape(
            a_extra, ROWS, depth
        )

    def other(j):
        total, unit = jnp.int32(0), 1
        while unit < devices:
            mine = lax.rem(lax.div(me_tile, unit), 2)
            flip = lax.rem(lax.div(j, unit), 2)
            total = total + (mine + flip - 2 * mine * flip) * unit
            unit *= 2
        return total

    def a_copy(j):
        to = other(j)
        return pltpu.make_async_remote_copy(
            src_ref=a_send.at[to],
            dst_ref=a_recv.at[me_tile],
            send_sem=a_send_sem.at[j],
            recv_sem=a_recv_sem.at[j],
            device_id=(to, me_tm),
            device_id_type=MESH,
        )

    @pl.loop(1, devices)
    def _(back):
        j = devices - back
        pack(other(j))
        a_copy(j).start()

    for w in (2, 3):
        start_main(w)
    pack(me_tile)
    a_recv[me_tile] = a_send[me_tile]

    base = me_tile * tiles

    @pl.loop(0, tiles)
    def _(row):
        mine = [device_tab[side, base + row] for side in range(2)]

        def count(other, sums):
            theirs = [device_tab[side, base + other] for side in range(2)]
            return tuple(
                sums[side]
                + (theirs[0] == mine[side]).astype(jnp.int32)
                + (theirs[1] == mine[side]).astype(jnp.int32)
                for side in range(2)
            )

        found = lax.fori_loop(0, row, count, (jnp.int32(0), jnp.int32(0)))
        for side in range(2):
            ranks[side, row] = jnp.minimum(found[side], capacity - 1)

    rate = rate_ref[...]

    def weight(part, t):
        step = (part * steps + t).astype(jnp.float32)
        return jnp.exp(rate * step / (steps * times))

    weights = [[weight(part, t) for t in range(steps)] for part in (me_tm, by_x, by_y)]

    def weights_of(p, w):
        return weights[0] if p == 0 else weights[1 + w % 2]

    inner = range(1, GB - 2)
    middle = ((0, 16, 17, 0), (GB - 2, 1, 47, 25), (GB - 1, 17, 15, 73))
    border = (
        (0, 0, 16),
        (0, 33, 16),
        (GB - 1, 1, 16),
        (GB - 1, 32, 16),
        (GB - 1, 0, 1),
        (GB - 1, 48, 1),
        (GB - 2, 0, 1),
        (GB - 2, 48, 1),
    )
    turn_centre = one_hot(width + 8, width, lambda row, column: column == width - row)
    last = width // GSTEP * GSTEP + ROWS - HMAX * 2

    def centre_sums(w, p, i):
        sums = [None] * GB
        mids = [None] * 3
        for t in range(steps):
            turned = pick(turn_centre, centre[0, p, w, i, t]) * weights_of(p, w)[t]
            kept[p, w, i, t, : 3 * ROWS] = turned[ROWS : 4 * ROWS]
            kept[p, w, i, t, 3 * ROWS :] = turned[6 * ROWS : 7 * ROWS]
            straight = centre[1, p, w, i, t].astype(jnp.float32)
            products = (
                turned[width - ROWS :] * straight[:24],
                turned[: 3 * ROWS] * straight[width - 3 * ROWS :],
                turned[:ROWS] * straight[width - ROWS :],
            )
            mids = [
                product if total is None else total + product
                for total, product in zip(mids, products)
            ]
            for g in inner:
                back = last - GSTEP * g
                ahead = GSTEP * (g - 1)
                product = turned[back : back + SPAN] * straight[ahead : ahead + SPAN]
                sums[g] = product if sums[g] is None else sums[g] + product
        return sums, jnp.concatenate(mids, axis=0)

    b_rims = 2 * half * steps * 2
    b_extra = b_send.shape[1] - b_rims
    rim_rows = b_rims // 2 * ROWS
    turn_rims = one_hot(
        rim_rows,
        rim_rows,
        lambda row, column: column == row // ROWS * (2 * ROWS) + ROWS - 1 - row,
    )

    def edge_sums(rims_ref, w, p):
        extra = rims_ref[w, b_rims:].reshape(b_extra * ROWS, depth).astype(jnp.float32)
        turned_rims = pick(turn_rims, rims_ref[w, : b_rims // 2].reshape(rim_rows, depth))
        found = []
        for i in range(half):
            total = None
            for t in range(steps):
                scale = weights_of(p, w)[t]
                place = i * pieces + t
                block = (i * steps + t) * 2
                left = turned_rims[block * ROWS : (block + 1) * ROWS] * scale
                right = turned_rims[(block + 1) * ROWS : (block + 2) * ROWS] * scale
                rims_rcv = b_rims // 2 + block
                rcv_left = rims_ref[w, rims_rcv].astype(jnp.float32)
                rcv_right = rims_ref[w, rims_rcv + 1].astype(jnp.float32)
                turned = kept[p, w, i, t]
                near = centre[1, p, w, i, t, ROWS : 3 * ROWS].astype(jnp.float32)
                far = centre[1, p, w, i, t, width - 3 * ROWS :].astype(jnp.float32)
                src_extra = extra[place : place + 1] * scale
                rcv_extra = extra[place + steps : place + steps + 1]
                product = jnp.concatenate(
                    [
                        turned[3 * ROWS :] * rcv_left,
                        left * near[1 : ROWS + 1],
                        right * far[ROWS + 1 : 2 * ROWS + 1],
                        turned[:ROWS] * rcv_right,
                        src_extra * far[ROWS : ROWS + 1],
                        turned[ROWS : ROWS + 1] * rcv_extra,
                        right[ROWS - 1 :] * far[:1],
                        turned[2 * ROWS : 2 * ROWS + 1] * rcv_right[:1],
                        jnp.zeros((4, depth), jnp.float32),
                    ],
                    axis=0,
                )
                total = product if total is None else total + product
            found.append(total)
        return found

    def own_centre(w):
        @pl.loop(0, half)
        def _(i):
            sums, mids = centre_sums(w, 0, i)
            for g in inner:
                acc[w, i, g] = sums[g]
            acc_mid[w, i] = mids

    def own_edge(w):
        for i, total in enumerate(edge_sums(b_own, w, 0)):
            acc_edge[w, i] = total

    def far_centre(w):
        for copy in main_copies[w]:
            copy.wait_recv()

        @pl.loop(0, half)
        def _(i):
            sums, mids = centre_sums(w, 1, i)
            mids = acc_mid[w, i] + mids
            if w < 2:
                first = OFFS * len(inner)
                for _, _, count, place in middle:
                    pc_send[w, i, first : first + count] = mids[place : place + count]
                    first += count
            else:
                acc_mid[w, i] = mids
            for k, g in enumerate(inner):
                total = acc[w, i, g] + sums[g]
                if w < 2:
                    pc_send[w, i, OFFS * k : OFFS * (k + 1)] = total[:OFFS]
                else:
                    acc[w, i, g] = total

    def far_edge(w):
        b_copies[w].wait_recv()
        target = pe_send if w < 2 else acc_edge
        for i, total in enumerate(edge_sums(b_recv, w, 1)):
            target[w, i] = acc_edge[w, i] + total

    def partial_copy(w, send, recv, k):
        return pltpu.make_async_remote_copy(
            src_ref=send.at[w],
            dst_ref=recv.at[w],
            send_sem=p_send_sem.at[k, w],
            recv_sem=p_recv_sem.at[k, w],
            device_id=(me_tile, owner[w]),
            device_id_type=MESH,
        )

    def unpack(first, target, w):
        row = lax.broadcasted_iota(jnp.int32, (b_extra * ROWS, half * a_extra * ROWS), 0)
        column = lax.broadcasted_iota(jnp.int32, (b_extra * ROWS, half * a_extra * ROWS), 1)
        chosen = jnp.full(row.shape, False)
        extras = []
        for i in range(half):
            tile = first + i
            for side in range(2):
                source = device_tab[side, base + tile]
                rank = ranks[side, tile]
                rim = a_recv[source, pl.ds(rank * pieces, pieces)]
                for f in range(2):
                    for t in range(steps):
                        target[w, ((f * half + i) * steps + t) * 2 + side] = rim[f * steps + t]
            extras.append(
                a_recv[source, capacity * pieces :].reshape(a_extra * ROWS, depth)
            )
            chosen = chosen | (
                (row >= i * pieces)
                & (row < (i + 1) * pieces)
                & (column == i * a_extra * ROWS + rank * pieces + row - i * pieces)
            )
        packed = pick(
            chosen.astype(jnp.float32).astype(jnp.bfloat16), jnp.concatenate(extras, axis=0)
        )
        target[w, b_rims:] = packed.astype(jnp.bfloat16).reshape(b_extra, ROWS, depth)

    def place_rows(tile, g, offs, count, rows):
        for part in range(depth // 128):
            turned_out[tile, part, pl.ds(offs * GB + g, count, stride=GB), :] = rows[
                :, 128 * part : 128 * (part + 1)
            ]

    def finish_early(w):
        @pl.loop(0, half)
        def _(i):
            tile = offset[w] + i
            first = 0
            for g in inner:
                got = pc_recv[w - 2, i, first : first + OFFS]
                place_rows(tile, g, 0, OFFS, acc[w, i, g][:OFFS] + got)
                first += OFFS
            mids = acc_mid[w, i]
            for g, offs, count, place in middle:
                got = pc_recv[w - 2, i, first : first + count]
                place_rows(tile, g, offs, count, mids[place : place + count] + got)
                first += count

    def finish_late(w):
        @pl.loop(0, half)
        def _(i):
            tile = offset[w] + i
            first = 0
            for g, offs, count in border:
                got = pe_recv[w - 2, i, first : first + count]
                place_rows(tile, g, offs, count, acc_edge[w, i, first : first + count] + got)
                first += count
            extent = extent_ref[me_tm * share + tile]
            cell = lax.broadcasted_iota(jnp.int32, (1, 128), 1)
            for part in range(depth // 128):
                mask = (cell + 128 * part < extent).astype(jnp.float32)
                out_ref[tile, :, 128 * part : 128 * (part + 1)] = (
                    turned_out[tile, part] * (1.0 / math.sqrt(steps * times)) * mask
                )

    for copy in own_copies:
        copy.wait()
    for w in range(4):
        own_centre(w)

    pc_copies = []
    for w in range(2):
        far_centre(w)
        copy = partial_copy(w, pc_send, pc_recv, 0)
        copy.start()
        pc_copies.append(copy)
    for w in (2, 3):
        far_centre(w)

    @pl.loop(1, devices)
    def _(j):
        a_copy(j).wait()

    b_copies = []

    def send_rims(w):
        unpack(first_tile(owner_there, w), b_send, w)
        copy = pltpu.make_async_remote_copy(
            src_ref=b_send.at[w],
            dst_ref=b_recv.at[w],
            send_sem=b_send_sem.at[w],
            recv_sem=b_recv_sem.at[w],
            device_id=(me_tile, partner[w]),
            device_id_type=MESH,
        )
        copy.start()
        b_copies.append(copy)

    for w in range(2):
        send_rims(w)
    for w in range(2):
        unpack(first_tile(owner, w), b_own, w)
        own_edge(w)
    for w in (2, 3):
        send_rims(w)

    pe_copies = []
    for w in range(2):
        far_edge(w)
        copy = partial_copy(w, pe_send, pe_recv, 1)
        copy.start()
        pe_copies.append(copy)
    for w in (2, 3):
        unpack(first_tile(owner, w), b_own, w)
        own_edge(w)
        far_edge(w)
    for w in (2, 3):
        pc_copies[w - 2].wait_recv()
        finish_early(w)
    for w in (2, 3):
        pe_copies[w - 2].wait_recv()
        finish_late(w)

    for copies in main_copies:
        for copy in copies:
            copy.wait_send()
    for copy in b_copies + pc_copies + pe_copies:
        copy.wait_send()


def paired(src_snap, rcv_snap, q_rate, nbr_device, nbr_index, depth_extent):
    tiles, steps, width, depth = src_snap.shape
    devices = lax.axis_size("tile")
    times = lax.axis_size("tm")
    capacity = (2 * tiles + devices - 1) // devices + 1
    share = tiles // times
    half = share // 2
    pieces = 2 * steps
    a_blocks = capacity * pieces + -(-capacity * pieces // ROWS)
    b_blocks = 2 * half * steps * 2 + -(-half * pieces // ROWS)
    inner_rows = 328
    outer_rows = 72
    sizes = (tiles, steps, width, depth, devices, times, capacity, share)
    bf16, f32 = jnp.bfloat16, jnp.float32
    products = share * GB * OFFS * depth * steps * times
    image = pl.pallas_call(
        functools.partial(pair_kernel, sizes),
        out_shape=jax.ShapeDtypeStruct((share, OFFS * GB, depth), f32),
        in_specs=[pl.BlockSpec(memory_space=pltpu.HBM)] * 6,
        out_specs=pl.BlockSpec(memory_space=pltpu.VMEM),
        scratch_shapes=[
            pltpu.SMEM(nbr_device.shape[::-1], jnp.int32),
            pltpu.SMEM(nbr_index.shape[::-1], jnp.int32),
            pltpu.SMEM(depth_extent.shape, jnp.int32),
            pltpu.VMEM((1, depth), f32),
            pltpu.SMEM((2, tiles), jnp.int32),
            pltpu.VMEM((2, 3, tiles, steps, ROWS, depth), bf16),
            pltpu.VMEM((devices, a_blocks, ROWS, depth), bf16),
            pltpu.VMEM((devices, a_blocks, ROWS, depth), bf16),
            pltpu.VMEM((4, b_blocks, ROWS, depth), bf16),
            pltpu.VMEM((4, b_blocks, ROWS, depth), bf16),
            pltpu.VMEM((4, b_blocks, ROWS, depth), bf16),
            pltpu.VMEM((2, 2, 4, half, steps, width, depth), bf16),
            pltpu.VMEM((4, half, GB, SPAN, depth), f32),
            pltpu.VMEM((4, half, 88, depth), f32),
            pltpu.VMEM((4, half, outer_rows, depth), f32),
            pltpu.VMEM((2, 4, half, steps, 4 * ROWS, depth), f32),
            pltpu.VMEM((share, depth // 128, OFFS * GB, 128), f32),
            pltpu.VMEM((2, half, inner_rows, depth), f32),
            pltpu.VMEM((2, half, inner_rows, depth), f32),
            pltpu.VMEM((2, half, outer_rows, depth), f32),
            pltpu.VMEM((2, half, outer_rows, depth), f32),
            pltpu.SemaphoreType.DMA((4,)),
            pltpu.SemaphoreType.DMA((6,)),
            pltpu.SemaphoreType.DMA((4, 2)),
            pltpu.SemaphoreType.DMA((4, 2)),
            pltpu.SemaphoreType.DMA((4, 2)),
            pltpu.SemaphoreType.DMA((devices,)),
            pltpu.SemaphoreType.DMA((devices,)),
            pltpu.SemaphoreType.DMA((4,)),
            pltpu.SemaphoreType.DMA((4,)),
            pltpu.SemaphoreType.DMA((2, 2)),
            pltpu.SemaphoreType.DMA((2, 2)),
        ],
        compiler_params=pltpu.CompilerParams(
            collective_id=1, has_side_effects=True, vmem_limit_bytes=60 * 1024 * 1024
        ),
        cost_estimate=pl.CostEstimate(
            flops=3 * products, bytes_accessed=4 * tiles * steps * width * depth, transcendentals=0
        ),
    )(nbr_device.T, nbr_index.T, depth_extent, q_rate.reshape(1, depth), src_snap, rcv_snap)
    return image.reshape(share, OFFS, GB, depth).transpose(0, 2, 1, 3)


def solution(mesh):
    placed = (P("tile", "tm", None, None), P("tile", "tm", None, None), P(), P(), P(), P("tile"))
    body = paired if mesh.shape["tm"] == 4 else local
    return jax.shard_map(
        body,
        mesh=mesh,
        in_specs=placed,
        out_specs=P(("tile", "tm"), None, None, None),
        check_vma=False,
    )
```
